128 devices in a mesh: ctx: 16 (over z_lo, x, core), head: 8 (over y, z_hi).
Axes of the slice: x: 4, y: 4, z: 4 (z_hi: 2, z_lo: 2; z = z_hi * 2 + z_lo), core: 2. Of those that a mesh axis runs over, the one named last changes fastest.
Arguments:
- node_rows: bfloat16 [8192, 4096], P('ctx', 'head')
- node_target: int32 [8192], P('ctx'), may hold values from 0 to 8191, as said below
- node_position: int32 [8192], P('ctx'), may hold values from 0 to 8191
- block_mask: int32 [64, 64], P('ctx'), may hold values from 0 to 1, as said below
- w_query: bfloat16 [4096, 4096], P(None, 'head'), may hold values from -0.09375 to 0.09375
- w_key: bfloat16 [4096, 1024], P(None, 'head'), may hold values from -0.09375 to 0.09375
- w_value: bfloat16 [4096, 1024], P(None, 'head'), may hold values from -0.09375 to 0.09375
- w_out: bfloat16 [4096, 4096], P('head'), may hold values from -0.09375 to 0.09375
Outputs:
- scored: bfloat16 [8192, 4096], P(('ctx', 'head'))
The draws below stay inside these ranges and needn't reach their ends.
Inputs may be any that keep to these rules, and one draw needn't show every extreme that they name: node_target is a permutation of the 8192 tree positions; the rows that one generator device holds send at most 64 rows to the 512 positions of one owner, and exactly 64 to some owner. block_mask[qb, kb] is 1 exactly when block kb lies strictly above block qb on its path to the root of a tree of blocks whose root is block 0; entries with kb >= qb are 0.
All inputs are finite; a program needn't handle non-finite values.
Results may differ from the reference program's by a relative error of at most 0.025.
The reference program's roundings to bfloat16 on the way (of `routed`, `weights` and `attended`) count: a program that leaves them out, or rounds other values in their place, can miss the bound.
Values may be sent and summed in bfloat16 or wider, within the bound.
A program may use at most 64 MiB of HBM per device.

```python
import math
import jax
import jax.numpy as jnp
import numpy as np
from jax import lax

D = 4096
HEADS = 32
KV_HEADS = 8
HD = 128
BLOCK = 128
TOK_DEV = 512
TOKENS = 8192
N_CTX = 16


def draw_node_rows(key, part):
    key_values = jax.random.fold_in(key, 0)
    values = jnp.clip(jax.random.normal(key_values, (TOKENS, D), jnp.float32), -6.0, 6.0)
    return values.astype(jnp.bfloat16)


def draw_node_target(key, part):
    owners = N_CTX
    per_device = TOK_DEV
    capacity = 2 * TOK_DEV // N_CTX
    even_share = (per_device - capacity) // (owners - 1)
    leftover = per_device - capacity - even_share * (owners - 1)
    share_table = np.array([capacity] + [even_share + (1 if slot_number < leftover else 0) for slot_number in range(owners - 1)], dtype=np.int32)
    key_order, key_slots, key_mixing = jax.random.split(jax.random.fold_in(key, 11), 3)
    rotation = jax.random.permutation(key_order, owners)
    counts = jnp.asarray(share_table)[(rotation[None, :] - jnp.arange(owners, dtype=jnp.int32)[:, None]) % owners]
    owner_starts = jnp.cumsum(counts, axis=0) - counts
    row_ends = jnp.cumsum(counts, axis=1)
    row_index = jnp.arange(per_device, dtype=jnp.int32)
    owner_of = jnp.sum((row_index[None, :, None] >= row_ends[:, None, :]).astype(jnp.int32), axis=2)
    row_first = jnp.take_along_axis(row_ends - counts, owner_of, axis=1)
    offset = jnp.take_along_axis(owner_starts, owner_of, axis=1) + row_index[None, :] - row_first
    shuffle = jax.vmap(lambda single: jax.random.permutation(single, per_device))(jax.random.split(key_slots, owners))
    target = owner_of * per_device + shuffle[owner_of, offset]
    mixing = jax.vmap(lambda single: jax.random.permutation(single, per_device))(jax.random.split(key_mixing, owners))
    target = jnp.take_along_axis(target, mixing, axis=1)
    return target.reshape(owners * per_device).astype(jnp.int32)


def draw_block_mask(key, part):
    blocks = TOKENS // BLOCK
    block_index = jnp.arange(blocks, dtype=jnp.int32)
    parents = jax.random.randint(jax.random.fold_in(key, 23), (blocks,), 0, jnp.maximum(block_index, 1)).astype(jnp.int32)

    def climb(step_number, state):
        current, ancestry = state
        current = parents[current]
        ancestry = ancestry.at[block_index, current].set(1)
        return (current, ancestry)
    current, ancestry = lax.fori_loop(0, blocks, climb, (block_index, jnp.zeros((blocks, blocks), jnp.int32)))
    return ancestry * (block_index[None, :] < block_index[:, None]).astype(jnp.int32)


def set_ends(result, rng, least, top_value):
    longest = result.shape.index(max(result.shape))
    spots = []
    for shift in (0, 1):
        where = [jax.random.randint(jax.random.fold_in(rng, axis), (), 0, length) for axis, length in enumerate(result.shape)]
        where[longest] = (where[longest] + shift) % result.shape[longest]
        spots.append(tuple(where))
    return result.at[spots[0]].set(least).at[spots[1]].set(top_value)


def steps_of(own_key, dims, cuts, least, high):
    def one(axis_at, shards_of):
        heights = jax.random.uniform(jax.random.fold_in(jax.random.fold_in(own_key, 6), axis_at), (shards_of,), jnp.float32, least / len(cuts), high / len(cuts))
        return jnp.repeat(jnp.exp(heights), dims[axis_at] // shards_of).reshape((-1,) + (1,) * (len(dims) - axis_at - 1))

    level = one(*cuts[0])
    for cut in cuts[1:]:
        level = level * one(*cut)
    return level


def gaussian(stream_key, extent, deviation, bound, cuts=(), kind=jnp.bfloat16):
    entries = jax.random.normal(stream_key, extent, jnp.float32) * deviation
    if len(cuts) > 0:
        entries = steps_of(stream_key, extent, cuts, -0.22, 0.18) * entries
    return jnp.clip(entries, min=-bound, max=bound).astype(kind)


def setup_inputs(seed: int = 0) -> dict:
    arg_keys = jax.random.split(jax.random.key(seed), 9)
    node_rows = draw_node_rows(jax.random.fold_in(arg_keys[8], 71), 0)
    node_target = draw_node_target(jax.random.fold_in(arg_keys[8], 71), 0)
    node_position = set_ends(jax.random.randint(arg_keys[2], (TOKENS,), 0, TOKENS), jax.random.fold_in(arg_keys[2], 1), 0, TOKENS - 1).astype(jnp.int32)
    block_mask = draw_block_mask(jax.random.fold_in(arg_keys[8], 71), 0)
    w_query = gaussian(arg_keys[4], (D, HEADS * HD), D ** -0.5, 0.09375, ((1, 8),))
    w_key = gaussian(arg_keys[5], (D, KV_HEADS * HD), D ** -0.5, 0.09375, ((1, 8),))
    w_value = gaussian(arg_keys[6], (D, KV_HEADS * HD), D ** -0.5, 0.09375, ((1, 8),))
    w_out = gaussian(arg_keys[7], (HEADS * HD, D), (HEADS * HD) ** -0.5, 0.09375, ((0, 8),))
    return dict(node_rows=node_rows, node_target=node_target, node_position=node_position, block_mask=block_mask, w_query=w_query, w_key=w_key, w_value=w_value, w_out=w_out)


ROPE_THETA = 500000.0
NEG_LARGE = -1e+30

def rotate(tensor, positions, head_size):
    half_size = head_size // 2
    inverse = jnp.exp(jnp.arange(half_size, dtype=jnp.float32) * (-2.0 * math.log(ROPE_THETA) / head_size))
    angles = positions.astype(jnp.float32)[:, None] * inverse[None, :]
    cosine = jnp.cos(angles)[:, None, :]
    sine = jnp.sin(angles)[:, None, :]
    first_half = tensor[..., :half_size]
    second_half = tensor[..., half_size:]
    return jnp.concatenate([first_half * cosine - second_half * sine, second_half * cosine + first_half * sine], axis=-1)

def reference(node_rows, node_target, node_position, block_mask, w_query, w_key, w_value, w_out):
    routed = jnp.zeros_like(node_rows).at[node_target].set(node_rows)
    queries = jnp.dot(routed, w_query, preferred_element_type=jnp.float32).reshape(TOKENS, HEADS, HD)
    keys_all = jnp.dot(routed, w_key, preferred_element_type=jnp.float32).reshape(TOKENS, KV_HEADS, HD)
    values_all = jnp.dot(routed, w_value, preferred_element_type=jnp.float32).reshape(TOKENS, KV_HEADS, HD)
    queries = lax.optimization_barrier(rotate(queries, node_position, HD).astype(jnp.bfloat16))
    keys_all = lax.optimization_barrier(rotate(keys_all, node_position, HD).astype(jnp.bfloat16))
    values_all = lax.optimization_barrier(values_all.astype(jnp.bfloat16))
    groups = HEADS // KV_HEADS
    grouped = queries.reshape(TOKENS, KV_HEADS, groups, HD).astype(jnp.float32)
    keyed = keys_all.astype(jnp.float32)
    valued = values_all.astype(jnp.float32)
    key_index = jnp.arange(TOKENS, dtype=jnp.int32)
    key_block = key_index // BLOCK

    def one_block(block_number):
        block_number = block_number.astype(jnp.int32)
        query_rows = lax.dynamic_slice_in_dim(grouped, block_number * BLOCK, BLOCK, 0)
        scores = jnp.einsum('qkgd,tkd->kgqt', query_rows, keyed) / math.sqrt(HD)
        query_index = block_number * BLOCK + jnp.arange(BLOCK, dtype=jnp.int32)
        mask_row = lax.dynamic_index_in_dim(block_mask, block_number, 0, keepdims=False)[key_block]
        earlier = ((key_block < block_number) & (mask_row == 1))[None, :]
        diagonal = (key_block == block_number)[None, :] & (key_index[None, :] <= query_index[:, None])
        allowed = earlier | diagonal
        masked = jnp.where(allowed, scores, NEG_LARGE)
        highest = lax.optimization_barrier(jnp.max(masked, axis=-1, keepdims=True))
        weights = jnp.where(allowed, jnp.exp(scores - highest), 0.0)
        denominator = lax.optimization_barrier(jnp.sum(weights, axis=-1))
        rounded = lax.optimization_barrier(weights.astype(jnp.bfloat16))
        mixed_heads = jnp.einsum('kgqt,tkd->qkgd', rounded.astype(jnp.float32), valued)
        mixed_heads = mixed_heads / jnp.transpose(denominator, (2, 0, 1))[..., None]
        return mixed_heads.reshape(BLOCK, HEADS * HD).astype(jnp.bfloat16)
    attended = lax.map(one_block, jnp.arange(TOKENS // BLOCK, dtype=jnp.int32)).reshape(TOKENS, HEADS * HD)
    return jnp.dot(attended, w_out, preferred_element_type=jnp.float32).astype(jnp.bfloat16)
```

```python
import functools
import math

import jax
import jax.numpy as jnp
from jax import lax
from jax.experimental import pallas as pl
from jax.experimental.pallas import tpu as pltpu
from jax.sharding import PartitionSpec as P

HD = 128
BLOCK = 128
ROPE_THETA = 500000.0
NEG_LARGE = -1e30
MIB = 1024 * 1024


def rotary_tables(positions, head_size):
    half_size = head_size // 2
    inverse = jnp.exp(
        jnp.arange(half_size, dtype=jnp.float32) * (-2.0 * math.log(ROPE_THETA) / head_size)
    )
    angles = positions.astype(jnp.float32)[:, None] * inverse[None, :]
    cosine = jnp.cos(angles)
    sine = jnp.sin(angles)
    return jnp.concatenate([cosine, cosine], axis=-1), jnp.concatenate([-sine, sine], axis=-1)


def attend_kernel(mask_ref, q_ref, kv_ref, out_ref, list_ref, acc_ref):
    ctx = lax.axis_index("ctx")
    local_blocks = q_ref.shape[0] // BLOCK
    heads = q_ref.shape[1] // HD
    block_count = mask_ref.shape[1]
    width = heads * BLOCK
    scale = 1.0 / math.sqrt(HD)

    for b in range(local_blocks):
        qb = ctx * local_blocks + b

        def build(kb, n):
            list_ref[n] = kb
            return n + jnp.where(kb < qb, mask_ref[b, kb], 0)

        count = lax.fori_loop(0, block_count, build, 0, unroll=8)
        list_ref[count] = 0
        rows = pl.ds(b * BLOCK, BLOCK)
        queries = jnp.concatenate(
            [q_ref[rows, h * HD : (h + 1) * HD] for h in range(heads)], axis=0
        )

        def scores_of(kb):
            keys = kv_ref[pl.ds(pl.multiple_of(kb * BLOCK, BLOCK), BLOCK), 0:HD]
            return (
                lax.dot_general(
                    keys, queries, (((1,), (1,)), ((), ())), preferred_element_type=jnp.float32
                )
                * scale
            )

        def mix(kb, weights):
            values = kv_ref[pl.ds(pl.multiple_of(kb * BLOCK, BLOCK), BLOCK), HD : 2 * HD]
            return lax.dot_general(
                values,
                weights.astype(jnp.bfloat16),
                (((0,), (0,)), ((), ())),
                preferred_element_type=jnp.float32,
            )

        key_at = lax.broadcasted_iota(jnp.int32, (BLOCK, width), 0)
        query_at = lax.broadcasted_iota(jnp.int32, (BLOCK, width), 1) % BLOCK
        scores = jnp.where(key_at <= query_at, scores_of(qb), NEG_LARGE)
        highest = jnp.max(scores, axis=0, keepdims=True)
        weights = jnp.exp(scores - highest)
        total = jnp.sum(weights, axis=0, keepdims=True)
        acc_ref[...] = mix(qb, weights)

        def step(i, state):
            highest, total = state
            first = list_ref[2 * i]
            second = list_ref[2 * i + 1]
            has_second = 2 * i + 1 < count
            second = jnp.where(has_second, second, 0)
            drop = jnp.where(has_second, 0.0, NEG_LARGE).astype(jnp.float32)
            scores0 = scores_of(first)
            scores1 = scores_of(second) + drop
            new_highest = jnp.maximum(
                highest,
                jnp.maximum(
                    jnp.max(scores0, axis=0, keepdims=True), jnp.max(scores1, axis=0, keepdims=True)
                ),
            )
            factor = jnp.exp(highest - new_highest)
            weights0 = jnp.exp(scores0 - new_highest)
            weights1 = jnp.exp(scores1 - new_highest)
            total = (
                total * factor
                + jnp.sum(weights0, axis=0, keepdims=True)
                + jnp.sum(weights1, axis=0, keepdims=True)
            )
            acc_ref[...] = acc_ref[...] * factor + mix(first, weights0) + mix(second, weights1)
            return new_highest, total

        highest, total = lax.fori_loop(0, (count + 1) // 2, step, (highest, total))
        attended = acc_ref[...] / total
        for h in range(heads):
            out_ref[rows, h * HD : (h + 1) * HD] = attended[
                :, h * BLOCK : (h + 1) * BLOCK
            ].T.astype(jnp.bfloat16)


def attend(block_mask, queries, kv):
    return pl.pallas_call(
        attend_kernel,
        out_shape=jax.ShapeDtypeStruct(queries.shape, jnp.bfloat16),
        in_specs=[
            pl.BlockSpec(memory_space=pltpu.SMEM),
            pl.BlockSpec(memory_space=pltpu.VMEM),
            pl.BlockSpec(memory_space=pltpu.VMEM),
        ],
        out_specs=pl.BlockSpec(memory_space=pltpu.VMEM),
        scratch_shapes=[
            pltpu.SMEM((128,), jnp.int32),
            pltpu.VMEM((HD, queries.shape[1]), jnp.float32),
        ],
        compiler_params=pltpu.CompilerParams(vmem_limit_bytes=32 * MIB),
        name="attend",
    )(block_mask, queries, kv)


def on_device(node_rows, node_target, node_position, block_mask, w_query, w_key, w_value, w_out):
    local_rows = node_rows.shape[0]
    row_offset = lax.axis_index("ctx") * local_rows
    all_rows, all_targets = (
        lax.all_gather(node_rows, "ctx", axis=0, tiled=True),
        lax.all_gather(node_target, "ctx", axis=0, tiled=True),
    )
    places = all_targets - row_offset
    places = jnp.where((places >= 0) & (places < local_rows), places, local_rows)
    routed = jnp.zeros_like(node_rows).at[places].set(all_rows, mode="drop")
    pieces_in = lax.all_gather(routed, "head", axis=1, tiled=True)
    query_proj, key_proj, value_proj = tuple(
        (
            jnp.dot(pieces_in, weight, preferred_element_type=jnp.float32)
            for weight in (w_query, w_key, w_value)
        )
    )
    cosine, sine = rotary_tables(node_position, HD)

    def rotate(tensor):
        heads = tensor.reshape(local_rows, -1, HD)
        turned = jnp.roll(heads, HD // 2, axis=-1)
        return (
            (heads * cosine[:, None, :] + turned * sine[:, None, :])
            .astype(jnp.bfloat16)
            .reshape(tensor.shape)
        )

    queries = rotate(query_proj)
    kv_local = jnp.concatenate([rotate(key_proj), value_proj.astype(jnp.bfloat16)], axis=1)
    kv = lax.all_gather(kv_local, "ctx", axis=0, tiled=True)
    attended = attend(block_mask, queries, kv)
    return lax.psum_scatter(
        jnp.dot(attended, w_out, preferred_element_type=jnp.float32).astype(jnp.bfloat16),
        "head",
        scatter_dimension=0,
        tiled=True,
    )


def solution(mesh):
    placed = (
        P("ctx", "head"),
        P("ctx"),
        P("ctx"),
        P("ctx", None),
        P(None, "head"),
        P(None, "head"),
        P(None, "head"),
        P("head", None),
    )
    return jax.shard_map(
        on_device, mesh=mesh, in_specs=placed, out_specs=P(("ctx", "head"), None), check_vma=False
    )
```

```python
import math

import jax
import jax.numpy as jnp
from jax import lax
from jax.experimental import pallas as pl
from jax.experimental.pallas import tpu as pltpu
from jax.sharding import PartitionSpec as P

HD = 128
BLOCK = 128
ROPE_THETA = 500000.0
NEG_LARGE = -1e30
MIB = 1024 * 1024


def rotary_tables(positions, head_size):
    half_size = head_size // 2
    inverse = jnp.exp(
        jnp.arange(half_size, dtype=jnp.float32) * (-2.0 * math.log(ROPE_THETA) / head_size)
    )
    angles = positions.astype(jnp.float32)[:, None] * inverse[None, :]
    cosine = jnp.cos(angles)
    sine = jnp.sin(angles)
    return jnp.concatenate([cosine, cosine], axis=-1), jnp.concatenate([-sine, sine], axis=-1)


def attend_kernel(mask_ref, q_ref, kv_ref, out_ref, list_ref, acc_ref):
    ctx = lax.axis_index("ctx")
    local_blocks = q_ref.shape[0] // BLOCK
    heads = q_ref.shape[1] // HD
    block_count = mask_ref.shape[1]
    width = heads * BLOCK
    scale = 1.0 / math.sqrt(HD)

    for b in range(local_blocks):
        qb = ctx * local_blocks + b

        def build(kb, n):
            list_ref[n] = kb
            return n + jnp.where(kb < qb, mask_ref[b, kb], 0)

        count = lax.fori_loop(0, block_count, build, 0, unroll=8)
        list_ref[count] = 0
        rows = pl.ds(b * BLOCK, BLOCK)
        queries = jnp.concatenate(
            [q_ref[rows, h * HD : (h + 1) * HD] for h in range(heads)], axis=0
        )

        def scores_of(kb):
            keys = kv_ref[pl.ds(pl.multiple_of(kb * BLOCK, BLOCK), BLOCK), 0:HD]
            return (
                lax.dot_general(
                    keys, queries, (((1,), (1,)), ((), ())), preferred_element_type=jnp.float32
                )
                * scale
            )

        def mix(kb, weights):
            values = kv_ref[pl.ds(pl.multiple_of(kb * BLOCK, BLOCK), BLOCK), HD : 2 * HD]
            return lax.dot_general(
                values,
                weights.astype(jnp.bfloat16),
                (((0,), (0,)), ((), ())),
                preferred_element_type=jnp.float32,
            )

        key_at = lax.broadcasted_iota(jnp.int32, (BLOCK, width), 0)
        query_at = lax.broadcasted_iota(jnp.int32, (BLOCK, width), 1) % BLOCK
        scores = jnp.where(key_at <= query_at, scores_of(qb), NEG_LARGE)
        highest = jnp.max(scores, axis=0, keepdims=True)
        weights = jnp.exp(scores - highest)
        total = jnp.sum(weights, axis=0, keepdims=True)
        acc_ref[...] = mix(qb, weights)

        def step(i, state):
            highest, total = state
            first = list_ref[2 * i]
            second = list_ref[2 * i + 1]
            has_second = 2 * i + 1 < count
            second = jnp.where(has_second, second, 0)
            drop = jnp.where(has_second, 0.0, NEG_LARGE).astype(jnp.float32)
            scores0 = scores_of(first)
            scores1 = scores_of(second) + drop
            new_highest = jnp.maximum(
                highest,
                jnp.maximum(
                    jnp.max(scores0, axis=0, keepdims=True), jnp.max(scores1, axis=0, keepdims=True)
                ),
            )
            factor = jnp.exp(highest - new_highest)
            weights0 = jnp.exp(scores0 - new_highest)
            weights1 = jnp.exp(scores1 - new_highest)
            total = (
                total * factor
                + jnp.sum(weights0, axis=0, keepdims=True)
                + jnp.sum(weights1, axis=0, keepdims=True)
            )
            acc_ref[...] = acc_ref[...] * factor + mix(first, weights0) + mix(second, weights1)
            return new_highest, total

        highest, total = lax.fori_loop(0, (count + 1) // 2, step, (highest, total))
        attended = acc_ref[...] / total
        for h in range(heads):
            out_ref[rows, h * HD : (h + 1) * HD] = attended[
                :, h * BLOCK : (h + 1) * BLOCK
            ].T.astype(jnp.bfloat16)


def attend(block_mask, queries, kv):
    return pl.pallas_call(
        attend_kernel,
        out_shape=jax.ShapeDtypeStruct(queries.shape, jnp.bfloat16),
        in_specs=[
            pl.BlockSpec(memory_space=pltpu.SMEM),
            pl.BlockSpec(memory_space=pltpu.VMEM),
            pl.BlockSpec(memory_space=pltpu.VMEM),
        ],
        out_specs=pl.BlockSpec(memory_space=pltpu.VMEM),
        scratch_shapes=[
            pltpu.SMEM((128,), jnp.int32),
            pltpu.VMEM((HD, queries.shape[1]), jnp.float32),
        ],
        compiler_params=pltpu.CompilerParams(vmem_limit_bytes=32 * MIB),
        name="attend",
    )(block_mask, queries, kv)


def ring_places():
    head = lax.axis_index("head")
    y, zh = head // 2, head % 2
    up = ((y + 1) % 4) * 2 + zh
    down = ((y + 3) % 4) * 2 + zh
    across = y * 2 + (1 - zh)
    return y, zh, up, down, across


def remote(src, dst, send_sem, recv_sem, **place):
    return pltpu.make_async_remote_copy(
        src_ref=src,
        dst_ref=dst,
        send_sem=send_sem,
        recv_sem=recv_sem,
        device_id=place,
        device_id_type=pl.DeviceIdType.MESH,
    )


OUT_CHUNKS = 4


def project_out_kernel(
    att_ref, w_hbm, out_ref, w_ref, part, far_out, far_in, near_out, near_in, z_out, z_in, w_sem,
    far_ss, far_rs, near_ss, near_rs, z_ss, z_rs,
):
    y, zh, up, down, across = ring_places()
    cw = part.shape[2]
    half = cw // 2
    loads = [
        pltpu.make_async_copy(w_hbm.at[:, pl.ds(c * cw, cw)], w_ref.at[c], w_sem.at[c])
        for c in range(OUT_CHUNKS)
    ]
    for load in loads:
        load.start()
    barrier = pltpu.get_barrier_semaphore()
    for peer in (up, down, across):
        pl.semaphore_signal(
            barrier, inc=1, device_id={"head": peer}, device_id_type=pl.DeviceIdType.MESH
        )
    pl.semaphore_wait(barrier, 3)

    def rows_of(c, place, lo):
        return part[c, pl.ds(pl.multiple_of(place * 128, 128), 128), lo : lo + half]

    def far(c, side):
        return remote(
            far_out.at[c, side], far_in.at[c, side], far_ss.at[c, side], far_rs.at[c, side],
            head=(up, down)[side],
        )

    def near(c, side, part_at):
        return remote(
            near_out.at[c, side, part_at],
            near_in.at[c, side, part_at],
            near_ss.at[c, side, part_at],
            near_rs.at[c, side, part_at],
            head=(up, down)[side],
        )

    def cross(c):
        return remote(z_out.at[c], z_in.at[c], z_ss.at[c], z_rs.at[c], head=across)

    def first(c):
        loads[c].wait()
        part[c] = jnp.dot(att_ref[...], w_ref[c], preferred_element_type=jnp.float32)
        for side in range(2):
            far_out[c, side] = rows_of(c, (y + 2) % 4, side * half).astype(jnp.bfloat16)
            far(c, side).start()
        near_out[c, 0, 1] = rows_of(c, (y + 1) % 4, half).astype(jnp.bfloat16)
        near(c, 0, 1).start()
        near_out[c, 1, 0] = rows_of(c, (y + 3) % 4, 0).astype(jnp.bfloat16)
        near(c, 1, 0).start()

    def second(c):
        far(c, 0).wait_recv()
        near_out[c, 0, 0] = (
            rows_of(c, (y + 1) % 4, 0) + far_in[c, 0].astype(jnp.float32)
        ).astype(jnp.bfloat16)
        near(c, 0, 0).start()
        far(c, 1).wait_recv()
        near_out[c, 1, 1] = (
            rows_of(c, (y + 3) % 4, half) + far_in[c, 1].astype(jnp.float32)
        ).astype(jnp.bfloat16)
        near(c, 1, 1).start()

    def third(c):
        for side in range(2):
            for at in range(2):
                near(c, side, at).wait_recv()
        mine = pl.multiple_of(y * 128, 128)
        for at in range(2):
            sl = slice(at * half, (at + 1) * half)
            other = pl.ds(pl.multiple_of((1 - zh) * 64, 64), 64)
            z_out[c, :, sl] = (
                part[c, pl.ds(pl.multiple_of(mine + (1 - zh) * 64, 64), 64), sl]
                + near_in[c, 0, at, other, :].astype(jnp.float32)
                + near_in[c, 1, at, other, :].astype(jnp.float32)
            ).astype(jnp.bfloat16)
        cross(c).start()
        for at in range(2):
            sl = slice(at * half, (at + 1) * half)
            own = pl.ds(pl.multiple_of(zh * 64, 64), 64)
            place = pl.ds(pl.multiple_of(mine + zh * 64, 64), 64)
            part[c, place, sl] = (
                part[c, place, sl]
                + near_in[c, 0, at, own, :].astype(jnp.float32)
                + near_in[c, 1, at, own, :].astype(jnp.float32)
            )

    def fourth(c):
        cross(c).wait_recv()
        place = pl.ds(pl.multiple_of(y * 128 + zh * 64, 64), 64)
        out_ref[:, c * cw : (c + 1) * cw] = (
            part[c, place, :] + z_in[c].astype(jnp.float32)
        ).astype(jnp.bfloat16)

    first(0)
    first(1)
    for c in range(OUT_CHUNKS):
        second(c)
        if c + 2 < OUT_CHUNKS:
            first(c + 2)
    for c in range(OUT_CHUNKS):
        third(c)
    for c in range(OUT_CHUNKS):
        fourth(c)
    for c in range(OUT_CHUNKS):
        for side in range(2):
            far(c, side).wait_send()
            for at in range(2):
                near(c, side, at).wait_send()
        cross(c).wait_send()


def project_out(attended, w_out):
    rows, depth = attended.shape
    width = w_out.shape[1]
    n, cw = OUT_CHUNKS, width // OUT_CHUNKS
    half = cw // 2
    bf16 = jnp.bfloat16
    dma = pltpu.SemaphoreType.DMA
    return pl.pallas_call(
        project_out_kernel,
        out_shape=jax.ShapeDtypeStruct((rows // 8, width), bf16),
        in_specs=[pl.BlockSpec(memory_space=pltpu.VMEM), pl.BlockSpec(memory_space=pl.ANY)],
        out_specs=pl.BlockSpec(memory_space=pltpu.VMEM),
        scratch_shapes=[
            pltpu.VMEM((n, depth, cw), bf16),
            pltpu.VMEM((n, rows, cw), jnp.float32),
            pltpu.VMEM((n, 2, rows // 4, half), bf16),
            pltpu.VMEM((n, 2, rows // 4, half), bf16),
            pltpu.VMEM((n, 2, 2, rows // 4, half), bf16),
            pltpu.VMEM((n, 2, 2, rows // 4, half), bf16),
            pltpu.VMEM((n, rows // 8, cw), bf16),
            pltpu.VMEM((n, rows // 8, cw), bf16),
            dma((n,)),
            dma((n, 2)),
            dma((n, 2)),
            dma((n, 2, 2)),
            dma((n, 2, 2)),
            dma((n,)),
            dma((n,)),
        ],
        compiler_params=pltpu.CompilerParams(
            collective_id=1, has_side_effects=True, vmem_limit_bytes=48 * MIB
        ),
        name="project_out",
    )(attended, w_out)


def on_device(node_rows, node_target, node_position, block_mask, w_query, w_key, w_value, w_out):
    local_rows = node_rows.shape[0]
    row_offset = lax.axis_index("ctx") * local_rows
    all_rows, all_targets = (
        lax.all_gather(node_rows, "ctx", axis=0, tiled=True),
        lax.all_gather(node_target, "ctx", axis=0, tiled=True),
    )
    places = all_targets - row_offset
    places = jnp.where((places >= 0) & (places < local_rows), places, local_rows)
    routed = jnp.zeros_like(node_rows).at[places].set(all_rows, mode="drop")
    pieces_in = lax.all_gather(routed, "head", axis=1, tiled=True)
    query_proj, key_proj, value_proj = tuple(
        (
            jnp.dot(pieces_in, weight, preferred_element_type=jnp.float32)
            for weight in (w_query, w_key, w_value)
        )
    )
    cosine, sine = rotary_tables(node_position, HD)

    def rotate(tensor):
        heads = tensor.reshape(local_rows, -1, HD)
        turned = jnp.roll(heads, HD // 2, axis=-1)
        return (
            (heads * cosine[:, None, :] + turned * sine[:, None, :])
            .astype(jnp.bfloat16)
            .reshape(tensor.shape)
        )

    queries = rotate(query_proj)
    kv_local = jnp.concatenate([rotate(key_proj), value_proj.astype(jnp.bfloat16)], axis=1)
    kv = lax.all_gather(kv_local, "ctx", axis=0, tiled=True)
    attended = attend(block_mask, queries, kv)
    return project_out(attended, w_out)


def solution(mesh):
    placed = (
        P("ctx", "head"),
        P("ctx"),
        P("ctx"),
        P("ctx", None),
        P(None, "head"),
        P(None, "head"),
        P(None, "head"),
        P("head", None),
    )
    return jax.shard_map(
        on_device, mesh=mesh, in_specs=placed, out_specs=P(("ctx", "head"), None), check_vma=False
    )
```

```python
import math

import jax
import jax.numpy as jnp
from jax import lax
from jax.experimental import pallas as pl
from jax.experimental.pallas import tpu as pltpu
from jax.sharding import PartitionSpec as P

HD = 128
BLOCK = 128
ROPE_THETA = 500000.0
NEG_LARGE = -1e30
MIB = 1024 * 1024


def rotary_tables(positions, head_size):
    half_size = head_size // 2
    inverse = jnp.exp(
        jnp.arange(half_size, dtype=jnp.float32) * (-2.0 * math.log(ROPE_THETA) / head_size)
    )
    angles = positions.astype(jnp.float32)[:, None] * inverse[None, :]
    cosine = jnp.cos(angles)
    sine = jnp.sin(angles)
    return jnp.concatenate([cosine, cosine], axis=-1), jnp.concatenate([-sine, sine], axis=-1)


def attend_kernel(mask_ref, q_ref, kv_ref, out_ref, list_ref, acc_ref):
    ctx = lax.axis_index("ctx")
    local_blocks = q_ref.shape[0] // BLOCK
    heads = q_ref.shape[1] // HD
    block_count = mask_ref.shape[1]
    width = heads * BLOCK
    scale = 1.0 / math.sqrt(HD)

    for b in range(local_blocks):
        qb = ctx * local_blocks + b

        def build(kb, n):
            list_ref[n] = kb
            return n + jnp.where(kb < qb, mask_ref[b, kb], 0)

        count = lax.fori_loop(0, block_count, build, 0, unroll=8)
        list_ref[count] = 0
        rows = pl.ds(b * BLOCK, BLOCK)
        queries = jnp.concatenate(
            [q_ref[rows, h * HD : (h + 1) * HD] for h in range(heads)], axis=0
        )

        def scores_of(kb):
            keys = kv_ref[pl.ds(pl.multiple_of(kb * BLOCK, BLOCK), BLOCK), 0:HD]
            return (
                lax.dot_general(
                    keys, queries, (((1,), (1,)), ((), ())), preferred_element_type=jnp.float32
                )
                * scale
            )

        def mix(kb, weights):
            values = kv_ref[pl.ds(pl.multiple_of(kb * BLOCK, BLOCK), BLOCK), HD : 2 * HD]
            return lax.dot_general(
                values,
                weights.astype(jnp.bfloat16),
                (((0,), (0,)), ((), ())),
                preferred_element_type=jnp.float32,
            )

        key_at = lax.broadcasted_iota(jnp.int32, (BLOCK, width), 0)
        query_at = lax.broadcasted_iota(jnp.int32, (BLOCK, width), 1) % BLOCK
        scores = jnp.where(key_at <= query_at, scores_of(qb), NEG_LARGE)
        highest = jnp.max(scores, axis=0, keepdims=True)
        weights = jnp.exp(scores - highest)
        total = jnp.sum(weights, axis=0, keepdims=True)
        acc_ref[...] = mix(qb, weights)

        def step(i, state):
            highest, total = state
            first = list_ref[2 * i]
            second = list_ref[2 * i + 1]
            has_second = 2 * i + 1 < count
            second = jnp.where(has_second, second, 0)
            drop = jnp.where(has_second, 0.0, NEG_LARGE).astype(jnp.float32)
            scores0 = scores_of(first)
            scores1 = scores_of(second) + drop
            new_highest = jnp.maximum(
                highest,
                jnp.maximum(
                    jnp.max(scores0, axis=0, keepdims=True), jnp.max(scores1, axis=0, keepdims=True)
                ),
            )
            factor = jnp.exp(highest - new_highest)
            weights0 = jnp.exp(scores0 - new_highest)
            weights1 = jnp.exp(scores1 - new_highest)
            total = (
                total * factor
                + jnp.sum(weights0, axis=0, keepdims=True)
                + jnp.sum(weights1, axis=0, keepdims=True)
            )
            acc_ref[...] = acc_ref[...] * factor + mix(first, weights0) + mix(second, weights1)
            return new_highest, total

        highest, total = lax.fori_loop(0, (count + 1) // 2, step, (highest, total))
        attended = acc_ref[...] / total
        for h in range(heads):
            out_ref[rows, h * HD : (h + 1) * HD] = attended[
                :, h * BLOCK : (h + 1) * BLOCK
            ].T.astype(jnp.bfloat16)


def attend(block_mask, queries, kv):
    return pl.pallas_call(
        attend_kernel,
        out_shape=jax.ShapeDtypeStruct(queries.shape, jnp.bfloat16),
        in_specs=[
            pl.BlockSpec(memory_space=pltpu.SMEM),
            pl.BlockSpec(memory_space=pltpu.VMEM),
            pl.BlockSpec(memory_space=pltpu.VMEM),
        ],
        out_specs=pl.BlockSpec(memory_space=pltpu.VMEM),
        scratch_shapes=[
            pltpu.SMEM((128,), jnp.int32),
            pltpu.VMEM((HD, queries.shape[1]), jnp.float32),
        ],
        compiler_params=pltpu.CompilerParams(vmem_limit_bytes=32 * MIB),
        name="attend",
    )(block_mask, queries, kv)


def ring_places():
    head = lax.axis_index("head")
    y, zh = head // 2, head % 2
    up = ((y + 1) % 4) * 2 + zh
    down = ((y + 3) % 4) * 2 + zh
    across = y * 2 + (1 - zh)
    return y, zh, up, down, across


def remote(src, dst, send_sem, recv_sem, **place):
    return pltpu.make_async_remote_copy(
        src_ref=src,
        dst_ref=dst,
        send_sem=send_sem,
        recv_sem=recv_sem,
        device_id=place,
        device_id_type=pl.DeviceIdType.MESH,
    )


OUT_CHUNKS = 4


def project_out_kernel(
    att_ref, w_hbm, out_ref, w_ref, part, far_out, far_in, near_out, near_in, z_out, z_in, w_sem,
    far_ss, far_rs, near_ss, near_rs, z_ss, z_rs,
):
    y, zh, up, down, across = ring_places()
    cw = part.shape[2]
    half = cw // 2
    loads = [
        pltpu.make_async_copy(w_hbm.at[:, pl.ds(c * cw, cw)], w_ref.at[c], w_sem.at[c])
        for c in range(OUT_CHUNKS)
    ]
    for load in loads:
        load.start()
    barrier = pltpu.get_barrier_semaphore()
    for peer in (up, down, across):
        pl.semaphore_signal(
            barrier, inc=1, device_id={"head": peer}, device_id_type=pl.DeviceIdType.MESH
        )
    pl.semaphore_wait(barrier, 3)

    def rows_of(c, place, lo):
        return part[c, pl.ds(pl.multiple_of(place * 128, 128), 128), lo : lo + half]

    def far(c, side):
        return remote(
            far_out.at[c, side], far_in.at[c, side], far_ss.at[c, side], far_rs.at[c, side],
            head=(up, down)[side],
        )

    def near(c, side, part_at):
        return remote(
            near_out.at[c, side, part_at],
            near_in.at[c, side, part_at],
            near_ss.at[c, side, part_at],
            near_rs.at[c, side, part_at],
            head=(up, down)[side],
        )

    def cross(c):
        return remote(z_out.at[c], z_in.at[c], z_ss.at[c], z_rs.at[c], head=across)

    def first(c):
        loads[c].wait()
        part[c] = jnp.dot(att_ref[...], w_ref[c], preferred_element_type=jnp.float32)
        for side in range(2):
            far_out[c, side] = rows_of(c, (y + 2) % 4, side * half).astype(jnp.bfloat16)
            far(c, side).start()
        near_out[c, 0, 1] = rows_of(c, (y + 1) % 4, half).astype(jnp.bfloat16)
        near(c, 0, 1).start()
        near_out[c, 1, 0] = rows_of(c, (y + 3) % 4, 0).astype(jnp.bfloat16)
        near(c, 1, 0).start()

    def second(c):
        far(c, 0).wait_recv()
        near_out[c, 0, 0] = (
            rows_of(c, (y + 1) % 4, 0) + far_in[c, 0].astype(jnp.float32)
        ).astype(jnp.bfloat16)
        near(c, 0, 0).start()
        far(c, 1).wait_recv()
        near_out[c, 1, 1] = (
            rows_of(c, (y + 3) % 4, half) + far_in[c, 1].astype(jnp.float32)
        ).astype(jnp.bfloat16)
        near(c, 1, 1).start()

    def third(c):
        for side in range(2):
            for at in range(2):
                near(c, side, at).wait_recv()
        mine = pl.multiple_of(y * 128, 128)
        for at in range(2):
            sl = slice(at * half, (at + 1) * half)
            other = pl.ds(pl.multiple_of((1 - zh) * 64, 64), 64)
            z_out[c, :, sl] = (
                part[c, pl.ds(pl.multiple_of(mine + (1 - zh) * 64, 64), 64), sl]
                + near_in[c, 0, at, other, :].astype(jnp.float32)
                + near_in[c, 1, at, other, :].astype(jnp.float32)
            ).astype(jnp.bfloat16)
        cross(c).start()
        for at in range(2):
            sl = slice(at * half, (at + 1) * half)
            own = pl.ds(pl.multiple_of(zh * 64, 64), 64)
            place = pl.ds(pl.multiple_of(mine + zh * 64, 64), 64)
            part[c, place, sl] = (
                part[c, place, sl]
                + near_in[c, 0, at, own, :].astype(jnp.float32)
                + near_in[c, 1, at, own, :].astype(jnp.float32)
            )

    def fourth(c):
        cross(c).wait_recv()
        place = pl.ds(pl.multiple_of(y * 128 + zh * 64, 64), 64)
        out_ref[:, c * cw : (c + 1) * cw] = (
            part[c, place, :] + z_in[c].astype(jnp.float32)
        ).astype(jnp.bfloat16)

    first(0)
    first(1)
    for c in range(OUT_CHUNKS):
        second(c)
        if c + 2 < OUT_CHUNKS:
            first(c + 2)
    for c in range(OUT_CHUNKS):
        third(c)
    for c in range(OUT_CHUNKS):
        fourth(c)
    for c in range(OUT_CHUNKS):
        for side in range(2):
            far(c, side).wait_send()
            for at in range(2):
                near(c, side, at).wait_send()
        cross(c).wait_send()


def project_out(attended, w_out):
    rows, depth = attended.shape
    width = w_out.shape[1]
    n, cw = OUT_CHUNKS, width // OUT_CHUNKS
    half = cw // 2
    bf16 = jnp.bfloat16
    dma = pltpu.SemaphoreType.DMA
    return pl.pallas_call(
        project_out_kernel,
        out_shape=jax.ShapeDtypeStruct((rows // 8, width), bf16),
        in_specs=[pl.BlockSpec(memory_space=pltpu.VMEM), pl.BlockSpec(memory_space=pl.ANY)],
        out_specs=pl.BlockSpec(memory_space=pltpu.VMEM),
        scratch_shapes=[
            pltpu.VMEM((n, depth, cw), bf16),
            pltpu.VMEM((n, rows, cw), jnp.float32),
            pltpu.VMEM((n, 2, rows // 4, half), bf16),
            pltpu.VMEM((n, 2, rows // 4, half), bf16),
            pltpu.VMEM((n, 2, 2, rows // 4, half), bf16),
            pltpu.VMEM((n, 2, 2, rows // 4, half), bf16),
            pltpu.VMEM((n, rows // 8, cw), bf16),
            pltpu.VMEM((n, rows // 8, cw), bf16),
            dma((n,)),
            dma((n, 2)),
            dma((n, 2)),
            dma((n, 2, 2)),
            dma((n, 2, 2)),
            dma((n,)),
            dma((n,)),
        ],
        compiler_params=pltpu.CompilerParams(
            collective_id=1, has_side_effects=True, vmem_limit_bytes=48 * MIB
        ),
        name="project_out",
    )(attended, w_out)


IN_CHUNKS = 2
SLOTS = 64


def gather_kernel(
    target_ref, x_ref, cos_ref, sin_ref, wq_hbm, wk_hbm, wv_hbm, q_ref, kv_ref,
    w_ref, pick, place, send, recv, meta_out, meta_in, pieces, acc,
    w_sem, row_ss, row_rs, meta_ss, meta_rs, ag_ss, ag_rs,
):
    ctx = lax.axis_index("ctx")
    peers = lax.axis_size("ctx")
    rows, cols = x_ref.shape
    chunk = cols // IN_CHUNKS
    y, zh, up, down, across = ring_places()
    own_piece = y * 2 + zh
    bf16 = jnp.bfloat16
    loads = [
        pltpu.make_async_copy(wq_hbm, w_ref.at[:, 0:512], w_sem.at[0]),
        pltpu.make_async_copy(wk_hbm, w_ref.at[:, 512:640], w_sem.at[1]),
        pltpu.make_async_copy(wv_hbm, w_ref.at[:, 640:768], w_sem.at[2]),
    ]
    for load in loads:
        load.start()
    barrier = pltpu.get_barrier_semaphore()
    for k in range(1, peers):
        pl.semaphore_signal(
            barrier, inc=1, device_id={"ctx": (ctx + k) % peers},
            device_id_type=pl.DeviceIdType.MESH,
        )
    for peer in (up, down, across):
        pl.semaphore_signal(
            barrier, inc=1, device_id={"head": peer}, device_id_type=pl.DeviceIdType.MESH
        )

    target = target_ref[...]
    owner = target // rows
    local = target - owner * rows
    owned = lax.broadcasted_iota(jnp.int32, (peers, rows), 0) == owner
    owned_f = jnp.where(owned, 1.0, 0.0).astype(jnp.float32)
    earlier = (
        lax.broadcasted_iota(jnp.int32, (rows, rows), 0)
        < lax.broadcasted_iota(jnp.int32, (rows, rows), 1)
    )
    before = jnp.dot(
        owned_f.astype(bf16),
        jnp.where(earlier, 1.0, 0.0).astype(bf16),
        preferred_element_type=jnp.float32,
    )
    rank = jnp.sum(owned_f * before, axis=0, keepdims=True)
    slot = owner * SLOTS + rank.astype(jnp.int32)
    for i in range(peers):
        at = lax.broadcasted_iota(jnp.int32, (SLOTS, rows), 0) + i * SLOTS
        pick[i * SLOTS : (i + 1) * SLOTS, :] = jnp.where(at == slot, 1.0, 0.0).astype(bf16)
    line = lax.broadcasted_iota(jnp.int32, (8, rows), 0)
    high = local // 16
    facts = jnp.where(line == 0, high, jnp.where(line == 1, local - high * 16, 1))
    facts = lax.dot_general(
        facts.astype(jnp.float32).astype(bf16), pick[...], (((1,), (1,)), ((), ())),
        preferred_element_type=jnp.float32,
    )
    goes_to = jnp.where(facts[2:3] > 0.5, facts[0:1] * 16.0 + facts[1:2], -1.0)
    goes_to = jnp.broadcast_to(goes_to, (8, peers * SLOTS))
    for i in range(peers // 2):
        tile = goes_to[:, i * 128 : (i + 1) * 128]
        meta_out[2 * i] = tile
        meta_out[2 * i + 1] = pltpu.roll(tile, SLOTS, 1)

    def meta_copy(k):
        to = (ctx + k) % peers
        return remote(meta_out.at[to], meta_in.at[k], meta_ss.at[k], meta_rs.at[k], ctx=to)

    def row_copy(f, k):
        to = (ctx + k) % peers
        return remote(
            send.at[f, pl.ds(pl.multiple_of(to * SLOTS, SLOTS), SLOTS)],
            recv.at[f, pl.ds(k * SLOTS, SLOTS)],
            row_ss.at[f, k], row_rs.at[f, k], ctx=to,
        )

    for f in range(IN_CHUNKS):
        send[f] = jnp.dot(
            pick[...], x_ref[:, f * chunk : (f + 1) * chunk], preferred_element_type=jnp.float32
        ).astype(bf16)
        if f == 0:
            pl.semaphore_wait(barrier, peers - 1 + 3)
            for k in range(1, peers):
                meta_copy(k).start()
        for k in range(1, peers):
            row_copy(f, k).start()
        recv[f, 0:SLOTS, :] = send[f, pl.ds(pl.multiple_of(ctx * SLOTS, SLOTS), SLOTS), :]
    meta_in[0] = meta_out[ctx]

    for k in range(1, peers):
        meta_copy(k).wait_recv()
    lane = lax.broadcasted_iota(jnp.int32, (8, 128), 1)
    for i in range(peers // 2):
        both = jnp.where(lane < SLOTS, meta_in[2 * i], pltpu.roll(meta_in[2 * i + 1], SLOTS, 1))
        both = both[0:1].astype(jnp.int32)
        at = lax.broadcasted_iota(jnp.int32, (rows, 128), 0)
        place[:, i * 128 : (i + 1) * 128] = jnp.where(at == both, 1.0, 0.0).astype(bf16)

    half = rows // 2
    piece = lambda dy, other: ((y + dy) % 4) * 2 + ((1 - zh) if other else zh)

    def spread(f, e):
        src, lo, n, to = (
            (piece(0, 0), 0, rows, across),
            (piece(0, 0), 0, rows, up),
            (piece(0, 0), 0, rows, down),
            (piece(3, 0), 0, half, up),
            (piece(1, 0), half, half, down),
            (piece(0, 1), 0, rows, up),
            (piece(0, 1), 0, rows, down),
            (piece(3, 1), 0, half, up),
            (piece(1, 1), half, half, down),
        )[e]
        ref = pieces.at[src, f, pl.ds(lo, n)]
        return remote(ref, ref, ag_ss.at[f, e], ag_rs.at[f, e], head=to)

    def project(f, index, first=False):
        deep = pl.ds(pl.multiple_of(index * cols + f * chunk, chunk), chunk)
        term = jnp.dot(pieces[index, f], w_ref[deep, :], preferred_element_type=jnp.float32)
        acc[...] = term if first else acc[...] + term

    for f in range(IN_CHUNKS):
        for k in range(1, peers):
            row_copy(f, k).wait_recv()
        pieces[own_piece, f] = jnp.dot(
            place[...], recv[f], preferred_element_type=jnp.float32
        ).astype(bf16)
        for e in (0, 1, 2):
            spread(f, e).start()
    for load in loads:
        load.wait()

    def near(f):
        project(f, own_piece, first=f == 0)
        spread(f, 1).wait_recv()
        spread(f, 3).start()
        spread(f, 2).wait_recv()
        spread(f, 4).start()
        spread(f, 0).wait_recv()
        spread(f, 5).start()
        spread(f, 6).start()
        project(f, piece(3, 0))
        project(f, piece(1, 0))
        project(f, piece(0, 1))

    def far(f):
        spread(f, 3).wait_recv()
        spread(f, 4).wait_recv()
        project(f, piece(2, 0))

    def near_other(f):
        spread(f, 5).wait_recv()
        spread(f, 7).start()
        spread(f, 6).wait_recv()
        spread(f, 8).start()
        project(f, piece(3, 1))
        project(f, piece(1, 1))

    def far_other(f):
        spread(f, 7).wait_recv()
        spread(f, 8).wait_recv()
        project(f, piece(2, 1))

    near(0)
    near(1)
    near_other(0)
    far(0)
    far(1)
    near_other(1)
    far_other(0)
    far_other(1)

    cosine, sine = cos_ref[...], sin_ref[...]
    for h in range(6):
        tensor = acc[:, h * HD : (h + 1) * HD]
        if h < 5:
            tensor = tensor * cosine + pltpu.roll(tensor, HD // 2, 1) * sine
        tensor = tensor.astype(bf16)
        if h < 4:
            q_ref[:, h * HD : (h + 1) * HD] = tensor
        else:
            kv_ref[:, (h - 4) * HD : (h - 3) * HD] = tensor

    for k in range(1, peers):
        meta_copy(k).wait_send()
        for f in range(IN_CHUNKS):
            row_copy(f, k).wait_send()
    for f in range(IN_CHUNKS):
        for e in range(9):
            spread(f, e).wait_send()


def gather_and_project(node_rows, node_target, cosine, sine, w_query, w_key, w_value):
    rows, cols = node_rows.shape
    peers = lax.axis_size("ctx")
    chunk = cols // IN_CHUNKS
    bf16 = jnp.bfloat16
    dma = pltpu.SemaphoreType.DMA
    vmem = pl.BlockSpec(memory_space=pltpu.VMEM)
    anywhere = pl.BlockSpec(memory_space=pl.ANY)
    return pl.pallas_call(
        gather_kernel,
        out_shape=(
            jax.ShapeDtypeStruct((rows, 512), bf16),
            jax.ShapeDtypeStruct((rows, 256), bf16),
        ),
        in_specs=[vmem, vmem, vmem, vmem, anywhere, anywhere, anywhere],
        out_specs=(vmem, vmem),
        scratch_shapes=[
            pltpu.VMEM((w_query.shape[0], 768), bf16),
            pltpu.VMEM((peers * SLOTS, rows), bf16),
            pltpu.VMEM((rows, peers * SLOTS), bf16),
            pltpu.VMEM((IN_CHUNKS, peers * SLOTS, chunk), bf16),
            pltpu.VMEM((IN_CHUNKS, peers * SLOTS, chunk), bf16),
            pltpu.VMEM((peers, 8, 128), jnp.float32),
            pltpu.VMEM((peers, 8, 128), jnp.float32),
            pltpu.VMEM((8, IN_CHUNKS, rows, chunk), bf16),
            pltpu.VMEM((rows, 768), jnp.float32),
            dma((3,)),
            dma((IN_CHUNKS, peers)),
            dma((IN_CHUNKS, peers)),
            dma((peers,)),
            dma((peers,)),
            dma((IN_CHUNKS, 9)),
            dma((IN_CHUNKS, 9)),
        ],
        compiler_params=pltpu.CompilerParams(
            collective_id=2, has_side_effects=True, vmem_limit_bytes=48 * MIB
        ),
        name="gather_and_project",
    )(node_target.reshape(1, rows), node_rows, cosine, sine, w_query, w_key, w_value)


def on_device(node_rows, node_target, node_position, block_mask, w_query, w_key, w_value, w_out):
    cosine, sine = rotary_tables(node_position, HD)
    queries, kv_local = gather_and_project(
        node_rows, node_target, cosine, sine, w_query, w_key, w_value
    )
    kv = lax.all_gather(kv_local, "ctx", axis=0, tiled=True)
    attended = attend(block_mask, queries, kv)
    return project_out(attended, w_out)


def solution(mesh):
    placed = (
        P("ctx", "head"),
        P("ctx"),
        P("ctx"),
        P("ctx", None),
        P(None, "head"),
        P(None, "head"),
        P(None, "head"),
        P("head", None),
    )
    return jax.shard_map(
        on_device, mesh=mesh, in_specs=placed, out_specs=P(("ctx", "head"), None), check_vma=False
    )
```

```python
import math

import jax
import jax.numpy as jnp
from jax import lax
from jax.experimental import pallas as pl
from jax.experimental.pallas import tpu as pltpu
from jax.sharding import PartitionSpec as P

HD = 128
BLOCK = 128
ROPE_THETA = 500000.0
NEG_LARGE = -1e30
MIB = 1024 * 1024


def rotary_tables(positions, head_size):
    half_size = head_size // 2
    inverse = jnp.exp(
        jnp.arange(half_size, dtype=jnp.float32) * (-2.0 * math.log(ROPE_THETA) / head_size)
    )
    angles = positions.astype(jnp.float32)[:, None] * inverse[None, :]
    cosine = jnp.cos(angles)
    sine = jnp.sin(angles)
    return jnp.concatenate([cosine, cosine], axis=-1), jnp.concatenate([-sine, sine], axis=-1)


def attend_kernel(mask_ref, q_ref, kv_ref, out_ref, list_ref, acc_ref):
    ctx = lax.axis_index("ctx")
    local_blocks = q_ref.shape[0] // BLOCK
    heads = q_ref.shape[1] // HD
    block_count = mask_ref.shape[1]
    width = heads * BLOCK
    scale = 1.0 / math.sqrt(HD)

    for b in range(local_blocks):
        qb = ctx * local_blocks + b

        def build(kb, n):
            list_ref[n] = kb
            return n + jnp.where(kb < qb, mask_ref[b, kb], 0)

        count = lax.fori_loop(0, block_count, build, 0, unroll=8)
        list_ref[count] = 0
        rows = pl.ds(b * BLOCK, BLOCK)
        queries = jnp.concatenate(
            [q_ref[rows, h * HD : (h + 1) * HD] for h in range(heads)], axis=0
        )

        def scores_of(kb):
            keys = kv_ref[pl.ds(pl.multiple_of(kb * BLOCK, BLOCK), BLOCK), 0:HD]
            return (
                lax.dot_general(
                    keys, queries, (((1,), (1,)), ((), ())), preferred_element_type=jnp.float32
                )
                * scale
            )

        def mix(kb, weights):
            values = kv_ref[pl.ds(pl.multiple_of(kb * BLOCK, BLOCK), BLOCK), HD : 2 * HD]
            return lax.dot_general(
                values,
                weights.astype(jnp.bfloat16),
                (((0,), (0,)), ((), ())),
                preferred_element_type=jnp.float32,
            )

        key_at = lax.broadcasted_iota(jnp.int32, (BLOCK, width), 0)
        query_at = lax.broadcasted_iota(jnp.int32, (BLOCK, width), 1) % BLOCK
        scores = jnp.where(key_at <= query_at, scores_of(qb), NEG_LARGE)
        highest = jnp.max(scores, axis=0, keepdims=True)
        weights = jnp.exp(scores - highest)
        total = jnp.sum(weights, axis=0, keepdims=True)
        acc_ref[...] = mix(qb, weights)

        def step(i, state):
            highest, total = state
            first = list_ref[2 * i]
            second = list_ref[2 * i + 1]
            has_second = 2 * i + 1 < count
            second = jnp.where(has_second, second, 0)
            drop = jnp.where(has_second, 0.0, NEG_LARGE).astype(jnp.float32)
            scores0 = scores_of(first)
            scores1 = scores_of(second) + drop
            new_highest = jnp.maximum(
                highest,
                jnp.maximum(
                    jnp.max(scores0, axis=0, keepdims=True), jnp.max(scores1, axis=0, keepdims=True)
                ),
            )
            factor = jnp.exp(highest - new_highest)
            weights0 = jnp.exp(scores0 - new_highest)
            weights1 = jnp.exp(scores1 - new_highest)
            total = (
                total * factor
                + jnp.sum(weights0, axis=0, keepdims=True)
                + jnp.sum(weights1, axis=0, keepdims=True)
            )
            acc_ref[...] = acc_ref[...] * factor + mix(first, weights0) + mix(second, weights1)
            return new_highest, total

        highest, total = lax.fori_loop(0, (count + 1) // 2, step, (highest, total))
        attended = acc_ref[...] / total
        for h in range(heads):
            out_ref[rows, h * HD : (h + 1) * HD] = attended[
                :, h * BLOCK : (h + 1) * BLOCK
            ].T.astype(jnp.bfloat16)


def attend(block_mask, queries, kv):
    return pl.pallas_call(
        attend_kernel,
        out_shape=jax.ShapeDtypeStruct(queries.shape, jnp.bfloat16),
        in_specs=[
            pl.BlockSpec(memory_space=pltpu.SMEM),
            pl.BlockSpec(memory_space=pltpu.VMEM),
            pl.BlockSpec(memory_space=pltpu.VMEM),
        ],
        out_specs=pl.BlockSpec(memory_space=pltpu.VMEM),
        scratch_shapes=[
            pltpu.SMEM((128,), jnp.int32),
            pltpu.VMEM((HD, queries.shape[1]), jnp.float32),
        ],
        compiler_params=pltpu.CompilerParams(vmem_limit_bytes=32 * MIB),
        name="attend",
    )(block_mask, queries, kv)


def ring_places():
    head = lax.axis_index("head")
    y, zh = head // 2, head % 2
    up = ((y + 1) % 4) * 2 + zh
    down = ((y + 3) % 4) * 2 + zh
    across = y * 2 + (1 - zh)
    return y, zh, up, down, across


def remote(src, dst, send_sem, recv_sem, **place):
    return pltpu.make_async_remote_copy(
        src_ref=src,
        dst_ref=dst,
        send_sem=send_sem,
        recv_sem=recv_sem,
        device_id=place,
        device_id_type=pl.DeviceIdType.MESH,
    )


OUT_CHUNKS = 4


def project_out_kernel(
    att_ref, w_hbm, out_ref, w_ref, part, far_out, far_in, near_out, near_in, z_out, z_in, w_sem,
    far_ss, far_rs, near_ss, near_rs, z_ss, z_rs,
):
    y, zh, up, down, across = ring_places()
    cw = part.shape[2]
    half = cw // 2
    loads = [
        pltpu.make_async_copy(w_hbm.at[:, pl.ds(c * cw, cw)], w_ref.at[c], w_sem.at[c])
        for c in range(OUT_CHUNKS)
    ]
    for load in loads:
        load.start()
    barrier = pltpu.get_barrier_semaphore()
    for peer in (up, down, across):
        pl.semaphore_signal(
            barrier, inc=1, device_id={"head": peer}, device_id_type=pl.DeviceIdType.MESH
        )
    pl.semaphore_wait(barrier, 3)

    def rows_of(c, place, lo):
        return part[c, pl.ds(pl.multiple_of(place * 128, 128), 128), lo : lo + half]

    def far(c, side):
        return remote(
            far_out.at[c, side], far_in.at[c, side], far_ss.at[c, side], far_rs.at[c, side],
            head=(up, down)[side],
        )

    def near(c, side, part_at):
        return remote(
            near_out.at[c, side, part_at],
            near_in.at[c, side, part_at],
            near_ss.at[c, side, part_at],
            near_rs.at[c, side, part_at],
            head=(up, down)[side],
        )

    def cross(c):
        return remote(z_out.at[c], z_in.at[c], z_ss.at[c], z_rs.at[c], head=across)

    def first(c):
        loads[c].wait()
        part[c] = jnp.dot(att_ref[...], w_ref[c], preferred_element_type=jnp.float32)
        for side in range(2):
            far_out[c, side] = rows_of(c, (y + 2) % 4, side * half).astype(jnp.bfloat16)
            far(c, side).start()
        near_out[c, 0, 1] = rows_of(c, (y + 1) % 4, half).astype(jnp.bfloat16)
        near(c, 0, 1).start()
        near_out[c, 1, 0] = rows_of(c, (y + 3) % 4, 0).astype(jnp.bfloat16)
        near(c, 1, 0).start()

    def second(c):
        far(c, 0).wait_recv()
        near_out[c, 0, 0] = (
            rows_of(c, (y + 1) % 4, 0) + far_in[c, 0].astype(jnp.float32)
        ).astype(jnp.bfloat16)
        near(c, 0, 0).start()
        far(c, 1).wait_recv()
        near_out[c, 1, 1] = (
            rows_of(c, (y + 3) % 4, half) + far_in[c, 1].astype(jnp.float32)
        ).astype(jnp.bfloat16)
        near(c, 1, 1).start()

    def third(c):
        for side in range(2):
            for at in range(2):
                near(c, side, at).wait_recv()
        mine = pl.multiple_of(y * 128, 128)
        for at in range(2):
            sl = slice(at * half, (at + 1) * half)
            other = pl.ds(pl.multiple_of((1 - zh) * 64, 64), 64)
            z_out[c, :, sl] = (
                part[c, pl.ds(pl.multiple_of(mine + (1 - zh) * 64, 64), 64), sl]
                + near_in[c, 0, at, other, :].astype(jnp.float32)
                + near_in[c, 1, at, other, :].astype(jnp.float32)
            ).astype(jnp.bfloat16)
        cross(c).start()
        for at in range(2):
            sl = slice(at * half, (at + 1) * half)
            own = pl.ds(pl.multiple_of(zh * 64, 64), 64)
            place = pl.ds(pl.multiple_of(mine + zh * 64, 64), 64)
            part[c, place, sl] = (
                part[c, place, sl]
                + near_in[c, 0, at, own, :].astype(jnp.float32)
                + near_in[c, 1, at, own, :].astype(jnp.float32)
            )

    def fourth(c):
        cross(c).wait_recv()
        place = pl.ds(pl.multiple_of(y * 128 + zh * 64, 64), 64)
        out_ref[:, c * cw : (c + 1) * cw] = (
            part[c, place, :] + z_in[c].astype(jnp.float32)
        ).astype(jnp.bfloat16)

    first(0)
    first(1)
    for c in range(OUT_CHUNKS):
        second(c)
        if c + 2 < OUT_CHUNKS:
            first(c + 2)
    for c in range(OUT_CHUNKS):
        third(c)
    for c in range(OUT_CHUNKS):
        fourth(c)
    for c in range(OUT_CHUNKS):
        for side in range(2):
            far(c, side).wait_send()
            for at in range(2):
                near(c, side, at).wait_send()
        cross(c).wait_send()


def project_out(attended, w_out):
    rows, depth = attended.shape
    width = w_out.shape[1]
    n, cw = OUT_CHUNKS, width // OUT_CHUNKS
    half = cw // 2
    bf16 = jnp.bfloat16
    dma = pltpu.SemaphoreType.DMA
    return pl.pallas_call(
        project_out_kernel,
        out_shape=jax.ShapeDtypeStruct((rows // 8, width), bf16),
        in_specs=[pl.BlockSpec(memory_space=pltpu.VMEM), pl.BlockSpec(memory_space=pl.ANY)],
        out_specs=pl.BlockSpec(memory_space=pltpu.VMEM),
        scratch_shapes=[
            pltpu.VMEM((n, depth, cw), bf16),
            pltpu.VMEM((n, rows, cw), jnp.float32),
            pltpu.VMEM((n, 2, rows // 4, half), bf16),
            pltpu.VMEM((n, 2, rows // 4, half), bf16),
            pltpu.VMEM((n, 2, 2, rows // 4, half), bf16),
            pltpu.VMEM((n, 2, 2, rows // 4, half), bf16),
            pltpu.VMEM((n, rows // 8, cw), bf16),
            pltpu.VMEM((n, rows // 8, cw), bf16),
            dma((n,)),
            dma((n, 2)),
            dma((n, 2)),
            dma((n, 2, 2)),
            dma((n, 2, 2)),
            dma((n,)),
            dma((n,)),
        ],
        compiler_params=pltpu.CompilerParams(
            collective_id=1, has_side_effects=True, vmem_limit_bytes=48 * MIB
        ),
        name="project_out",
    )(attended, w_out)


IN_CHUNKS = 4
PARTS = 2
SLOTS = 64


def gather_kernel(
    target_ref, x_hbm, cos_hbm, sin_hbm, wq_hbm, wk_hbm, wv_hbm, q_ref, kv_ref,
    x_ref, cos_ref, sin_ref, w_ref, pick, place, send, recv, meta_out, meta_in, pieces, acc,
    kv_own, in_sem, row_ss, row_rs, meta_ss, meta_rs, ag_ss, ag_rs, kv_sem, kv_ss, kv_rs,
):
    ctx = lax.axis_index("ctx")
    peers = lax.axis_size("ctx")
    rows, cols = x_ref.shape
    chunk = cols // IN_CHUNKS
    part_rows = rows // PARTS
    y, zh, up, down, across = ring_places()
    bf16 = jnp.bfloat16
    loads = [
        pltpu.make_async_copy(src, dst, in_sem.at[i])
        for i, (src, dst) in enumerate(
            (
                (x_hbm, x_ref),
                (wq_hbm, w_ref.at[:, 0:512]),
                (wk_hbm, w_ref.at[:, 512:640]),
                (wv_hbm, w_ref.at[:, 640:768]),
                (cos_hbm, cos_ref),
                (sin_hbm, sin_ref),
            )
        )
    ]
    for load in loads:
        load.start()
    barrier = pltpu.get_barrier_semaphore()
    for k in range(1, peers):
        pl.semaphore_signal(
            barrier, inc=1, device_id={"ctx": (ctx + k) % peers},
            device_id_type=pl.DeviceIdType.MESH,
        )
    for peer in (up, down, across):
        pl.semaphore_signal(
            barrier, inc=1, device_id={"head": peer}, device_id_type=pl.DeviceIdType.MESH
        )

    target = target_ref[...]
    owner = target // rows
    local = target - owner * rows
    owned = lax.broadcasted_iota(jnp.int32, (peers, rows), 0) == owner
    owned_f = jnp.where(owned, 1.0, 0.0).astype(jnp.float32)
    earlier = (
        lax.broadcasted_iota(jnp.int32, (rows, rows), 0)
        < lax.broadcasted_iota(jnp.int32, (rows, rows), 1)
    )
    before = jnp.dot(
        owned_f.astype(bf16),
        jnp.where(earlier, 1.0, 0.0).astype(bf16),
        preferred_element_type=jnp.float32,
    )
    rank = jnp.sum(owned_f * before, axis=0, keepdims=True)
    slot = owner * SLOTS + rank.astype(jnp.int32)
    for i in range(peers):
        at = lax.broadcasted_iota(jnp.int32, (SLOTS, rows), 0) + i * SLOTS
        pick[i * SLOTS : (i + 1) * SLOTS, :] = jnp.where(at == slot, 1.0, 0.0).astype(bf16)

    def meta_copy(k):
        to = (ctx + k) % peers
        return remote(meta_out.at[to], meta_in.at[k], meta_ss.at[k], meta_rs.at[k], ctx=to)

    def row_copy(f, k):
        to = (ctx + k) % peers
        return remote(
            send.at[f, pl.ds(pl.multiple_of(to * SLOTS, SLOTS), SLOTS)],
            recv.at[f, pl.ds(k * SLOTS, SLOTS)],
            row_ss.at[f, k], row_rs.at[f, k], ctx=to,
        )

    loads[0].wait()
    for f in range(IN_CHUNKS):
        send[f] = jnp.dot(
            pick[...], x_ref[:, f * chunk : (f + 1) * chunk], preferred_element_type=jnp.float32
        ).astype(bf16)
        if f == 0:
            pl.semaphore_wait(barrier, peers - 1 + 3)
        for k in range(1, peers):
            row_copy(f, k).start()
        recv[f, 0:SLOTS, :] = send[f, pl.ds(pl.multiple_of(ctx * SLOTS, SLOTS), SLOTS), :]
        if f == 0:
            line = lax.broadcasted_iota(jnp.int32, (8, rows), 0)
            high = local // 16
            facts = jnp.where(line == 0, high, jnp.where(line == 1, local - high * 16, 1))
            facts = lax.dot_general(
                facts.astype(jnp.float32).astype(bf16), pick[...], (((1,), (1,)), ((), ())),
                preferred_element_type=jnp.float32,
            )
            goes_to = jnp.where(facts[2:3] > 0.5, facts[0:1] * 16.0 + facts[1:2], -1.0)
            goes_to = jnp.broadcast_to(goes_to, (8, peers * SLOTS))
            for i in range(peers // 2):
                tile = goes_to[:, i * 128 : (i + 1) * 128]
                meta_out[2 * i] = tile
                meta_out[2 * i + 1] = pltpu.roll(tile, SLOTS, 1)
            for k in range(1, peers):
                meta_copy(k).start()
            meta_in[0] = meta_out[ctx]

    for k in range(1, peers):
        meta_copy(k).wait_recv()
    lane = lax.broadcasted_iota(jnp.int32, (8, 128), 1)
    for i in range(peers // 2):
        both = jnp.where(lane < SLOTS, meta_in[2 * i], pltpu.roll(meta_in[2 * i + 1], SLOTS, 1))
        both = both[0:1].astype(jnp.int32)
        at = lax.broadcasted_iota(jnp.int32, (rows, 128), 0)
        place[:, i * 128 : (i + 1) * 128] = jnp.where(at == both, 1.0, 0.0).astype(bf16)

    half = part_rows // 2

    def piece(dy, other):
        return ((y + dy) % 4) * 2 + ((1 - zh) if other else zh)

    def spread(n, e):
        part, f = divmod(n, IN_CHUNKS)
        src, lo, size, to = (
            (piece(0, 0), 0, part_rows, across),
            (piece(0, 0), 0, part_rows, up),
            (piece(0, 0), 0, part_rows, down),
            (piece(3, 0), 0, half, up),
            (piece(1, 0), half, half, down),
            (piece(0, 1), 0, part_rows, up),
            (piece(0, 1), 0, part_rows, down),
            (piece(2, 0), 0, part_rows, across),
        )[e]
        ref = pieces.at[src, part, f, pl.ds(lo, size)]
        return remote(ref, ref, ag_ss.at[n, e], ag_rs.at[n, e], head=to)

    def project(n, index, first=False):
        part, f = divmod(n, IN_CHUNKS)
        if f < IN_CHUNKS - 1:
            return
        piece_rows = jnp.concatenate(
            [pieces[index, part, g] for g in range(IN_CHUNKS)], axis=1
        )
        deep = pl.ds(pl.multiple_of(index * cols, cols), cols)
        term = jnp.dot(piece_rows, w_ref[deep, :], preferred_element_type=jnp.float32)
        acc[part] = term if first else acc[part] + term

    def begin(n):
        part, f = divmod(n, IN_CHUNKS)
        if part == 0:
            for k in range(1, peers):
                row_copy(f, k).wait_recv()
        here = slice(part * part_rows, (part + 1) * part_rows)
        pieces[piece(0, 0), part, f] = jnp.dot(
            place[here, :], recv[f], preferred_element_type=jnp.float32
        ).astype(bf16)
        for e in (1, 2, 0):
            spread(n, e).start()
        if n == IN_CHUNKS - 1:
            for load in loads[1:]:
                load.wait()
        project(n, piece(0, 0), first=True)

    def near(n):
        spread(n, 1).wait_recv()
        spread(n, 3).start()
        spread(n, 2).wait_recv()
        spread(n, 4).start()
        spread(n, 0).wait_recv()
        spread(n, 5).start()
        spread(n, 6).start()
        project(n, piece(3, 0))
        project(n, piece(1, 0))
        project(n, piece(0, 1))

    def far(n):
        spread(n, 3).wait_recv()
        spread(n, 4).wait_recv()
        spread(n, 7).start()
        project(n, piece(2, 0))

    def other(n):
        spread(n, 5).wait_recv()
        spread(n, 6).wait_recv()
        project(n, piece(3, 1))
        project(n, piece(1, 1))
        spread(n, 7).wait_recv()
        project(n, piece(2, 1))

    zl, x, core = ctx // 8, (ctx // 2) % 4, ctx % 2
    kv_half = part_rows // 2

    def block(dx, other_z, other_core=0):
        z = (1 - zl) if other_z else zl
        c = (1 - core) if other_core else core
        return z * 8 + ((x + dx) % 4) * 2 + c

    kv_pieces = ((0, 0), (0, 1), (3, 0), (1, 0), (2, 0), (3, 1), (1, 1), (2, 1))

    def share(part, e):
        right, left, over = block(1, 0), block(3, 0), block(0, 1)
        if e >= 8:
            src, lo, size, to = block(*kv_pieces[e - 8]), 0, part_rows, block(0, 0, 1)
        else:
            src, lo, size, to = (
                (block(0, 0), 0, part_rows, over),
                (block(0, 0), 0, part_rows, right),
                (block(0, 0), 0, part_rows, left),
                (block(3, 0), 0, kv_half, right),
                (block(1, 0), kv_half, kv_half, left),
                (block(0, 1), 0, part_rows, right),
                (block(0, 1), 0, part_rows, left),
                (block(2, 0), 0, part_rows, over),
            )[e]
        ref = kv_ref.at[
            pl.ds(pl.multiple_of(src * rows + part * part_rows + lo, 16), size)
        ]
        source = kv_own.at[part] if e in (0, 1, 2, 8) else ref
        return remote(source, ref, kv_ss.at[part, e], kv_rs.at[part, e], ctx=to)

    def keep(part):
        at = pl.ds(pl.multiple_of(ctx * rows + part * part_rows, 16), part_rows)
        return pltpu.make_async_copy(kv_own.at[part], kv_ref.at[at], kv_sem.at[part])

    def finish(part):
        here = slice(part * part_rows, (part + 1) * part_rows)
        cosine, sine = cos_ref[here, :], sin_ref[here, :]
        for h in (4, 5, 0, 1, 2, 3):
            tensor = acc[part, :, h * HD : (h + 1) * HD]
            if h < 5:
                tensor = tensor * cosine + pltpu.roll(tensor, HD // 2, 1) * sine
            tensor = tensor.astype(bf16)
            if h < 4:
                q_ref[here, h * HD : (h + 1) * HD] = tensor
            else:
                kv_own[part, :, (h - 4) * HD : (h - 3) * HD] = tensor
            if h == 5:
                for e in (1, 2, 0, 8):
                    share(part, e).start()
                keep(part).start()

    def share_near(part):
        share(part, 1).wait_recv()
        share(part, 3).start()
        share(part, 10).start()
        share(part, 2).wait_recv()
        share(part, 4).start()
        share(part, 11).start()
        share(part, 0).wait_recv()
        share(part, 5).start()
        share(part, 6).start()
        share(part, 9).start()

    def share_far(part):
        share(part, 3).wait_recv()
        share(part, 4).wait_recv()
        share(part, 7).start()
        share(part, 12).start()

    def share_other(part):
        share(part, 5).wait_recv()
        share(part, 13).start()
        share(part, 6).wait_recv()
        share(part, 14).start()
        share(part, 7).wait_recv()
        share(part, 15).start()

    count = IN_CHUNKS * PARTS
    begin(0)
    begin(1)
    for n in range(count + 2):
        if n < count:
            near(n)
        if n + 2 < count:
            begin(n + 2)
        if 1 <= n <= count:
            far(n - 1)
        if n >= 2:
            other(n - 2)
        if n == IN_CHUNKS + 1:
            finish(0)
        if n == IN_CHUNKS + 2:
            share_near(0)
        if n == IN_CHUNKS + 3:
            share_far(0)
    finish(1)
    share_other(0)
    share_near(1)
    share_far(1)
    share_other(1)
    for part in range(PARTS):
        for e in range(8, 16):
            share(part, e).wait_recv()

    for k in range(1, peers):
        meta_copy(k).wait_send()
        for f in range(IN_CHUNKS):
            row_copy(f, k).wait_send()
    for n in range(count):
        for e in range(8):
            spread(n, e).wait_send()
    for part in range(PARTS):
        keep(part).wait()
        for e in range(16):
            share(part, e).wait_send()


def gather_and_project(node_rows, node_target, cosine, sine, w_query, w_key, w_value):
    rows, cols = node_rows.shape
    peers = lax.axis_size("ctx")
    chunk = cols // IN_CHUNKS
    part_rows = rows // PARTS
    bf16 = jnp.bfloat16
    dma = pltpu.SemaphoreType.DMA
    vmem = pl.BlockSpec(memory_space=pltpu.VMEM)
    hbm = pl.BlockSpec(memory_space=pltpu.HBM)
    return pl.pallas_call(
        gather_kernel,
        out_shape=(
            jax.ShapeDtypeStruct((rows, 512), bf16),
            jax.ShapeDtypeStruct((rows * peers, 256), bf16),
        ),
        in_specs=[vmem] + [hbm] * 6,
        out_specs=(vmem, hbm),
        scratch_shapes=[
            pltpu.VMEM((rows, cols), bf16),
            pltpu.VMEM((rows, HD), jnp.float32),
            pltpu.VMEM((rows, HD), jnp.float32),
            pltpu.VMEM((w_query.shape[0], 768), bf16),
            pltpu.VMEM((peers * SLOTS, rows), bf16),
            pltpu.VMEM((rows, peers * SLOTS), bf16),
            pltpu.VMEM((IN_CHUNKS, peers * SLOTS, chunk), bf16),
            pltpu.VMEM((IN_CHUNKS, peers * SLOTS, chunk), bf16),
            pltpu.VMEM((peers, 8, 128), jnp.float32),
            pltpu.VMEM((peers, 8, 128), jnp.float32),
            pltpu.VMEM((8, PARTS, IN_CHUNKS, part_rows, chunk), bf16),
            pltpu.VMEM((PARTS, part_rows, 768), jnp.float32),
            pltpu.VMEM((PARTS, part_rows, 256), bf16),
            dma((6,)),
            dma((IN_CHUNKS, peers)),
            dma((IN_CHUNKS, peers)),
            dma((peers,)),
            dma((peers,)),
            dma((PARTS * IN_CHUNKS, 8)),
            dma((PARTS * IN_CHUNKS, 8)),
            dma((PARTS,)),
            dma((PARTS, 16)),
            dma((PARTS, 16)),
        ],
        compiler_params=pltpu.CompilerParams(
            collective_id=2, has_side_effects=True, vmem_limit_bytes=48 * MIB
        ),
        name="gather_and_project",
    )(node_target.reshape(1, rows), node_rows, cosine, sine, w_query, w_key, w_value)


def on_device(node_rows, node_target, node_position, block_mask, w_query, w_key, w_value, w_out):
    cosine, sine = rotary_tables(node_position, HD)
    queries, kv = gather_and_project(
        node_rows, node_target, cosine, sine, w_query, w_key, w_value
    )
    attended = attend(block_mask, queries, kv)
    return project_out(attended, w_out)


def solution(mesh):
    placed = (
        P("ctx", "head"),
        P("ctx"),
        P("ctx"),
        P("ctx", None),
        P(None, "head"),
        P(None, "head"),
        P(None, "head"),
        P("head", None),
    )
    return jax.shard_map(
        on_device, mesh=mesh, in_specs=placed, out_specs=P(("ctx", "head"), None), check_vma=False
    )
```

```python
import math

import jax
import jax.numpy as jnp
from jax import lax
from jax.experimental import pallas as pl
from jax.experimental.pallas import tpu as pltpu
from jax.sharding import PartitionSpec as P

HD = 128
BLOCK = 128
ROPE_THETA = 500000.0
NEG_LARGE = -1e30
MIB = 1024 * 1024


def rotary_tables(positions, head_size):
    half_size = head_size // 2
    inverse = jnp.exp(
        jnp.arange(half_size, dtype=jnp.float32) * (-2.0 * math.log(ROPE_THETA) / head_size)
    )
    angles = positions.astype(jnp.float32)[:, None] * inverse[None, :]
    cosine = jnp.cos(angles)
    sine = jnp.sin(angles)
    return jnp.concatenate([cosine, cosine], axis=-1), jnp.concatenate([-sine, sine], axis=-1)


def attend_kernel(mask_ref, q_ref, kv_ref, out_ref, list_ref, acc_ref):
    ctx = lax.axis_index("ctx")
    local_blocks = q_ref.shape[0] // BLOCK
    heads = q_ref.shape[1] // HD
    block_count = mask_ref.shape[1]
    width = heads * BLOCK
    scale = 1.0 / math.sqrt(HD)

    for b in range(local_blocks):
        qb = ctx * local_blocks + b

        def build(kb, n):
            list_ref[n] = kb
            return n + jnp.where(kb < qb, mask_ref[b, kb], 0)

        count = lax.fori_loop(0, block_count, build, 0, unroll=8)
        list_ref[count] = 0
        rows = pl.ds(b * BLOCK, BLOCK)
        queries = jnp.concatenate(
            [q_ref[rows, h * HD : (h + 1) * HD] for h in range(heads)], axis=0
        )

        def scores_of(kb):
            keys = kv_ref[pl.ds(pl.multiple_of(kb * BLOCK, BLOCK), BLOCK), 0:HD]
            return (
                lax.dot_general(
                    keys, queries, (((1,), (1,)), ((), ())), preferred_element_type=jnp.float32
                )
                * scale
            )

        def mix(kb, weights):
            values = kv_ref[pl.ds(pl.multiple_of(kb * BLOCK, BLOCK), BLOCK), HD : 2 * HD]
            return lax.dot_general(
                values,
                weights.astype(jnp.bfloat16),
                (((0,), (0,)), ((), ())),
                preferred_element_type=jnp.float32,
            )

        key_at = lax.broadcasted_iota(jnp.int32, (BLOCK, width), 0)
        query_at = lax.broadcasted_iota(jnp.int32, (BLOCK, width), 1) % BLOCK
        scores = jnp.where(key_at <= query_at, scores_of(qb), NEG_LARGE)
        highest = jnp.max(scores, axis=0, keepdims=True)
        weights = jnp.exp(scores - highest)
        total = jnp.sum(weights, axis=0, keepdims=True)
        acc_ref[...] = mix(qb, weights)

        def step(i, state):
            highest, total = state
            first = list_ref[2 * i]
            second = list_ref[2 * i + 1]
            has_second = 2 * i + 1 < count
            second = jnp.where(has_second, second, 0)
            drop = jnp.where(has_second, 0.0, NEG_LARGE).astype(jnp.float32)
            scores0 = scores_of(first)
            scores1 = scores_of(second) + drop
            new_highest = jnp.maximum(
                highest,
                jnp.maximum(
                    jnp.max(scores0, axis=0, keepdims=True), jnp.max(scores1, axis=0, keepdims=True)
                ),
            )
            factor = jnp.exp(highest - new_highest)
            weights0 = jnp.exp(scores0 - new_highest)
            weights1 = jnp.exp(scores1 - new_highest)
            total = (
                total * factor
                + jnp.sum(weights0, axis=0, keepdims=True)
                + jnp.sum(weights1, axis=0, keepdims=True)
            )
            acc_ref[...] = acc_ref[...] * factor + mix(first, weights0) + mix(second, weights1)
            return new_highest, total

        highest, total = lax.fori_loop(0, (count + 1) // 2, step, (highest, total))
        attended = acc_ref[...] / total
        for h in range(heads):
            out_ref[rows, h * HD : (h + 1) * HD] = attended[
                :, h * BLOCK : (h + 1) * BLOCK
            ].T.astype(jnp.bfloat16)


def attend(block_mask, queries, kv):
    return pl.pallas_call(
        attend_kernel,
        out_shape=jax.ShapeDtypeStruct(queries.shape, jnp.bfloat16),
        in_specs=[
            pl.BlockSpec(memory_space=pltpu.SMEM),
            pl.BlockSpec(memory_space=pltpu.VMEM),
            pl.BlockSpec(memory_space=pltpu.VMEM),
        ],
        out_specs=pl.BlockSpec(memory_space=pltpu.VMEM),
        scratch_shapes=[
            pltpu.SMEM((128,), jnp.int32),
            pltpu.VMEM((HD, queries.shape[1]), jnp.float32),
        ],
        compiler_params=pltpu.CompilerParams(vmem_limit_bytes=60 * MIB),
        name="attend",
    )(block_mask, queries, kv)


def ring_places():
    head = lax.axis_index("head")
    y, zh = head // 2, head % 2
    up = ((y + 1) % 4) * 2 + zh
    down = ((y + 3) % 4) * 2 + zh
    across = y * 2 + (1 - zh)
    return y, zh, up, down, across


def remote(src, dst, send_sem, recv_sem, **place):
    return pltpu.make_async_remote_copy(
        src_ref=src,
        dst_ref=dst,
        send_sem=send_sem,
        recv_sem=recv_sem,
        device_id=place,
        device_id_type=pl.DeviceIdType.MESH,
    )


OUT_CHUNKS = 8


def project_out_kernel(
    att_ref, w_hbm, out_ref, w_ref, part, far_out, far_in, near_out, near_in, other_out, other_in,
    z_out, z_in, w_sem, far_ss, far_rs, near_ss, near_rs, other_ss, other_rs, z_ss, z_rs,
):
    y, zh, up, down, across = ring_places()
    cw = part.shape[2]
    half = cw // 2
    seat = part.shape[1] // 8
    loads = [
        pltpu.make_async_copy(w_hbm.at[:, pl.ds(c * cw, cw)], w_ref.at[c], w_sem.at[c])
        for c in range(OUT_CHUNKS)
    ]
    for load in loads:
        load.start()
    barrier = pltpu.get_barrier_semaphore()
    for peer in (up, down, across):
        pl.semaphore_signal(
            barrier, inc=1, device_id={"head": peer}, device_id_type=pl.DeviceIdType.MESH
        )

    def rows_of(c, dy, other, lo=0, size=None):
        index = ((y + dy) % 4) * 2 + ((1 - zh) if other else zh)
        return part[
            c, pl.ds(pl.multiple_of(index * seat, seat), seat), lo : lo + (size or cw)
        ]

    def far(c, side):
        return remote(
            far_out.at[c, side], far_in.at[c, side], far_ss.at[c, side], far_rs.at[c, side],
            head=(up, down)[side],
        )

    def near(c, side, at):
        return remote(
            near_out.at[c, side, at], near_in.at[c, side, at],
            near_ss.at[c, side, at], near_rs.at[c, side, at],
            head=(up, down)[side],
        )

    def other(c, side):
        return remote(
            other_out.at[c, side], other_in.at[c, side], other_ss.at[c, side],
            other_rs.at[c, side], head=(up, down)[side],
        )

    def cross(c, which):
        return remote(
            z_out.at[c, which], z_in.at[c, which], z_ss.at[c, which], z_rs.at[c, which],
            head=across,
        )

    f32, bf16 = jnp.float32, jnp.bfloat16

    def first(c):
        loads[c].wait()
        part[c] = jnp.dot(att_ref[...], w_ref[c], preferred_element_type=f32)
        if c == 0:
            pl.semaphore_wait(barrier, 3)
        z_out[c, 0] = rows_of(c, 2, True).astype(bf16)
        cross(c, 0).start()
        for side, dy in ((0, 1), (1, 3)):
            other_out[c, side] = rows_of(c, dy, True).astype(bf16)
            other(c, side).start()
        near_out[c, 0, 1] = rows_of(c, 1, False, half, half).astype(bf16)
        near(c, 0, 1).start()
        near_out[c, 1, 0] = rows_of(c, 3, False, 0, half).astype(bf16)
        near(c, 1, 0).start()

    def second(c):
        cross(c, 0).wait_recv()
        for side in range(2):
            far_out[c, side] = (
                rows_of(c, 2, False, side * half, half)
                + z_in[c, 0, :, side * half : (side + 1) * half].astype(f32)
            ).astype(bf16)
            far(c, side).start()

    def third(c):
        for side, dy in ((0, 1), (1, 3)):
            far(c, side).wait_recv()
            near_out[c, side, side] = (
                rows_of(c, dy, False, side * half, half) + far_in[c, side].astype(f32)
            ).astype(bf16)
            near(c, side, side).start()

    def fourth(c):
        other(c, 0).wait_recv()
        other(c, 1).wait_recv()
        z_out[c, 1] = (
            rows_of(c, 0, True) + other_in[c, 0].astype(f32) + other_in[c, 1].astype(f32)
        ).astype(bf16)
        cross(c, 1).start()

    def fifth(c):
        for side in range(2):
            for at in range(2):
                near(c, side, at).wait_recv()
        cross(c, 1).wait_recv()
        for at in range(2):
            here = slice(at * half, (at + 1) * half)
            out_ref[:, c * cw + at * half : c * cw + (at + 1) * half] = (
                rows_of(c, 0, False, at * half, half)
                + near_in[c, 0, at].astype(f32)
                + near_in[c, 1, at].astype(f32)
                + z_in[c, 1, :, here].astype(f32)
            ).astype(bf16)

    first(0)
    first(1)
    for n in range(OUT_CHUNKS + 3):
        if n < OUT_CHUNKS:
            second(n)
        if n + 2 < OUT_CHUNKS:
            first(n + 2)
        if 1 <= n <= OUT_CHUNKS:
            third(n - 1)
            fourth(n - 1)
        if n >= 3:
            fifth(n - 3)
    for c in range(OUT_CHUNKS):
        for side in range(2):
            far(c, side).wait_send()
            other(c, side).wait_send()
            cross(c, side).wait_send()
            for at in range(2):
                near(c, side, at).wait_send()


def project_out(attended, w_out):
    rows, depth = attended.shape
    width = w_out.shape[1]
    n, cw = OUT_CHUNKS, width // OUT_CHUNKS
    half = cw // 2
    seat = rows // 8
    bf16 = jnp.bfloat16
    dma = pltpu.SemaphoreType.DMA
    return pl.pallas_call(
        project_out_kernel,
        out_shape=jax.ShapeDtypeStruct((seat, width), bf16),
        in_specs=[
            pl.BlockSpec(memory_space=pltpu.VMEM),
            pl.BlockSpec(memory_space=pltpu.HBM),
        ],
        out_specs=pl.BlockSpec(memory_space=pltpu.VMEM),
        scratch_shapes=[
            pltpu.VMEM((n, depth, cw), bf16),
            pltpu.VMEM((n, rows, cw), jnp.float32),
            pltpu.VMEM((n, 2, seat, half), bf16),
            pltpu.VMEM((n, 2, seat, half), bf16),
            pltpu.VMEM((n, 2, 2, seat, half), bf16),
            pltpu.VMEM((n, 2, 2, seat, half), bf16),
            pltpu.VMEM((n, 2, seat, cw), bf16),
            pltpu.VMEM((n, 2, seat, cw), bf16),
            pltpu.VMEM((n, 2, seat, cw), bf16),
            pltpu.VMEM((n, 2, seat, cw), bf16),
            dma((n,)),
            dma((n, 2)),
            dma((n, 2)),
            dma((n, 2, 2)),
            dma((n, 2, 2)),
            dma((n, 2)),
            dma((n, 2)),
            dma((n, 2)),
            dma((n, 2)),
        ],
        compiler_params=pltpu.CompilerParams(
            collective_id=1, has_side_effects=True, vmem_limit_bytes=60 * MIB
        ),
        name="project_out",
    )(attended, w_out)


IN_CHUNKS = 4
PARTS = 2
SLOTS = 64


def gather_kernel(
    target_ref, x_hbm, cos_hbm, sin_hbm, wq_hbm, wk_hbm, wv_hbm, q_ref, kv_ref,
    x_ref, cos_ref, sin_ref, w_ref, pick, place, send, recv, meta_out, meta_in, pieces, acc,
    kv_own, in_sem, row_ss, row_rs, meta_ss, meta_rs, ag_ss, ag_rs, kv_sem, kv_ss, kv_rs,
):
    ctx = lax.axis_index("ctx")
    peers = lax.axis_size("ctx")
    rows, cols = x_ref.shape
    chunk = cols // IN_CHUNKS
    part_rows = rows // PARTS
    y, zh, up, down, across = ring_places()
    bf16 = jnp.bfloat16
    loads = [
        pltpu.make_async_copy(src, dst, in_sem.at[i])
        for i, (src, dst) in enumerate(
            (
                (x_hbm, x_ref),
                (wq_hbm, w_ref.at[:, 0:512]),
                (wk_hbm, w_ref.at[:, 512:640]),
                (wv_hbm, w_ref.at[:, 640:768]),
                (cos_hbm, cos_ref),
                (sin_hbm, sin_ref),
            )
        )
    ]
    for load in loads:
        load.start()
    barrier = pltpu.get_barrier_semaphore()
    for k in range(1, peers):
        pl.semaphore_signal(
            barrier, inc=1, device_id={"ctx": (ctx + k) % peers},
            device_id_type=pl.DeviceIdType.MESH,
        )
    for peer in (up, down, across):
        pl.semaphore_signal(
            barrier, inc=1, device_id={"head": peer}, device_id_type=pl.DeviceIdType.MESH
        )

    target = target_ref[...]
    owner = target // rows
    local = target - owner * rows
    owned = lax.broadcasted_iota(jnp.int32, (peers, rows), 0) == owner
    owned_f = jnp.where(owned, 1.0, 0.0).astype(jnp.float32)
    earlier = (
        lax.broadcasted_iota(jnp.int32, (rows, rows), 0)
        < lax.broadcasted_iota(jnp.int32, (rows, rows), 1)
    )
    before = jnp.dot(
        owned_f.astype(bf16),
        jnp.where(earlier, 1.0, 0.0).astype(bf16),
        preferred_element_type=jnp.float32,
    )
    rank = jnp.sum(owned_f * before, axis=0, keepdims=True)
    slot = owner * SLOTS + rank.astype(jnp.int32)
    for i in range(peers):
        at = lax.broadcasted_iota(jnp.int32, (SLOTS, rows), 0) + i * SLOTS
        pick[i * SLOTS : (i + 1) * SLOTS, :] = jnp.where(at == slot, 1.0, 0.0).astype(bf16)

    def meta_copy(k):
        to = (ctx + k) % peers
        return remote(meta_out.at[to], meta_in.at[k], meta_ss.at[k], meta_rs.at[k], ctx=to)

    def row_copy(f, k):
        to = (ctx + k) % peers
        return remote(
            send.at[f, pl.ds(pl.multiple_of(to * SLOTS, SLOTS), SLOTS)],
            recv.at[f, pl.ds(k * SLOTS, SLOTS)],
            row_ss.at[f, k], row_rs.at[f, k], ctx=to,
        )

    loads[0].wait()
    for f in range(IN_CHUNKS):
        send[f] = jnp.dot(
            pick[...], x_ref[:, f * chunk : (f + 1) * chunk], preferred_element_type=jnp.float32
        ).astype(bf16)
        if f == 0:
            pl.semaphore_wait(barrier, peers - 1 + 3)
        for k in range(1, peers):
            row_copy(f, k).start()
        recv[f, 0:SLOTS, :] = send[f, pl.ds(pl.multiple_of(ctx * SLOTS, SLOTS), SLOTS), :]
        if f == 0:
            line = lax.broadcasted_iota(jnp.int32, (8, rows), 0)
            high = local // 16
            facts = jnp.where(line == 0, high, jnp.where(line == 1, local - high * 16, 1))
            facts = lax.dot_general(
                facts.astype(jnp.float32).astype(bf16), pick[...], (((1,), (1,)), ((), ())),
                preferred_element_type=jnp.float32,
            )
            goes_to = jnp.where(facts[2:3] > 0.5, facts[0:1] * 16.0 + facts[1:2], -1.0)
            goes_to = jnp.broadcast_to(goes_to, (8, peers * SLOTS))
            for i in range(peers // 2):
                tile = goes_to[:, i * 128 : (i + 1) * 128]
                meta_out[2 * i] = tile
                meta_out[2 * i + 1] = pltpu.roll(tile, SLOTS, 1)
            for k in range(1, peers):
                meta_copy(k).start()
            meta_in[0] = meta_out[ctx]

    for k in range(1, peers):
        meta_copy(k).wait_recv()
    lane = lax.broadcasted_iota(jnp.int32, (8, 128), 1)
    for i in range(peers // 2):
        both = jnp.where(lane < SLOTS, meta_in[2 * i], pltpu.roll(meta_in[2 * i + 1], SLOTS, 1))
        both = both[0:1].astype(jnp.int32)
        at = lax.broadcasted_iota(jnp.int32, (rows, 128), 0)
        place[:, i * 128 : (i + 1) * 128] = jnp.where(at == both, 1.0, 0.0).astype(bf16)

    half = part_rows // 2

    def piece(dy, other):
        return ((y + dy) % 4) * 2 + ((1 - zh) if other else zh)

    def spread(n, e):
        part, f = divmod(n, IN_CHUNKS)
        src, lo, size, to = (
            (piece(0, 0), 0, part_rows, across),
            (piece(0, 0), 0, part_rows, up),
            (piece(0, 0), 0, part_rows, down),
            (piece(3, 0), 0, half, up),
            (piece(1, 0), half, half, down),
            (piece(0, 1), 0, part_rows, up),
            (piece(0, 1), 0, part_rows, down),
            (piece(2, 0), 0, part_rows, across),
        )[e]
        ref = pieces.at[src, part, f, pl.ds(lo, size)]
        return remote(ref, ref, ag_ss.at[n, e], ag_rs.at[n, e], head=to)

    def project(n, index, first=False):
        part, f = divmod(n, IN_CHUNKS)
        if f < IN_CHUNKS - 1:
            return
        piece_rows = jnp.concatenate(
            [pieces[index, part, g] for g in range(IN_CHUNKS)], axis=1
        )
        deep = pl.ds(pl.multiple_of(index * cols, cols), cols)
        term = jnp.dot(piece_rows, w_ref[deep, :], preferred_element_type=jnp.float32)
        acc[part] = term if first else acc[part] + term

    def begin(n):
        part, f = divmod(n, IN_CHUNKS)
        if part == 0:
            for k in range(1, peers):
                row_copy(f, k).wait_recv()
        here = slice(part * part_rows, (part + 1) * part_rows)
        pieces[piece(0, 0), part, f] = jnp.dot(
            place[here, :], recv[f], preferred_element_type=jnp.float32
        ).astype(bf16)
        for e in (1, 2, 0):
            spread(n, e).start()
        if n == IN_CHUNKS - 1:
            for load in loads[1:]:
                load.wait()
        project(n, piece(0, 0), first=True)

    def near(n):
        spread(n, 1).wait_recv()
        spread(n, 3).start()
        spread(n, 2).wait_recv()
        spread(n, 4).start()
        spread(n, 0).wait_recv()
        spread(n, 5).start()
        spread(n, 6).start()
        project(n, piece(3, 0))
        project(n, piece(1, 0))
        project(n, piece(0, 1))

    def far(n):
        spread(n, 3).wait_recv()
        spread(n, 4).wait_recv()
        spread(n, 7).start()
        project(n, piece(2, 0))

    def other(n):
        spread(n, 5).wait_recv()
        spread(n, 6).wait_recv()
        project(n, piece(3, 1))
        project(n, piece(1, 1))
        spread(n, 7).wait_recv()
        project(n, piece(2, 1))

    zl, x, core = ctx // 8, (ctx // 2) % 4, ctx % 2
    kv_half = part_rows // 2

    def block(dx, other_z, other_core=0):
        z = (1 - zl) if other_z else zl
        c = (1 - core) if other_core else core
        return z * 8 + ((x + dx) % 4) * 2 + c

    kv_pieces = ((0, 0), (0, 1), (3, 0), (1, 0), (2, 0), (3, 1), (1, 1), (2, 1))

    def share(part, e):
        right, left, over = block(1, 0), block(3, 0), block(0, 1)
        if e >= 8:
            src, lo, size, to = block(*kv_pieces[e - 8]), 0, part_rows, block(0, 0, 1)
        else:
            src, lo, size, to = (
                (block(0, 0), 0, part_rows, over),
                (block(0, 0), 0, part_rows, right),
                (block(0, 0), 0, part_rows, left),
                (block(3, 0), 0, kv_half, right),
                (block(1, 0), kv_half, kv_half, left),
                (block(0, 1), 0, part_rows, right),
                (block(0, 1), 0, part_rows, left),
                (block(2, 0), 0, part_rows, over),
            )[e]
        ref = kv_ref.at[
            pl.ds(pl.multiple_of(src * rows + part * part_rows + lo, 16), size)
        ]
        source = kv_own.at[part] if e in (0, 1, 2, 8) else ref
        return remote(source, ref, kv_ss.at[part, e], kv_rs.at[part, e], ctx=to)

    def keep(part):
        at = pl.ds(pl.multiple_of(ctx * rows + part * part_rows, 16), part_rows)
        return pltpu.make_async_copy(kv_own.at[part], kv_ref.at[at], kv_sem.at[part])

    def finish(part):
        here = slice(part * part_rows, (part + 1) * part_rows)
        cosine, sine = cos_ref[here, :], sin_ref[here, :]
        for h in (4, 5, 0, 1, 2, 3):
            tensor = acc[part, :, h * HD : (h + 1) * HD]
            if h < 5:
                tensor = tensor * cosine + pltpu.roll(tensor, HD // 2, 1) * sine
            tensor = tensor.astype(bf16)
            if h < 4:
                q_ref[here, h * HD : (h + 1) * HD] = tensor
            else:
                kv_own[part, :, (h - 4) * HD : (h - 3) * HD] = tensor
            if h == 5:
                for e in (1, 2, 0, 8):
                    share(part, e).start()
                keep(part).start()

    def share_near(part):
        share(part, 1).wait_recv()
        share(part, 3).start()
        share(part, 10).start()
        share(part, 2).wait_recv()
        share(part, 4).start()
        share(part, 11).start()
        share(part, 0).wait_recv()
        share(part, 5).start()
        share(part, 6).start()
        share(part, 9).start()

    def share_far(part):
        share(part, 3).wait_recv()
        share(part, 4).wait_recv()
        share(part, 7).start()
        share(part, 12).start()

    def share_other(part):
        share(part, 5).wait_recv()
        share(part, 13).start()
        share(part, 6).wait_recv()
        share(part, 14).start()
        share(part, 7).wait_recv()
        share(part, 15).start()

    count = IN_CHUNKS * PARTS
    begin(0)
    begin(1)
    for n in range(count + 2):
        if n < count:
            near(n)
        if n + 2 < count:
            begin(n + 2)
        if 1 <= n <= count:
            far(n - 1)
        if n >= 2:
            other(n - 2)
        if n == IN_CHUNKS + 1:
            finish(0)
        if n == IN_CHUNKS + 2:
            share_near(0)
        if n == IN_CHUNKS + 3:
            share_far(0)
    finish(1)
    share_other(0)
    share_near(1)
    share_far(1)
    share_other(1)
    for part in range(PARTS):
        for e in range(8, 16):
            share(part, e).wait_recv()

    for k in range(1, peers):
        meta_copy(k).wait_send()
        for f in range(IN_CHUNKS):
            row_copy(f, k).wait_send()
    for n in range(count):
        for e in range(8):
            spread(n, e).wait_send()
    for part in range(PARTS):
        keep(part).wait()
        for e in range(16):
            share(part, e).wait_send()


def gather_and_project(node_rows, node_target, cosine, sine, w_query, w_key, w_value):
    rows, cols = node_rows.shape
    peers = lax.axis_size("ctx")
    chunk = cols // IN_CHUNKS
    part_rows = rows // PARTS
    bf16 = jnp.bfloat16
    dma = pltpu.SemaphoreType.DMA
    vmem = pl.BlockSpec(memory_space=pltpu.VMEM)
    hbm = pl.BlockSpec(memory_space=pltpu.HBM)
    return pl.pallas_call(
        gather_kernel,
        out_shape=(
            jax.ShapeDtypeStruct((rows, 512), bf16),
            jax.ShapeDtypeStruct((rows * peers, 256), bf16),
        ),
        in_specs=[vmem] + [hbm] * 6,
        out_specs=(vmem, hbm),
        scratch_shapes=[
            pltpu.VMEM((rows, cols), bf16),
            pltpu.VMEM((rows, HD), jnp.float32),
            pltpu.VMEM((rows, HD), jnp.float32),
            pltpu.VMEM((w_query.shape[0], 768), bf16),
            pltpu.VMEM((peers * SLOTS, rows), bf16),
            pltpu.VMEM((rows, peers * SLOTS), bf16),
            pltpu.VMEM((IN_CHUNKS, peers * SLOTS, chunk), bf16),
            pltpu.VMEM((IN_CHUNKS, peers * SLOTS, chunk), bf16),
            pltpu.VMEM((peers, 8, 128), jnp.float32),
            pltpu.VMEM((peers, 8, 128), jnp.float32),
            pltpu.VMEM((8, PARTS, IN_CHUNKS, part_rows, chunk), bf16),
            pltpu.VMEM((PARTS, part_rows, 768), jnp.float32),
            pltpu.VMEM((PARTS, part_rows, 256), bf16),
            dma((6,)),
            dma((IN_CHUNKS, peers)),
            dma((IN_CHUNKS, peers)),
            dma((peers,)),
            dma((peers,)),
            dma((PARTS * IN_CHUNKS, 8)),
            dma((PARTS * IN_CHUNKS, 8)),
            dma((PARTS,)),
            dma((PARTS, 16)),
            dma((PARTS, 16)),
        ],
        compiler_params=pltpu.CompilerParams(
            collective_id=2, has_side_effects=True, vmem_limit_bytes=60 * MIB
        ),
        name="gather_and_project",
    )(node_target.reshape(1, rows), node_rows, cosine, sine, w_query, w_key, w_value)


def on_device(node_rows, node_target, node_position, block_mask, w_query, w_key, w_value, w_out):
    cosine, sine = rotary_tables(node_position, HD)
    queries, kv = gather_and_project(
        node_rows, node_target, cosine, sine, w_query, w_key, w_value
    )
    attended = attend(block_mask, queries, kv)
    return project_out(attended, w_out)


def solution(mesh):
    placed = (
        P("ctx", "head"),
        P("ctx"),
        P("ctx"),
        P("ctx", None),
        P(None, "head"),
        P(None, "head"),
        P(None, "head"),
        P("head", None),
    )
    return jax.shard_map(
        on_device, mesh=mesh, in_specs=placed, out_specs=P(("ctx", "head"), None), check_vma=False
    )
```

```python
import math

import jax
import jax.numpy as jnp
from jax import lax
from jax.experimental import pallas as pl
from jax.experimental.pallas import tpu as pltpu
from jax.sharding import PartitionSpec as P

HD = 128
BLOCK = 128
ROPE_THETA = 500000.0
NEG_LARGE = -1e30
MIB = 1024 * 1024


def rotary_tables(positions, head_size):
    half_size = head_size // 2
    inverse = jnp.exp(
        jnp.arange(half_size, dtype=jnp.float32) * (-2.0 * math.log(ROPE_THETA) / head_size)
    )
    angles = positions.astype(jnp.float32)[:, None] * inverse[None, :]
    cosine = jnp.cos(angles)
    sine = jnp.sin(angles)
    return jnp.concatenate([cosine, cosine], axis=-1), jnp.concatenate([-sine, sine], axis=-1)


def attend_kernel(mask_ref, q_ref, kv_hbm, out_ref, list_ref, kv_ref, own_ref, acc_ref, stat_ref, sem):
    ctx = lax.axis_index("ctx")
    rows = q_ref.shape[0]
    local_blocks = rows // BLOCK
    heads = q_ref.shape[1] // HD
    block_count = mask_ref.shape[1]
    width = heads * BLOCK
    scale = math.log2(math.e) / math.sqrt(HD)
    own = pl.ds(pl.multiple_of(ctx * rows, BLOCK), rows)
    own_load = pltpu.make_async_copy(kv_hbm.at[own], own_ref, sem.at[0])
    load = pltpu.make_async_copy(kv_hbm, kv_ref, sem.at[1])
    own_load.start()
    load.start()

    def build(kb, counts):
        for b in range(local_blocks):
            list_ref[b, counts[b]] = kb
        return tuple(n + mask_ref[b, kb] for b, n in enumerate(counts))

    counts = lax.fori_loop(
        0, block_count, build, (jnp.int32(0),) * local_blocks, unroll=8
    )

    def queries_of(b):
        at = slice(b * BLOCK, (b + 1) * BLOCK)
        return jnp.concatenate([q_ref[at, h * HD : (h + 1) * HD] for h in range(heads)], axis=0)

    def score(keys, b):
        return scale * lax.dot_general(
            keys, queries_of(b), (((1,), (1,)), ((), ())), preferred_element_type=jnp.float32
        )

    def mix(values, weights):
        return lax.dot_general(
            values, weights.astype(jnp.bfloat16), (((0,), (0,)), ((), ())),
            preferred_element_type=jnp.float32,
        )

    own_load.wait()
    key_at = lax.broadcasted_iota(jnp.int32, (BLOCK, width), 0)
    query_at = lax.broadcasted_iota(jnp.int32, (BLOCK, width), 1) % BLOCK
    for b in range(local_blocks):
        at = slice(b * BLOCK, (b + 1) * BLOCK)
        scores = jnp.where(key_at <= query_at, score(own_ref[at, 0:HD], b), NEG_LARGE)
        highest = jnp.max(scores, axis=0, keepdims=True)
        weights = jnp.exp2(scores - highest)
        stat_ref[b, 0:1] = highest
        stat_ref[b, 1:2] = jnp.sum(weights, axis=0, keepdims=True)
        acc_ref[b] = mix(own_ref[at, HD : 2 * HD], weights)
    load.wait()

    def add_two(b, i):
        places, drops = [], []
        for at in (2 * i, 2 * i + 1):
            real = at < counts[b]
            kb = jnp.where(real, list_ref[b, jnp.where(real, at, 0)], 0)
            places.append(pl.ds(pl.multiple_of(kb * BLOCK, BLOCK), BLOCK))
            drops.append(jnp.where(real, 0.0, NEG_LARGE).astype(jnp.float32))
        keys = jnp.concatenate([kv_ref[at, 0:HD] for at in places], axis=0)
        values = jnp.concatenate([kv_ref[at, HD : 2 * HD] for at in places], axis=0)
        scores = score(keys, b)
        scores = jnp.concatenate(
            [scores[:BLOCK] + drops[0], scores[BLOCK:] + drops[1]], axis=0
        )
        old = stat_ref[b, 0:1]
        highest = jnp.maximum(old, jnp.max(scores, axis=0, keepdims=True))
        factor = jnp.exp2(old - highest)
        weights = jnp.exp2(scores - highest)
        stat_ref[b, 0:1] = highest
        stat_ref[b, 1:2] = stat_ref[b, 1:2] * factor + jnp.sum(weights, axis=0, keepdims=True)
        acc_ref[b] = acc_ref[b] * factor + mix(values, weights)

    for b in range(0, local_blocks, 2):

        def step(i, carry, b=b):
            add_two(b, i)
            add_two(b + 1, i)
            return carry

        lax.fori_loop(0, (jnp.maximum(counts[b], counts[b + 1]) + 1) // 2, step, 0)
    for b in range(local_blocks):
        attended = acc_ref[b] / stat_ref[b, 1:2]
        for h in range(heads):
            out_ref[b * BLOCK : (b + 1) * BLOCK, h * HD : (h + 1) * HD] = attended[
                :, h * BLOCK : (h + 1) * BLOCK
            ].T.astype(jnp.bfloat16)


def attend(block_mask, queries, kv):
    rows, width = queries.shape
    blocks = rows // BLOCK
    return pl.pallas_call(
        attend_kernel,
        out_shape=jax.ShapeDtypeStruct(queries.shape, jnp.bfloat16),
        in_specs=[
            pl.BlockSpec(memory_space=pltpu.SMEM),
            pl.BlockSpec(memory_space=pltpu.VMEM),
            pl.BlockSpec(memory_space=pltpu.HBM),
        ],
        out_specs=pl.BlockSpec(memory_space=pltpu.VMEM),
        scratch_shapes=[
            pltpu.SMEM((blocks, 128), jnp.int32),
            pltpu.VMEM(kv.shape, jnp.bfloat16),
            pltpu.VMEM((rows, kv.shape[1]), jnp.bfloat16),
            pltpu.VMEM((blocks, HD, width), jnp.float32),
            pltpu.VMEM((blocks, 8, width), jnp.float32),
            pltpu.SemaphoreType.DMA((2,)),
        ],
        compiler_params=pltpu.CompilerParams(vmem_limit_bytes=60 * MIB),
        name="attend",
    )(block_mask, queries, kv)


def ring_places():
    head = lax.axis_index("head")
    y, zh = head // 2, head % 2
    up = ((y + 1) % 4) * 2 + zh
    down = ((y + 3) % 4) * 2 + zh
    across = y * 2 + (1 - zh)
    return y, zh, up, down, across


def remote(src, dst, send_sem, recv_sem, **place):
    return pltpu.make_async_remote_copy(
        src_ref=src,
        dst_ref=dst,
        send_sem=send_sem,
        recv_sem=recv_sem,
        device_id=place,
        device_id_type=pl.DeviceIdType.MESH,
    )


OUT_CHUNKS = 8


def project_out_kernel(
    att_ref, w_hbm, out_ref, w_ref, part, far_out, far_in, near_out, near_in, other_out, other_in,
    z_out, z_in, w_sem, far_ss, far_rs, near_ss, near_rs, other_ss, other_rs, z_ss, z_rs,
):
    y, zh, up, down, across = ring_places()
    cw = part.shape[2]
    half = cw // 2
    seat = part.shape[1] // 8
    loads = [
        pltpu.make_async_copy(w_hbm.at[:, pl.ds(c * cw, cw)], w_ref.at[c], w_sem.at[c])
        for c in range(OUT_CHUNKS)
    ]
    loads[0].start()
    barrier = pltpu.get_barrier_semaphore()
    for peer in (up, down, across):
        pl.semaphore_signal(
            barrier, inc=1, device_id={"head": peer}, device_id_type=pl.DeviceIdType.MESH
        )

    def rows_of(c, dy, other, lo=0, size=None):
        index = ((y + dy) % 4) * 2 + ((1 - zh) if other else zh)
        return part[
            c, pl.ds(pl.multiple_of(index * seat, seat), seat), lo : lo + (size or cw)
        ]

    def far(c, side):
        return remote(
            far_out.at[c, side], far_in.at[c, side], far_ss.at[c, side], far_rs.at[c, side],
            head=(up, down)[side],
        )

    def near(c, side, at):
        return remote(
            near_out.at[c, side, at], near_in.at[c, side, at],
            near_ss.at[c, side, at], near_rs.at[c, side, at],
            head=(up, down)[side],
        )

    def other(c, side):
        return remote(
            other_out.at[c, side], other_in.at[c, side], other_ss.at[c, side],
            other_rs.at[c, side], head=(up, down)[side],
        )

    def cross(c, which):
        return remote(
            z_out.at[c, which], z_in.at[c, which], z_ss.at[c, which], z_rs.at[c, which],
            head=across,
        )

    f32, bf16 = jnp.float32, jnp.bfloat16

    def first(c):
        loads[c].wait()
        if c == 0:
            for load in loads[1:]:
                load.start()
        part[c] = jnp.dot(att_ref[...], w_ref[c], preferred_element_type=f32)
        if c == 0:
            pl.semaphore_wait(barrier, 3)
        z_out[c, 0] = rows_of(c, 2, True).astype(bf16)
        cross(c, 0).start()
        for side, dy in ((0, 1), (1, 3)):
            other_out[c, side] = rows_of(c, dy, True).astype(bf16)
            other(c, side).start()
        near_out[c, 0, 1] = rows_of(c, 1, False, half, half).astype(bf16)
        near(c, 0, 1).start()
        near_out[c, 1, 0] = rows_of(c, 3, False, 0, half).astype(bf16)
        near(c, 1, 0).start()

    def second(c):
        cross(c, 0).wait_recv()
        for side in range(2):
            far_out[c, side] = (
                rows_of(c, 2, False, side * half, half)
                + z_in[c, 0, :, side * half : (side + 1) * half].astype(f32)
            ).astype(bf16)
            far(c, side).start()

    def third(c):
        for side, dy in ((0, 1), (1, 3)):
            far(c, side).wait_recv()
            near_out[c, side, side] = (
                rows_of(c, dy, False, side * half, half) + far_in[c, side].astype(f32)
            ).astype(bf16)
            near(c, side, side).start()

    def fourth(c):
        other(c, 0).wait_recv()
        other(c, 1).wait_recv()
        z_out[c, 1] = (
            rows_of(c, 0, True) + other_in[c, 0].astype(f32) + other_in[c, 1].astype(f32)
        ).astype(bf16)
        cross(c, 1).start()

    def fifth(c):
        for side in range(2):
            for at in range(2):
                near(c, side, at).wait_recv()
        cross(c, 1).wait_recv()
        for at in range(2):
            here = slice(at * half, (at + 1) * half)
            out_ref[:, c * cw + at * half : c * cw + (at + 1) * half] = (
                rows_of(c, 0, False, at * half, half)
                + near_in[c, 0, at].astype(f32)
                + near_in[c, 1, at].astype(f32)
                + z_in[c, 1, :, here].astype(f32)
            ).astype(bf16)

    first(0)
    first(1)
    for n in range(OUT_CHUNKS + 3):
        if n < OUT_CHUNKS:
            second(n)
        if n + 2 < OUT_CHUNKS:
            first(n + 2)
        if 1 <= n <= OUT_CHUNKS:
            third(n - 1)
            fourth(n - 1)
        if n >= 3:
            fifth(n - 3)
    for c in range(OUT_CHUNKS):
        for side in range(2):
            far(c, side).wait_send()
            other(c, side).wait_send()
            cross(c, side).wait_send()
            for at in range(2):
                near(c, side, at).wait_send()


def project_out(attended, w_out):
    rows, depth = attended.shape
    width = w_out.shape[1]
    n, cw = OUT_CHUNKS, width // OUT_CHUNKS
    half = cw // 2
    seat = rows // 8
    bf16 = jnp.bfloat16
    dma = pltpu.SemaphoreType.DMA
    return pl.pallas_call(
        project_out_kernel,
        out_shape=jax.ShapeDtypeStruct((seat, width), bf16),
        in_specs=[
            pl.BlockSpec(memory_space=pltpu.VMEM),
            pl.BlockSpec(memory_space=pltpu.HBM),
        ],
        out_specs=pl.BlockSpec(memory_space=pltpu.VMEM),
        scratch_shapes=[
            pltpu.VMEM((n, depth, cw), bf16),
            pltpu.VMEM((n, rows, cw), jnp.float32),
            pltpu.VMEM((n, 2, seat, half), bf16),
            pltpu.VMEM((n, 2, seat, half), bf16),
            pltpu.VMEM((n, 2, 2, seat, half), bf16),
            pltpu.VMEM((n, 2, 2, seat, half), bf16),
            pltpu.VMEM((n, 2, seat, cw), bf16),
            pltpu.VMEM((n, 2, seat, cw), bf16),
            pltpu.VMEM((n, 2, seat, cw), bf16),
            pltpu.VMEM((n, 2, seat, cw), bf16),
            dma((n,)),
            dma((n, 2)),
            dma((n, 2)),
            dma((n, 2, 2)),
            dma((n, 2, 2)),
            dma((n, 2)),
            dma((n, 2)),
            dma((n, 2)),
            dma((n, 2)),
        ],
        compiler_params=pltpu.CompilerParams(
            collective_id=1, has_side_effects=True, vmem_limit_bytes=56 * MIB
        ),
        name="project_out",
    )(attended, w_out)


IN_CHUNKS = 2
PART_ROWS = (256, 256)
PART_CHUNKS = (2, 1)
SLOTS = 64
AHEAD = 3
QUERIES_LATER = 0
STEPS = [(p, f) for p, n in enumerate(PART_CHUNKS) for f in range(n)]
PARTS = len(PART_ROWS)


def gather_kernel(
    target_ref, x_hbm, cos_hbm, sin_hbm, wq_hbm, wk_hbm, wv_hbm, q_ref, kv_ref,
    x_ref, cos_ref, sin_ref, w_ref, pick, place, send, recv, meta_out, meta_in, in_sem, row_ss,
    row_rs, meta_ss, meta_rs, ag_ss, ag_rs, kv_sem, kv_ss, kv_rs, *per_part,
):
    ctx = lax.axis_index("ctx")
    peers = lax.axis_size("ctx")
    rows, cols = x_ref.shape
    chunk = cols // IN_CHUNKS
    pieces, acc, kv_own = (per_part[i * PARTS : (i + 1) * PARTS] for i in range(3))
    starts = [sum(PART_ROWS[:p]) for p in range(PARTS)]
    y, zh, up, down, across = ring_places()
    bf16 = jnp.bfloat16
    loads = [
        pltpu.make_async_copy(src, dst, in_sem.at[i])
        for i, (src, dst) in enumerate(
            (
                (x_hbm, x_ref),
                (wq_hbm, w_ref.at[:, 0:512]),
                (wk_hbm, w_ref.at[:, 512:640]),
                (wv_hbm, w_ref.at[:, 640:768]),
                (cos_hbm, cos_ref),
                (sin_hbm, sin_ref),
            )
        )
    ]
    loads[0].start()
    barrier = pltpu.get_barrier_semaphore()
    for k in range(1, peers):
        pl.semaphore_signal(
            barrier, inc=1, device_id={"ctx": (ctx + k) % peers},
            device_id_type=pl.DeviceIdType.MESH,
        )
    for peer in (up, down, across):
        pl.semaphore_signal(
            barrier, inc=1, device_id={"head": peer}, device_id_type=pl.DeviceIdType.MESH
        )

    target = target_ref[...]
    owner = target // rows
    local = target - owner * rows
    owned = lax.broadcasted_iota(jnp.int32, (peers, rows), 0) == owner
    owned_f = jnp.where(owned, 1.0, 0.0).astype(jnp.float32)
    earlier = (
        lax.broadcasted_iota(jnp.int32, (rows, rows), 0)
        < lax.broadcasted_iota(jnp.int32, (rows, rows), 1)
    )
    before = jnp.dot(
        owned_f.astype(bf16),
        jnp.where(earlier, 1.0, 0.0).astype(bf16),
        preferred_element_type=jnp.float32,
    )
    rank = jnp.sum(owned_f * before, axis=0, keepdims=True)
    slot = owner * SLOTS + rank.astype(jnp.int32)
    for i in range(peers):
        at = lax.broadcasted_iota(jnp.int32, (SLOTS, rows), 0) + i * SLOTS
        pick[i * SLOTS : (i + 1) * SLOTS, :] = jnp.where(at == slot, 1.0, 0.0).astype(bf16)

    def meta_copy(k):
        to = (ctx + k) % peers
        return remote(meta_out.at[to], meta_in.at[k], meta_ss.at[k], meta_rs.at[k], ctx=to)

    def row_copy(f, k):
        to = (ctx + k) % peers
        return remote(
            send.at[f, pl.ds(pl.multiple_of(to * SLOTS, SLOTS), SLOTS)],
            recv.at[f, pl.ds(k * SLOTS, SLOTS)],
            row_ss.at[f, k], row_rs.at[f, k], ctx=to,
        )

    line = lax.broadcasted_iota(jnp.int32, (8, rows), 0)
    high = local // 16
    facts = jnp.where(line == 0, high, jnp.where(line == 1, local - high * 16, 1))
    facts = lax.dot_general(
        facts.astype(jnp.float32).astype(bf16), pick[...], (((1,), (1,)), ((), ())),
        preferred_element_type=jnp.float32,
    )
    goes_to = jnp.where(facts[2:3] > 0.5, facts[0:1] * 16.0 + facts[1:2], -1.0)
    goes_to = jnp.broadcast_to(goes_to, (8, peers * SLOTS))
    for i in range(peers // 2):
        tile = goes_to[:, i * 128 : (i + 1) * 128]
        meta_out[2 * i] = tile
        meta_out[2 * i + 1] = pltpu.roll(tile, SLOTS, 1)
    pl.semaphore_wait(barrier, peers - 1 + 3)
    for k in range(1, peers):
        meta_copy(k).start()
    meta_in[0] = meta_out[ctx]

    loads[0].wait()
    for load in loads[1:]:
        load.start()
    for f in range(IN_CHUNKS):
        send[f] = jnp.dot(
            pick[...], x_ref[:, f * chunk : (f + 1) * chunk], preferred_element_type=jnp.float32
        ).astype(bf16)
        for k in range(1, peers):
            row_copy(f, k).start()
        recv[f, 0:SLOTS, :] = send[f, pl.ds(pl.multiple_of(ctx * SLOTS, SLOTS), SLOTS), :]

    for k in range(1, peers):
        meta_copy(k).wait_recv()
    lane = lax.broadcasted_iota(jnp.int32, (8, 128), 1)
    for i in range(peers // 2):
        both = jnp.where(lane < SLOTS, meta_in[2 * i], pltpu.roll(meta_in[2 * i + 1], SLOTS, 1))
        both = both[0:1].astype(jnp.int32)
        at = lax.broadcasted_iota(jnp.int32, (rows, 128), 0)
        place[:, i * 128 : (i + 1) * 128] = jnp.where(at == both, 1.0, 0.0).astype(bf16)

    def piece(dy, other):
        return ((y + dy) % 4) * 2 + ((1 - zh) if other else zh)

    def spread(n, e):
        part, f = STEPS[n]
        size, half = PART_ROWS[part], PART_ROWS[part] // 2
        src, lo, size, to = (
            (piece(0, 0), 0, size, across),
            (piece(0, 0), 0, size, up),
            (piece(0, 0), 0, size, down),
            (piece(3, 0), 0, half, up),
            (piece(1, 0), half, half, down),
            (piece(0, 1), 0, size, up),
            (piece(0, 1), 0, size, down),
            (piece(2, 0), 0, size, across),
        )[e]
        ref = pieces[part].at[src, f, pl.ds(lo, size)]
        return remote(ref, ref, ag_ss.at[n, e], ag_rs.at[n, e], head=to)

    def product(part, index, columns):
        piece_rows = jnp.concatenate(
            [pieces[part][index, g] for g in range(PART_CHUNKS[part])], axis=1
        )
        deep = index * cols
        deep = pl.ds(deep if isinstance(deep, int) else pl.multiple_of(deep, cols), cols)
        return jnp.dot(piece_rows, w_ref[deep, columns], preferred_element_type=jnp.float32)

    def project(n, index, first=False):
        part, f = STEPS[n]
        if f < PART_CHUNKS[part] - 1:
            return
        term = product(part, index, slice(512, 768))
        acc[part][...] = term if first else acc[part][...] + term

    def begin(n):
        part, f = STEPS[n]
        if part == 0:
            for k in range(1, peers):
                row_copy(f, k).wait_recv()
        here = slice(starts[part], starts[part] + PART_ROWS[part])
        wide = IN_CHUNKS // PART_CHUNKS[part]
        for g in range(wide):
            pieces[part][piece(0, 0), f, :, g * chunk : (g + 1) * chunk] = jnp.dot(
                place[here, :], recv[f * wide + g], preferred_element_type=jnp.float32
            ).astype(bf16)
        for e in (1, 2, 0):
            spread(n, e).start()
        if n == IN_CHUNKS - 1:
            for load in loads[1:]:
                load.wait()
        project(n, piece(0, 0), first=True)

    def near(n):
        spread(n, 1).wait_recv()
        spread(n, 3).start()
        spread(n, 2).wait_recv()
        spread(n, 4).start()
        spread(n, 0).wait_recv()
        spread(n, 5).start()
        spread(n, 6).start()
        project(n, piece(3, 0))
        project(n, piece(1, 0))
        project(n, piece(0, 1))

    def far(n):
        spread(n, 3).wait_recv()
        spread(n, 4).wait_recv()
        spread(n, 7).start()
        project(n, piece(2, 0))

    def other(n):
        spread(n, 5).wait_recv()
        spread(n, 6).wait_recv()
        project(n, piece(3, 1))
        project(n, piece(1, 1))
        spread(n, 7).wait_recv()
        project(n, piece(2, 1))

    zl, x, core = ctx // 8, (ctx // 2) % 4, ctx % 2

    def block(dx, other_z, other_core=0):
        z = (1 - zl) if other_z else zl
        c = (1 - core) if other_core else core
        return z * 8 + ((x + dx) % 4) * 2 + c

    kv_pieces = ((0, 0), (0, 1), (3, 0), (1, 0), (2, 0), (3, 1), (1, 1), (2, 1))

    def share(part, e):
        right, left, over = block(1, 0), block(3, 0), block(0, 1)
        part_rows, kv_half = PART_ROWS[part], PART_ROWS[part] // 2
        if e >= 8:
            src, lo, size, to = block(*kv_pieces[e - 8]), 0, part_rows, block(0, 0, 1)
        else:
            src, lo, size, to = (
                (block(0, 0), 0, part_rows, over),
                (block(0, 0), 0, part_rows, right),
                (block(0, 0), 0, part_rows, left),
                (block(3, 0), 0, kv_half, right),
                (block(1, 0), kv_half, kv_half, left),
                (block(0, 1), 0, part_rows, right),
                (block(0, 1), 0, part_rows, left),
                (block(2, 0), 0, part_rows, over),
            )[e]
        ref = kv_ref.at[
            pl.ds(pl.multiple_of(src * rows + starts[part] + lo, 16), size)
        ]
        source = kv_own[part] if e in (0, 1, 2, 8) else ref
        return remote(source, ref, kv_ss.at[part, e], kv_rs.at[part, e], ctx=to)

    def keep(part):
        at = pl.ds(pl.multiple_of(ctx * rows + starts[part], 16), PART_ROWS[part])
        return pltpu.make_async_copy(kv_own[part], kv_ref.at[at], kv_sem.at[part])

    def turn(tensor, here):
        return tensor * cos_ref[here, :] + pltpu.roll(tensor, HD // 2, 1) * sin_ref[here, :]

    def finish(part):
        here = slice(starts[part], starts[part] + PART_ROWS[part])
        kv_own[part][:, 0:HD] = turn(acc[part][:, 0:HD], here).astype(bf16)
        kv_own[part][:, HD : 2 * HD] = acc[part][:, HD : 2 * HD].astype(bf16)
        for e in (1, 2, 0, 8):
            share(part, e).start()
        keep(part).start()

    def finish_queries(part):
        here = slice(starts[part], starts[part] + PART_ROWS[part])
        query = product(part, 0, slice(0, 512))
        for index in range(1, 8):
            query = query + product(part, index, slice(0, 512))
        for h in range(4):
            at = slice(h * HD, (h + 1) * HD)
            q_ref[here, at] = turn(query[:, at], here).astype(bf16)

    def share_near(part):
        share(part, 1).wait_recv()
        share(part, 3).start()
        share(part, 10).start()
        share(part, 2).wait_recv()
        share(part, 4).start()
        share(part, 11).start()
        share(part, 0).wait_recv()
        share(part, 5).start()
        share(part, 6).start()
        share(part, 9).start()

    def share_far(part):
        share(part, 3).wait_recv()
        share(part, 4).wait_recv()
        share(part, 7).start()
        share(part, 12).start()

    def share_other(part):
        share(part, 5).wait_recv()
        share(part, 13).start()
        share(part, 6).wait_recv()
        share(part, 14).start()
        share(part, 7).wait_recv()
        share(part, 15).start()

    count = len(STEPS)
    due = {}
    for part in range(PARTS):
        last = sum(PART_CHUNKS[: part + 1]) + 1
        for later, rank_in, act in (
            (0, 0, finish), (1, 1, share_near), (2, 1, share_far), (3, 1, share_other),
            (QUERIES_LATER, 2, finish_queries),
        ):
            due.setdefault(last + later, []).append((rank_in, part, act))
    begin(0)
    begin(1)
    begun = 2
    for n in range(max(due) + 1):
        if n < count:
            near(n)
        while begun < min(count, n + (3 if n + 3 <= IN_CHUNKS - 1 or n < 1 else AHEAD + 1)):
            begin(begun)
            begun += 1
        if 1 <= n <= count:
            far(n - 1)
        if 2 <= n <= count + 1:
            other(n - 2)
        for rank_in, part, act in sorted(due.get(n, []), key=lambda item: item[:2]):
            act(part)
    for part in range(PARTS):
        for e in range(8, 16):
            share(part, e).wait_recv()

    for k in range(1, peers):
        meta_copy(k).wait_send()
        for f in range(IN_CHUNKS):
            row_copy(f, k).wait_send()
    for n in range(count):
        for e in range(8):
            spread(n, e).wait_send()
    for part in range(PARTS):
        keep(part).wait()
        for e in range(16):
            share(part, e).wait_send()


def gather_and_project(node_rows, node_target, cosine, sine, w_query, w_key, w_value):
    rows, cols = node_rows.shape
    peers = lax.axis_size("ctx")
    chunk = cols // IN_CHUNKS
    bf16 = jnp.bfloat16
    dma = pltpu.SemaphoreType.DMA
    vmem = pl.BlockSpec(memory_space=pltpu.VMEM)
    hbm = pl.BlockSpec(memory_space=pltpu.HBM)
    return pl.pallas_call(
        gather_kernel,
        out_shape=(
            jax.ShapeDtypeStruct((rows, 512), bf16),
            jax.ShapeDtypeStruct((rows * peers, 256), bf16),
        ),
        in_specs=[vmem] + [hbm] * 6,
        out_specs=(vmem, hbm),
        scratch_shapes=[
            pltpu.VMEM((rows, cols), bf16),
            pltpu.VMEM((rows, HD), jnp.float32),
            pltpu.VMEM((rows, HD), jnp.float32),
            pltpu.VMEM((w_query.shape[0], 768), bf16),
            pltpu.VMEM((peers * SLOTS, rows), bf16),
            pltpu.VMEM((rows, peers * SLOTS), bf16),
            pltpu.VMEM((IN_CHUNKS, peers * SLOTS, chunk), bf16),
            pltpu.VMEM((IN_CHUNKS, peers * SLOTS, chunk), bf16),
            pltpu.VMEM((peers, 8, 128), jnp.float32),
            pltpu.VMEM((peers, 8, 128), jnp.float32),
            dma((6,)),
            dma((IN_CHUNKS, peers)),
            dma((IN_CHUNKS, peers)),
            dma((peers,)),
            dma((peers,)),
            dma((len(STEPS), 8)),
            dma((len(STEPS), 8)),
            dma((PARTS,)),
            dma((PARTS, 16)),
            dma((PARTS, 16)),
        ]
        + [pltpu.VMEM((8, n, r, cols // n), bf16) for r, n in zip(PART_ROWS, PART_CHUNKS)]
        + [pltpu.VMEM((r, 256), jnp.float32) for r in PART_ROWS]
        + [pltpu.VMEM((r, 256), bf16) for r in PART_ROWS],
        compiler_params=pltpu.CompilerParams(
            collective_id=2, has_side_effects=True, vmem_limit_bytes=60 * MIB
        ),
        name="gather_and_project",
    )(node_target.reshape(1, rows), node_rows, cosine, sine, w_query, w_key, w_value)


def on_device(node_rows, node_target, node_position, block_mask, w_query, w_key, w_value, w_out):
    cosine, sine = rotary_tables(node_position, HD)
    queries, kv = gather_and_project(
        node_rows, node_target, cosine, sine, w_query, w_key, w_value
    )
    attended = attend(block_mask, queries, kv)
    return project_out(attended, w_out)


def solution(mesh):
    placed = (
        P("ctx", "head"),
        P("ctx"),
        P("ctx"),
        P("ctx", None),
        P(None, "head"),
        P(None, "head"),
        P(None, "head"),
        P("head", None),
    )
    return jax.shard_map(
        on_device, mesh=mesh, in_specs=placed, out_specs=P(("ctx", "head"), None), check_vma=False
    )
```

```python
import math

import jax
import jax.numpy as jnp
import numpy as np
from jax import lax
from jax.experimental import pallas as pl
from jax.experimental.pallas import tpu as pltpu
from jax.sharding import PartitionSpec as P

HD = 128
BLOCK = 128
ROPE_THETA = 500000.0
NEG_LARGE = -1e30
MIB = 1024 * 1024


def attend_kernel(mask_ref, q_ref, kv_hbm, out_ref, list_ref, kv_ref, own_ref, acc_ref, stat_ref, sem):
    ctx = lax.axis_index("ctx")
    rows = q_ref.shape[0]
    local_blocks = rows // BLOCK
    heads = q_ref.shape[1] // HD
    block_count = mask_ref.shape[1]
    width = heads * BLOCK
    scale = math.log2(math.e) / math.sqrt(HD)
    own = pl.ds(pl.multiple_of(ctx * rows, BLOCK), rows)
    own_load = pltpu.make_async_copy(kv_hbm.at[own], own_ref, sem.at[0])
    load = pltpu.make_async_copy(kv_hbm, kv_ref, sem.at[1])
    own_load.start()
    load.start()

    def build(kb, counts):
        for b in range(local_blocks):
            list_ref[b, counts[b]] = kb
        return tuple(n + mask_ref[b, kb] for b, n in enumerate(counts))

    counts = lax.fori_loop(
        0, block_count, build, (jnp.int32(0),) * local_blocks, unroll=8
    )

    def queries_of(b):
        at = slice(b * BLOCK, (b + 1) * BLOCK)
        return jnp.concatenate([q_ref[at, h * HD : (h + 1) * HD] for h in range(heads)], axis=0)

    def score(keys, b):
        return scale * lax.dot_general(
            keys, queries_of(b), (((1,), (1,)), ((), ())), preferred_element_type=jnp.float32
        )

    def mix(values, weights):
        return lax.dot_general(
            values, weights.astype(jnp.bfloat16), (((0,), (0,)), ((), ())),
            preferred_element_type=jnp.float32,
        )

    own_load.wait()
    key_at = lax.broadcasted_iota(jnp.int32, (BLOCK, width), 0)
    query_at = lax.broadcasted_iota(jnp.int32, (BLOCK, width), 1) % BLOCK
    for b in range(local_blocks):
        at = slice(b * BLOCK, (b + 1) * BLOCK)
        scores = jnp.where(key_at <= query_at, score(own_ref[at, 0:HD], b), NEG_LARGE)
        highest = jnp.max(scores, axis=0, keepdims=True)
        weights = jnp.exp2(scores - highest)
        stat_ref[b, 0:1] = highest
        stat_ref[b, 1:2] = jnp.sum(weights, axis=0, keepdims=True)
        acc_ref[b] = mix(own_ref[at, HD : 2 * HD], weights)
    load.wait()

    def add_two(b, i):
        places, drops = [], []
        for at in (2 * i, 2 * i + 1):
            real = at < counts[b]
            kb = jnp.where(real, list_ref[b, jnp.where(real, at, 0)], 0)
            places.append(pl.ds(pl.multiple_of(kb * BLOCK, BLOCK), BLOCK))
            drops.append(jnp.where(real, 0.0, NEG_LARGE).astype(jnp.float32))
        keys = jnp.concatenate([kv_ref[at, 0:HD] for at in places], axis=0)
        values = jnp.concatenate([kv_ref[at, HD : 2 * HD] for at in places], axis=0)
        scores = score(keys, b)
        scores = jnp.concatenate(
            [scores[:BLOCK] + drops[0], scores[BLOCK:] + drops[1]], axis=0
        )
        old = stat_ref[b, 0:1]
        highest = jnp.maximum(old, jnp.max(scores, axis=0, keepdims=True))
        factor = jnp.exp2(old - highest)
        weights = jnp.exp2(scores - highest)
        stat_ref[b, 0:1] = highest
        stat_ref[b, 1:2] = stat_ref[b, 1:2] * factor + jnp.sum(weights, axis=0, keepdims=True)
        acc_ref[b] = acc_ref[b] * factor + mix(values, weights)

    for b in range(0, local_blocks, 2):

        def step(i, carry, b=b):
            add_two(b, i)
            add_two(b + 1, i)
            return carry

        lax.fori_loop(0, (jnp.maximum(counts[b], counts[b + 1]) + 1) // 2, step, 0)
    for b in range(local_blocks):
        attended = (acc_ref[b] * (1.0 / stat_ref[b, 1:2])).astype(jnp.bfloat16)
        for h in range(heads):
            out_ref[b * BLOCK : (b + 1) * BLOCK, h * HD : (h + 1) * HD] = attended[
                :, h * BLOCK : (h + 1) * BLOCK
            ].T


def attend(block_mask, queries, kv):
    rows, width = queries.shape
    blocks = rows // BLOCK
    return pl.pallas_call(
        attend_kernel,
        out_shape=jax.ShapeDtypeStruct(queries.shape, jnp.bfloat16),
        in_specs=[
            pl.BlockSpec(memory_space=pltpu.SMEM),
            pl.BlockSpec(memory_space=pltpu.VMEM),
            pl.BlockSpec(memory_space=pltpu.HBM),
        ],
        out_specs=pl.BlockSpec(memory_space=pltpu.VMEM),
        scratch_shapes=[
            pltpu.SMEM((blocks, 128), jnp.int32),
            pltpu.VMEM(kv.shape, jnp.bfloat16),
            pltpu.VMEM((rows, kv.shape[1]), jnp.bfloat16),
            pltpu.VMEM((blocks, HD, width), jnp.float32),
            pltpu.VMEM((blocks, 8, width), jnp.float32),
            pltpu.SemaphoreType.DMA((2,)),
        ],
        compiler_params=pltpu.CompilerParams(vmem_limit_bytes=60 * MIB),
        name="attend",
    )(block_mask, queries, kv)


def ring_places():
    head = lax.axis_index("head")
    y, zh = head // 2, head % 2
    up = ((y + 1) % 4) * 2 + zh
    down = ((y + 3) % 4) * 2 + zh
    across = y * 2 + (1 - zh)
    return y, zh, up, down, across


def remote(src, dst, send_sem, recv_sem, **place):
    return pltpu.make_async_remote_copy(
        src_ref=src,
        dst_ref=dst,
        send_sem=send_sem,
        recv_sem=recv_sem,
        device_id=place,
        device_id_type=pl.DeviceIdType.MESH,
    )


OUT_CHUNKS = 8


def project_out_kernel(
    att_ref, w_hbm, out_ref, w_ref, part, far_out, far_in, near_out, near_in, other_out, other_in,
    z_out, z_in, w_sem, far_ss, far_rs, near_ss, near_rs, other_ss, other_rs, z_ss, z_rs,
):
    y, zh, up, down, across = ring_places()
    cw = part.shape[2]
    half = cw // 2
    seat = part.shape[1] // 8
    loads = [
        pltpu.make_async_copy(w_hbm.at[:, pl.ds(c * cw, cw)], w_ref.at[c], w_sem.at[c])
        for c in range(OUT_CHUNKS)
    ]
    loads[0].start()
    barrier = pltpu.get_barrier_semaphore()
    for peer in (up, down, across):
        pl.semaphore_signal(
            barrier, inc=1, device_id={"head": peer}, device_id_type=pl.DeviceIdType.MESH
        )

    def rows_of(c, dy, other, lo=0, size=None):
        index = ((y + dy) % 4) * 2 + ((1 - zh) if other else zh)
        return part[
            c, pl.ds(pl.multiple_of(index * seat, seat), seat), lo : lo + (size or cw)
        ]

    def far(c, side):
        return remote(
            far_out.at[c, side], far_in.at[c, side], far_ss.at[c, side], far_rs.at[c, side],
            head=(up, down)[side],
        )

    def near(c, side, at):
        return remote(
            near_out.at[c, side, at], near_in.at[c, side, at],
            near_ss.at[c, side, at], near_rs.at[c, side, at],
            head=(up, down)[side],
        )

    def other(c, side):
        return remote(
            other_out.at[c, side], other_in.at[c, side], other_ss.at[c, side],
            other_rs.at[c, side], head=(up, down)[side],
        )

    def cross(c, which):
        return remote(
            z_out.at[c, which], z_in.at[c, which], z_ss.at[c, which], z_rs.at[c, which],
            head=across,
        )

    f32, bf16 = jnp.float32, jnp.bfloat16

    def first(c):
        loads[c].wait()
        if c == 0:
            for load in loads[1:]:
                load.start()
        part[c] = jnp.dot(att_ref[...], w_ref[c], preferred_element_type=f32)
        if c == 0:
            pl.semaphore_wait(barrier, 3)
        z_out[c, 0] = rows_of(c, 2, True).astype(bf16)
        cross(c, 0).start()
        for side, dy in ((0, 1), (1, 3)):
            other_out[c, side] = rows_of(c, dy, True).astype(bf16)
            other(c, side).start()
        near_out[c, 0, 1] = rows_of(c, 1, False, half, half).astype(bf16)
        near(c, 0, 1).start()
        near_out[c, 1, 0] = rows_of(c, 3, False, 0, half).astype(bf16)
        near(c, 1, 0).start()

    def second(c):
        cross(c, 0).wait_recv()
        for side in range(2):
            far_out[c, side] = (
                rows_of(c, 2, False, side * half, half)
                + z_in[c, 0, :, side * half : (side + 1) * half].astype(f32)
            ).astype(bf16)
            far(c, side).start()

    def third(c):
        for side, dy in ((0, 1), (1, 3)):
            far(c, side).wait_recv()
            near_out[c, side, side] = (
                rows_of(c, dy, False, side * half, half) + far_in[c, side].astype(f32)
            ).astype(bf16)
            near(c, side, side).start()

    def fourth(c):
        other(c, 0).wait_recv()
        other(c, 1).wait_recv()
        z_out[c, 1] = (
            rows_of(c, 0, True) + other_in[c, 0].astype(f32) + other_in[c, 1].astype(f32)
        ).astype(bf16)
        cross(c, 1).start()

    def fifth(c):
        for side in range(2):
            for at in range(2):
                near(c, side, at).wait_recv()
        cross(c, 1).wait_recv()
        for at in range(2):
            here = slice(at * half, (at + 1) * half)
            out_ref[:, c * cw + at * half : c * cw + (at + 1) * half] = (
                rows_of(c, 0, False, at * half, half)
                + near_in[c, 0, at].astype(f32)
                + near_in[c, 1, at].astype(f32)
                + z_in[c, 1, :, here].astype(f32)
            ).astype(bf16)

    first(0)
    first(1)
    for n in range(OUT_CHUNKS + 3):
        if n < OUT_CHUNKS:
            second(n)
        if n + 2 < OUT_CHUNKS:
            first(n + 2)
        if 1 <= n <= OUT_CHUNKS:
            third(n - 1)
            fourth(n - 1)
        if n >= 3:
            fifth(n - 3)
    for c in range(OUT_CHUNKS):
        for side in range(2):
            far(c, side).wait_send()
            other(c, side).wait_send()
            cross(c, side).wait_send()
            for at in range(2):
                near(c, side, at).wait_send()


def project_out(attended, w_out):
    rows, depth = attended.shape
    width = w_out.shape[1]
    n, cw = OUT_CHUNKS, width // OUT_CHUNKS
    half = cw // 2
    seat = rows // 8
    bf16 = jnp.bfloat16
    dma = pltpu.SemaphoreType.DMA
    return pl.pallas_call(
        project_out_kernel,
        out_shape=jax.ShapeDtypeStruct((seat, width), bf16),
        in_specs=[
            pl.BlockSpec(memory_space=pltpu.VMEM),
            pl.BlockSpec(memory_space=pltpu.HBM),
        ],
        out_specs=pl.BlockSpec(memory_space=pltpu.VMEM),
        scratch_shapes=[
            pltpu.VMEM((n, depth, cw), bf16),
            pltpu.VMEM((n, rows, cw), jnp.float32),
            pltpu.VMEM((n, 2, seat, half), bf16),
            pltpu.VMEM((n, 2, seat, half), bf16),
            pltpu.VMEM((n, 2, 2, seat, half), bf16),
            pltpu.VMEM((n, 2, 2, seat, half), bf16),
            pltpu.VMEM((n, 2, seat, cw), bf16),
            pltpu.VMEM((n, 2, seat, cw), bf16),
            pltpu.VMEM((n, 2, seat, cw), bf16),
            pltpu.VMEM((n, 2, seat, cw), bf16),
            dma((n,)),
            dma((n, 2)),
            dma((n, 2)),
            dma((n, 2, 2)),
            dma((n, 2, 2)),
            dma((n, 2)),
            dma((n, 2)),
            dma((n, 2)),
            dma((n, 2)),
        ],
        compiler_params=pltpu.CompilerParams(
            collective_id=1, has_side_effects=True, vmem_limit_bytes=56 * MIB
        ),
        name="project_out",
    )(attended, w_out)


IN_CHUNKS = 2
PART_ROWS = (256, 128, 128)
PART_CHUNKS = (2, 1, 1)
SLOTS = 64
AHEAD = 3
QUERIES_LATER = 0
STEPS = [(p, f) for p, n in enumerate(PART_CHUNKS) for f in range(n)]
PARTS = len(PART_ROWS)


def gather_kernel(
    target_ref, position_ref, turn_ref, x_hbm, wq_hbm, wk_hbm, wv_hbm, q_ref, kv_ref,
    x_ref, cos_ref, sin_ref, w_ref, pick, place, send, recv, meta_out, meta_in, in_sem, row_ss,
    row_rs, meta_ss, meta_rs, ag_ss, ag_rs, kv_sem, kv_ss, kv_rs, *per_part,
):
    ctx = lax.axis_index("ctx")
    peers = lax.axis_size("ctx")
    rows, cols = x_ref.shape
    chunk = cols // IN_CHUNKS
    pieces, acc, kv_own = (per_part[i * PARTS : (i + 1) * PARTS] for i in range(3))
    starts = [sum(PART_ROWS[:p]) for p in range(PARTS)]
    y, zh, up, down, across = ring_places()
    bf16 = jnp.bfloat16
    loads = [
        pltpu.make_async_copy(src, dst, in_sem.at[i])
        for i, (src, dst) in enumerate(
            (
                (x_hbm, x_ref),
                (wq_hbm, w_ref.at[:, 0:512]),
                (wk_hbm, w_ref.at[:, 512:640]),
                (wv_hbm, w_ref.at[:, 640:768]),
            )
        )
    ]
    loads[0].start()
    barrier = pltpu.get_barrier_semaphore()
    for k in range(1, peers):
        pl.semaphore_signal(
            barrier, inc=1, device_id={"ctx": (ctx + k) % peers},
            device_id_type=pl.DeviceIdType.MESH,
        )
    for peer in (up, down, across):
        pl.semaphore_signal(
            barrier, inc=1, device_id={"head": peer}, device_id_type=pl.DeviceIdType.MESH
        )

    target = target_ref[...]
    owner = target // rows
    local = target - owner * rows
    owned = lax.broadcasted_iota(jnp.int32, (peers, rows), 0) == owner
    owned_f = jnp.where(owned, 1.0, 0.0).astype(jnp.float32)
    earlier = (
        lax.broadcasted_iota(jnp.int32, (rows, rows), 0)
        < lax.broadcasted_iota(jnp.int32, (rows, rows), 1)
    )
    before = jnp.dot(
        owned_f.astype(bf16),
        jnp.where(earlier, 1.0, 0.0).astype(bf16),
        preferred_element_type=jnp.float32,
    )
    rank = jnp.sum(owned_f * before, axis=0, keepdims=True)
    slot = owner * SLOTS + rank.astype(jnp.int32)
    for i in range(peers):
        at = lax.broadcasted_iota(jnp.int32, (SLOTS, rows), 0) + i * SLOTS
        pick[i * SLOTS : (i + 1) * SLOTS, :] = jnp.where(at == slot, 1.0, 0.0).astype(bf16)

    def meta_copy(k):
        to = (ctx + k) % peers
        return remote(meta_out.at[to], meta_in.at[k], meta_ss.at[k], meta_rs.at[k], ctx=to)

    def row_copy(f, k):
        to = (ctx + k) % peers
        return remote(
            send.at[f, pl.ds(pl.multiple_of(to * SLOTS, SLOTS), SLOTS)],
            recv.at[f, pl.ds(k * SLOTS, SLOTS)],
            row_ss.at[f, k], row_rs.at[f, k], ctx=to,
        )

    line = lax.broadcasted_iota(jnp.int32, (8, rows), 0)
    high = local // 16
    facts = jnp.where(line == 0, high, jnp.where(line == 1, local - high * 16, 1))
    facts = lax.dot_general(
        facts.astype(jnp.float32).astype(bf16), pick[...], (((1,), (1,)), ((), ())),
        preferred_element_type=jnp.float32,
    )
    goes_to = jnp.where(facts[2:3] > 0.5, facts[0:1] * 16.0 + facts[1:2], -1.0)
    goes_to = jnp.broadcast_to(goes_to, (8, peers * SLOTS))
    for i in range(peers // 2):
        tile = goes_to[:, i * 128 : (i + 1) * 128]
        meta_out[2 * i] = tile
        meta_out[2 * i + 1] = pltpu.roll(tile, SLOTS, 1)
    pl.semaphore_wait(barrier, peers - 1 + 3)
    for k in range(1, peers):
        meta_copy(k).start()
    meta_in[0] = meta_out[ctx]

    loads[0].wait()
    for load in loads[1:]:
        load.start()
    for f in range(IN_CHUNKS):
        send[f] = jnp.dot(
            pick[...], x_ref[:, f * chunk : (f + 1) * chunk], preferred_element_type=jnp.float32
        ).astype(bf16)
        for k in range(1, peers):
            row_copy(f, k).start()
        recv[f, 0:SLOTS, :] = send[f, pl.ds(pl.multiple_of(ctx * SLOTS, SLOTS), SLOTS), :]

    for i in range(rows // 128):
        here = slice(i * 128, (i + 1) * 128)
        angle = position_ref[:, here].astype(jnp.float32)
        angle = jnp.broadcast_to(angle, (128, 128)).T * turn_ref[0:1]
        cos_ref[here, :] = jnp.cos(angle)
        sin_ref[here, :] = jnp.sin(angle) * turn_ref[1:2]

    for k in range(1, peers):
        meta_copy(k).wait_recv()
    lane = lax.broadcasted_iota(jnp.int32, (8, 128), 1)
    for i in range(peers // 2):
        both = jnp.where(lane < SLOTS, meta_in[2 * i], pltpu.roll(meta_in[2 * i + 1], SLOTS, 1))
        both = both[0:1].astype(jnp.int32)
        at = lax.broadcasted_iota(jnp.int32, (rows, 128), 0)
        place[:, i * 128 : (i + 1) * 128] = jnp.where(at == both, 1.0, 0.0).astype(bf16)

    def piece(dy, other):
        return ((y + dy) % 4) * 2 + ((1 - zh) if other else zh)

    def spread(n, e):
        part, f = STEPS[n]
        size, half = PART_ROWS[part], PART_ROWS[part] // 2
        src, lo, size, to = (
            (piece(0, 0), 0, size, across),
            (piece(0, 0), 0, size, up),
            (piece(0, 0), 0, size, down),
            (piece(3, 0), 0, half, up),
            (piece(1, 0), half, half, down),
            (piece(0, 1), 0, size, up),
            (piece(0, 1), 0, size, down),
            (piece(2, 0), 0, size, across),
        )[e]
        ref = pieces[part].at[src, f, pl.ds(lo, size)]
        return remote(ref, ref, ag_ss.at[n, e], ag_rs.at[n, e], head=to)

    def product(part, index, columns):
        piece_rows = jnp.concatenate(
            [pieces[part][index, g] for g in range(PART_CHUNKS[part])], axis=1
        )
        deep = index * cols
        deep = pl.ds(deep if isinstance(deep, int) else pl.multiple_of(deep, cols), cols)
        return jnp.dot(piece_rows, w_ref[deep, columns], preferred_element_type=jnp.float32)

    def project(n, index, first=False):
        part, f = STEPS[n]
        if f < PART_CHUNKS[part] - 1:
            return
        term = product(part, index, slice(512, 768))
        acc[part][...] = term if first else acc[part][...] + term

    def begin(n):
        part, f = STEPS[n]
        if part == 0:
            for k in range(1, peers):
                row_copy(f, k).wait_recv()
        here = slice(starts[part], starts[part] + PART_ROWS[part])
        wide = IN_CHUNKS // PART_CHUNKS[part]
        for g in range(wide):
            pieces[part][piece(0, 0), f, :, g * chunk : (g + 1) * chunk] = jnp.dot(
                place[here, :], recv[f * wide + g], preferred_element_type=jnp.float32
            ).astype(bf16)
        for e in (1, 2, 0):
            spread(n, e).start()
        if n == IN_CHUNKS - 1:
            for load in loads[1:]:
                load.wait()
        project(n, piece(0, 0), first=True)

    def near(n):
        spread(n, 1).wait_recv()
        spread(n, 3).start()
        spread(n, 2).wait_recv()
        spread(n, 4).start()
        spread(n, 0).wait_recv()
        spread(n, 5).start()
        spread(n, 6).start()
        project(n, piece(3, 0))
        project(n, piece(1, 0))
        project(n, piece(0, 1))

    def far(n):
        spread(n, 3).wait_recv()
        spread(n, 4).wait_recv()
        spread(n, 7).start()
        project(n, piece(2, 0))

    def other(n):
        spread(n, 5).wait_recv()
        spread(n, 6).wait_recv()
        project(n, piece(3, 1))
        project(n, piece(1, 1))
        spread(n, 7).wait_recv()
        project(n, piece(2, 1))

    zl, x, core = ctx // 8, (ctx // 2) % 4, ctx % 2

    def block(dx, other_z, other_core=0):
        z = (1 - zl) if other_z else zl
        c = (1 - core) if other_core else core
        return z * 8 + ((x + dx) % 4) * 2 + c

    kv_pieces = ((0, 0), (0, 1), (3, 0), (1, 0), (2, 0), (3, 1), (1, 1), (2, 1))

    def share(part, e):
        right, left, over = block(1, 0), block(3, 0), block(0, 1)
        part_rows = PART_ROWS[part]
        if e >= 8:
            src, to = block(*kv_pieces[e - 8]), block(0, 0, 1)
        else:
            src, to = (
                (block(0, 0), over),
                (block(0, 0), right),
                (block(0, 0), left),
                (block(0, 0), block(2, 0)),
                (block(0, 1), right),
                (block(0, 1), left),
                (block(0, 1), block(2, 0)),
            )[e]
        ref = kv_ref.at[pl.ds(pl.multiple_of(src * rows + starts[part], 16), part_rows)]
        source = kv_own[part] if e in (0, 1, 2, 3, 8) else ref
        return remote(source, ref, kv_ss.at[part, e], kv_rs.at[part, e], ctx=to)

    def keep(part):
        at = pl.ds(pl.multiple_of(ctx * rows + starts[part], 16), PART_ROWS[part])
        return pltpu.make_async_copy(kv_own[part], kv_ref.at[at], kv_sem.at[part])

    def turn(tensor, here):
        return tensor * cos_ref[here, :] + pltpu.roll(tensor, HD // 2, 1) * sin_ref[here, :]

    def finish(part):
        here = slice(starts[part], starts[part] + PART_ROWS[part])
        kv_own[part][:, 0:HD] = turn(acc[part][:, 0:HD], here).astype(bf16)
        kv_own[part][:, HD : 2 * HD] = acc[part][:, HD : 2 * HD].astype(bf16)
        give(part, 0, zl == 0)
        give(part, 1, x < 3)
        give(part, 2, x == 0)
        give(part, 3, x < 2)
        share(part, 8).start()
        keep(part).start()

    def finish_queries(part):
        here = slice(starts[part], starts[part] + PART_ROWS[part])
        query = product(part, 0, slice(0, 512))
        for index in range(1, 8):
            query = query + product(part, index, slice(0, 512))
        for h in range(4):
            at = slice(h * HD, (h + 1) * HD)
            q_ref[here, at] = turn(query[:, at], here).astype(bf16)

    def give(part, e, when):
        @pl.when(when)
        def _():
            share(part, e).start()

    def share_near(part):
        @pl.when(zl == 1)
        def _():
            share(part, 0).wait_recv()
            for e in (4, 5, 6, 9):
                share(part, e).start()

    def pass_on(part, e, core_e, when):
        @pl.when(when)
        def _():
            share(part, e).wait_recv()
            share(part, core_e).start()

    def share_far(part):
        pass_on(part, 1, 10, x > 0)
        pass_on(part, 2, 11, x == 3)
        pass_on(part, 3, 12, x > 1)

    def share_other(part):
        @pl.when(zl == 1)
        def _():
            for e in (4, 5, 6):
                share(part, e).wait_recv()
                share(part, e + 9).start()

    count = len(STEPS)
    due = {}
    for part in range(PARTS):
        last = sum(PART_CHUNKS[: part + 1]) + 1
        for later, rank_in, act in (
            (0, 0, finish), (1, 1, share_near), (2, 1, share_far), (3, 1, share_other),
            (QUERIES_LATER, 2, finish_queries),
        ):
            due.setdefault(last + later, []).append((rank_in, part, act))
    begin(0)
    begin(1)
    begun = 2
    for n in range(max(due) + 1):
        if n < count:
            near(n)
        while begun < min(count, n + (3 if n + 3 <= IN_CHUNKS - 1 or n < 1 else AHEAD + 1)):
            begin(begun)
            begun += 1
        if 1 <= n <= count:
            far(n - 1)
        if 2 <= n <= count + 1:
            other(n - 2)
        for rank_in, part, act in sorted(due.get(n, []), key=lambda item: item[:2]):
            act(part)
    below = zl == 1
    sent = (
        (0, zl == 0), (1, x < 3), (2, x == 0), (3, x < 2), (4, below), (5, below), (6, below),
    )
    copied = (
        (8, None), (9, below), (10, x > 0), (11, x == 3), (12, x > 1), (13, below), (14, below),
        (15, below),
    )

    def drain(part, e, when, received):
        def wait():
            if received:
                share(part, e).wait_recv()
            else:
                share(part, e).wait_send()

        if when is None:
            wait()
        else:
            pl.when(when)(wait)

    for part in range(PARTS):
        for e, when in copied:
            drain(part, e, when, True)

    for k in range(1, peers):
        meta_copy(k).wait_send()
        for f in range(IN_CHUNKS):
            row_copy(f, k).wait_send()
    for n in range(count):
        for e in range(8):
            spread(n, e).wait_send()
    for part in range(PARTS):
        keep(part).wait()
        for e, when in sent + copied:
            drain(part, e, when, False)


def gather_and_project(node_rows, node_target, node_position, w_query, w_key, w_value):
    rows, cols = node_rows.shape
    peers = lax.axis_size("ctx")
    chunk = cols // IN_CHUNKS
    bf16 = jnp.bfloat16
    dma = pltpu.SemaphoreType.DMA
    vmem = pl.BlockSpec(memory_space=pltpu.VMEM)
    hbm = pl.BlockSpec(memory_space=pltpu.HBM)
    entry = np.arange(HD)
    inverse = ROPE_THETA ** ((entry % (HD // 2)) * (-2.0 / HD))
    turns = np.stack([inverse, np.where(entry < HD // 2, -1.0, 1.0)]).astype(np.float32)
    return pl.pallas_call(
        gather_kernel,
        out_shape=(
            jax.ShapeDtypeStruct((rows, 512), bf16),
            jax.ShapeDtypeStruct((rows * peers, 256), bf16),
        ),
        in_specs=[vmem] * 3 + [hbm] * 4,
        out_specs=(vmem, hbm),
        scratch_shapes=[
            pltpu.VMEM((rows, cols), bf16),
            pltpu.VMEM((rows, HD), jnp.float32),
            pltpu.VMEM((rows, HD), jnp.float32),
            pltpu.VMEM((w_query.shape[0], 768), bf16),
            pltpu.VMEM((peers * SLOTS, rows), bf16),
            pltpu.VMEM((rows, peers * SLOTS), bf16),
            pltpu.VMEM((IN_CHUNKS, peers * SLOTS, chunk), bf16),
            pltpu.VMEM((IN_CHUNKS, peers * SLOTS, chunk), bf16),
            pltpu.VMEM((peers, 8, 128), jnp.float32),
            pltpu.VMEM((peers, 8, 128), jnp.float32),
            dma((4,)),
            dma((IN_CHUNKS, peers)),
            dma((IN_CHUNKS, peers)),
            dma((peers,)),
            dma((peers,)),
            dma((len(STEPS), 8)),
            dma((len(STEPS), 8)),
            dma((PARTS,)),
            dma((PARTS, 16)),
            dma((PARTS, 16)),
        ]
        + [pltpu.VMEM((8, n, r, cols // n), bf16) for r, n in zip(PART_ROWS, PART_CHUNKS)]
        + [pltpu.VMEM((r, 256), jnp.float32) for r in PART_ROWS]
        + [pltpu.VMEM((r, 256), bf16) for r in PART_ROWS],
        compiler_params=pltpu.CompilerParams(
            collective_id=2, has_side_effects=True, vmem_limit_bytes=60 * MIB
        ),
        name="gather_and_project",
    )(
        node_target.reshape(1, rows), node_position.reshape(1, rows), jnp.asarray(turns), node_rows,
        w_query, w_key, w_value,
    )


def on_device(node_rows, node_target, node_position, block_mask, w_query, w_key, w_value, w_out):
    queries, kv = gather_and_project(
        node_rows, node_target, node_position, w_query, w_key, w_value
    )
    attended = attend(block_mask, queries, kv)
    return project_out(attended, w_out)


def solution(mesh):
    placed = (
        P("ctx", "head"),
        P("ctx"),
        P("ctx"),
        P("ctx", None),
        P(None, "head"),
        P(None, "head"),
        P(None, "head"),
        P("head", None),
    )
    return jax.shard_map(
        on_device, mesh=mesh, in_specs=placed, out_specs=P(("ctx", "head"), None), check_vma=False
    )
```

```python
import math

import jax
import jax.numpy as jnp
import numpy as np
from jax import lax
from jax.experimental import pallas as pl
from jax.experimental.pallas import tpu as pltpu
from jax.sharding import PartitionSpec as P

HD = 128
BLOCK = 128
ROPE_THETA = 500000.0
NEG_LARGE = -1e30
MIB = 1024 * 1024


def attend_kernel(mask_ref, q_ref, kv_hbm, out_ref, list_ref, kv_ref, own_ref, acc_ref, stat_ref, sem):
    ctx = lax.axis_index("ctx")
    rows = q_ref.shape[0]
    local_blocks = rows // BLOCK
    heads = q_ref.shape[1] // HD
    block_count = mask_ref.shape[1]
    width = heads * BLOCK
    scale = math.log2(math.e) / math.sqrt(HD)
    own = pl.ds(pl.multiple_of(ctx * rows, BLOCK), rows)
    own_load = pltpu.make_async_copy(kv_hbm.at[own], own_ref, sem.at[0])
    load = pltpu.make_async_copy(kv_hbm, kv_ref, sem.at[1])
    own_load.start()
    load.start()

    def build(kb, counts):
        for b in range(local_blocks):
            list_ref[b, counts[b]] = kb
        return tuple(n + mask_ref[b, kb] for b, n in enumerate(counts))

    counts = lax.fori_loop(
        0, block_count, build, (jnp.int32(0),) * local_blocks, unroll=8
    )

    def queries_of(b):
        at = slice(b * BLOCK, (b + 1) * BLOCK)
        return jnp.concatenate([q_ref[at, h * HD : (h + 1) * HD] for h in range(heads)], axis=0)

    def score(keys, b):
        return scale * lax.dot_general(
            keys, queries_of(b), (((1,), (1,)), ((), ())), preferred_element_type=jnp.float32
        )

    def mix(values, weights):
        return lax.dot_general(
            values, weights.astype(jnp.bfloat16), (((0,), (0,)), ((), ())),
            preferred_element_type=jnp.float32,
        )

    own_load.wait()
    key_at = lax.broadcasted_iota(jnp.int32, (BLOCK, width), 0)
    query_at = lax.broadcasted_iota(jnp.int32, (BLOCK, width), 1) % BLOCK
    for b in range(local_blocks):
        at = slice(b * BLOCK, (b + 1) * BLOCK)
        scores = jnp.where(key_at <= query_at, score(own_ref[at, 0:HD], b), NEG_LARGE)
        highest = jnp.max(scores, axis=0, keepdims=True)
        weights = jnp.exp2(scores - highest)
        stat_ref[b, 0:1] = highest
        stat_ref[b, 1:2] = jnp.sum(weights, axis=0, keepdims=True)
        acc_ref[b] = mix(own_ref[at, HD : 2 * HD], weights)
    load.wait()

    def add_two(b, i):
        places, drops = [], []
        for at in (2 * i, 2 * i + 1):
            real = at < counts[b]
            kb = jnp.where(real, list_ref[b, jnp.where(real, at, 0)], 0)
            places.append(pl.ds(pl.multiple_of(kb * BLOCK, BLOCK), BLOCK))
            drops.append(jnp.where(real, 0.0, NEG_LARGE).astype(jnp.float32))
        keys = jnp.concatenate([kv_ref[at, 0:HD] for at in places], axis=0)
        values = jnp.concatenate([kv_ref[at, HD : 2 * HD] for at in places], axis=0)
        scores = score(keys, b)
        scores = jnp.concatenate(
            [scores[:BLOCK] + drops[0], scores[BLOCK:] + drops[1]], axis=0
        )
        old = stat_ref[b, 0:1]
        highest = jnp.maximum(old, jnp.max(scores, axis=0, keepdims=True))
        factor = jnp.exp2(old - highest)
        weights = jnp.exp2(scores - highest)
        stat_ref[b, 0:1] = highest
        stat_ref[b, 1:2] = stat_ref[b, 1:2] * factor + jnp.sum(weights, axis=0, keepdims=True)
        acc_ref[b] = acc_ref[b] * factor + mix(values, weights)

    for b in range(0, local_blocks, 2):

        def step(i, carry, b=b):
            add_two(b, i)
            add_two(b + 1, i)
            return carry

        lax.fori_loop(0, (jnp.maximum(counts[b], counts[b + 1]) + 1) // 2, step, 0)
    for b in range(local_blocks):
        attended = (acc_ref[b] * (1.0 / stat_ref[b, 1:2])).astype(jnp.bfloat16)
        for h in range(heads):
            out_ref[b * BLOCK : (b + 1) * BLOCK, h * HD : (h + 1) * HD] = attended[
                :, h * BLOCK : (h + 1) * BLOCK
            ].T


def attend(block_mask, queries, kv):
    rows, width = queries.shape
    blocks = rows // BLOCK
    return pl.pallas_call(
        attend_kernel,
        out_shape=pltpu.VMEM(queries.shape, jnp.bfloat16),
        in_specs=[
            pl.BlockSpec(memory_space=pltpu.SMEM),
            pl.BlockSpec(memory_space=pltpu.VMEM),
            pl.BlockSpec(memory_space=pltpu.HBM),
        ],
        out_specs=pl.BlockSpec(memory_space=pltpu.VMEM),
        scratch_shapes=[
            pltpu.SMEM((blocks, 128), jnp.int32),
            pltpu.VMEM(kv.shape, jnp.bfloat16),
            pltpu.VMEM((rows, kv.shape[1]), jnp.bfloat16),
            pltpu.VMEM((blocks, HD, width), jnp.float32),
            pltpu.VMEM((blocks, 8, width), jnp.float32),
            pltpu.SemaphoreType.DMA((2,)),
        ],
        compiler_params=pltpu.CompilerParams(vmem_limit_bytes=60 * MIB),
        name="attend",
    )(block_mask, queries, kv)


def ring_places():
    head = lax.axis_index("head")
    y, zh = head // 2, head % 2
    up = ((y + 1) % 4) * 2 + zh
    down = ((y + 3) % 4) * 2 + zh
    across = y * 2 + (1 - zh)
    return y, zh, up, down, across


def remote(src, dst, send_sem, recv_sem, **place):
    return pltpu.make_async_remote_copy(
        src_ref=src,
        dst_ref=dst,
        send_sem=send_sem,
        recv_sem=recv_sem,
        device_id=place,
        device_id_type=pl.DeviceIdType.MESH,
    )


OUT_CHUNKS = 8


def project_out_kernel(
    att_ref, w_hbm, out_ref, w_ref, part, far_out, far_in, near_out, near_in, other_out, other_in,
    z_out, z_in, w_sem, far_ss, far_rs, near_ss, near_rs, other_ss, other_rs, z_ss, z_rs,
):
    y, zh, up, down, across = ring_places()
    cw = part.shape[2]
    half = cw // 2
    seat = part.shape[1] // 8
    loads = [
        pltpu.make_async_copy(w_hbm.at[:, pl.ds(c * cw, cw)], w_ref.at[c], w_sem.at[c])
        for c in range(OUT_CHUNKS)
    ]
    loads[0].start()
    barrier = pltpu.get_barrier_semaphore()
    for peer in (up, down, across):
        pl.semaphore_signal(
            barrier, inc=1, device_id={"head": peer}, device_id_type=pl.DeviceIdType.MESH
        )

    def rows_of(c, dy, other, lo=0, size=None):
        index = ((y + dy) % 4) * 2 + ((1 - zh) if other else zh)
        return part[
            c, pl.ds(pl.multiple_of(index * seat, seat), seat), lo : lo + (size or cw)
        ]

    def far(c, side):
        return remote(
            far_out.at[c, side], far_in.at[c, side], far_ss.at[c, side], far_rs.at[c, side],
            head=(up, down)[side],
        )

    def near(c, side, at):
        return remote(
            near_out.at[c, side, at], near_in.at[c, side, at],
            near_ss.at[c, side, at], near_rs.at[c, side, at],
            head=(up, down)[side],
        )

    def other(c, side):
        return remote(
            other_out.at[c, side], other_in.at[c, side], other_ss.at[c, side],
            other_rs.at[c, side], head=(up, down)[side],
        )

    def cross(c, which):
        return remote(
            z_out.at[c, which], z_in.at[c, which], z_ss.at[c, which], z_rs.at[c, which],
            head=across,
        )

    f32, bf16 = jnp.float32, jnp.bfloat16

    def first(c):
        loads[c].wait()
        if c == 0:
            for load in loads[1:]:
                load.start()
        part[c] = jnp.dot(att_ref[...], w_ref[c], preferred_element_type=f32)
        if c == 0:
            pl.semaphore_wait(barrier, 3)
        z_out[c, 0] = rows_of(c, 2, True).astype(bf16)
        cross(c, 0).start()
        for side, dy in ((0, 1), (1, 3)):
            other_out[c, side] = rows_of(c, dy, True).astype(bf16)
            other(c, side).start()
        near_out[c, 0, 1] = rows_of(c, 1, False, half, half).astype(bf16)
        near(c, 0, 1).start()
        near_out[c, 1, 0] = rows_of(c, 3, False, 0, half).astype(bf16)
        near(c, 1, 0).start()

    def second(c):
        cross(c, 0).wait_recv()
        for side in range(2):
            far_out[c, side] = (
                rows_of(c, 2, False, side * half, half)
                + z_in[c, 0, :, side * half : (side + 1) * half].astype(f32)
            ).astype(bf16)
            far(c, side).start()

    def third(c):
        for side, dy in ((0, 1), (1, 3)):
            far(c, side).wait_recv()
            near_out[c, side, side] = (
                rows_of(c, dy, False, side * half, half) + far_in[c, side].astype(f32)
            ).astype(bf16)
            near(c, side, side).start()

    def fourth(c):
        other(c, 0).wait_recv()
        other(c, 1).wait_recv()
        z_out[c, 1] = (
            rows_of(c, 0, True) + other_in[c, 0].astype(f32) + other_in[c, 1].astype(f32)
        ).astype(bf16)
        cross(c, 1).start()

    def fifth(c):
        for side in range(2):
            for at in range(2):
                near(c, side, at).wait_recv()
        cross(c, 1).wait_recv()
        for at in range(2):
            here = slice(at * half, (at + 1) * half)
            out_ref[:, c * cw + at * half : c * cw + (at + 1) * half] = (
                rows_of(c, 0, False, at * half, half)
                + near_in[c, 0, at].astype(f32)
                + near_in[c, 1, at].astype(f32)
                + z_in[c, 1, :, here].astype(f32)
            ).astype(bf16)

    first(0)
    first(1)
    for n in range(OUT_CHUNKS + 3):
        if n < OUT_CHUNKS:
            second(n)
        if n + 2 < OUT_CHUNKS:
            first(n + 2)
        if 1 <= n <= OUT_CHUNKS:
            third(n - 1)
            fourth(n - 1)
        if n >= 3:
            fifth(n - 3)
    for c in range(OUT_CHUNKS):
        for side in range(2):
            far(c, side).wait_send()
            other(c, side).wait_send()
            cross(c, side).wait_send()
            for at in range(2):
                near(c, side, at).wait_send()


def project_out(attended, w_out):
    rows, depth = attended.shape
    width = w_out.shape[1]
    n, cw = OUT_CHUNKS, width // OUT_CHUNKS
    half = cw // 2
    seat = rows // 8
    bf16 = jnp.bfloat16
    dma = pltpu.SemaphoreType.DMA
    return pl.pallas_call(
        project_out_kernel,
        out_shape=pltpu.VMEM((seat, width), bf16),
        in_specs=[
            pl.BlockSpec(memory_space=pltpu.VMEM),
            pl.BlockSpec(memory_space=pltpu.HBM),
        ],
        out_specs=pl.BlockSpec(memory_space=pltpu.VMEM),
        scratch_shapes=[
            pltpu.VMEM((n, depth, cw), bf16),
            pltpu.VMEM((n, rows, cw), jnp.float32),
            pltpu.VMEM((n, 2, seat, half), bf16),
            pltpu.VMEM((n, 2, seat, half), bf16),
            pltpu.VMEM((n, 2, 2, seat, half), bf16),
            pltpu.VMEM((n, 2, 2, seat, half), bf16),
            pltpu.VMEM((n, 2, seat, cw), bf16),
            pltpu.VMEM((n, 2, seat, cw), bf16),
            pltpu.VMEM((n, 2, seat, cw), bf16),
            pltpu.VMEM((n, 2, seat, cw), bf16),
            dma((n,)),
            dma((n, 2)),
            dma((n, 2)),
            dma((n, 2, 2)),
            dma((n, 2, 2)),
            dma((n, 2)),
            dma((n, 2)),
            dma((n, 2)),
            dma((n, 2)),
        ],
        compiler_params=pltpu.CompilerParams(
            collective_id=1, has_side_effects=True, vmem_limit_bytes=60 * MIB
        ),
        name="project_out",
    )(attended, w_out)


IN_CHUNKS = 2
PART_ROWS = (256, 128, 128)
PART_CHUNKS = (2, 1, 1)
SLOTS = 64
AHEAD = 3
QUERIES_LATER = 0
STEPS = [(p, f) for p, n in enumerate(PART_CHUNKS) for f in range(n)]
PARTS = len(PART_ROWS)


def gather_kernel(
    target_ref, position_ref, turn_ref, x_hbm, wq_hbm, wk_hbm, wv_hbm, q_ref, kv_ref,
    x_ref, cos_ref, sin_ref, w_ref, pick, place, send, recv, meta_out, meta_in, in_sem, row_ss,
    row_rs, meta_ss, meta_rs, ag_ss, ag_rs, kv_sem, kv_ss, kv_rs, *per_part,
):
    ctx = lax.axis_index("ctx")
    peers = lax.axis_size("ctx")
    rows, cols = x_ref.shape
    chunk = cols // IN_CHUNKS
    pieces, acc, kv_own = (per_part[i * PARTS : (i + 1) * PARTS] for i in range(3))
    starts = [sum(PART_ROWS[:p]) for p in range(PARTS)]
    y, zh, up, down, across = ring_places()
    bf16 = jnp.bfloat16
    loads = [
        pltpu.make_async_copy(src, dst, in_sem.at[i])
        for i, (src, dst) in enumerate(
            (
                (x_hbm, x_ref),
                (wq_hbm, w_ref.at[:, 0:512]),
                (wk_hbm, w_ref.at[:, 512:640]),
                (wv_hbm, w_ref.at[:, 640:768]),
            )
        )
    ]
    loads[0].start()
    barrier = pltpu.get_barrier_semaphore()
    for k in range(1, peers):
        pl.semaphore_signal(
            barrier, inc=1, device_id={"ctx": (ctx + k) % peers},
            device_id_type=pl.DeviceIdType.MESH,
        )
    for peer in (up, down, across):
        pl.semaphore_signal(
            barrier, inc=1, device_id={"head": peer}, device_id_type=pl.DeviceIdType.MESH
        )

    target = target_ref[...]
    owner = target // rows
    local = target - owner * rows
    owned = lax.broadcasted_iota(jnp.int32, (peers, rows), 0) == owner
    owned_f = jnp.where(owned, 1.0, 0.0).astype(jnp.float32)
    earlier = (
        lax.broadcasted_iota(jnp.int32, (rows, rows), 0)
        < lax.broadcasted_iota(jnp.int32, (rows, rows), 1)
    )
    before = jnp.dot(
        owned_f.astype(bf16),
        jnp.where(earlier, 1.0, 0.0).astype(bf16),
        preferred_element_type=jnp.float32,
    )
    rank = jnp.sum(owned_f * before, axis=0, keepdims=True)
    slot = owner * SLOTS + rank.astype(jnp.int32)
    for i in range(peers):
        at = lax.broadcasted_iota(jnp.int32, (SLOTS, rows), 0) + i * SLOTS
        pick[i * SLOTS : (i + 1) * SLOTS, :] = jnp.where(at == slot, 1.0, 0.0).astype(bf16)

    def meta_copy(k):
        to = (ctx + k) % peers
        return remote(meta_out.at[to], meta_in.at[k], meta_ss.at[k], meta_rs.at[k], ctx=to)

    def row_copy(f, k):
        to = (ctx + k) % peers
        return remote(
            send.at[f, pl.ds(pl.multiple_of(to * SLOTS, SLOTS), SLOTS)],
            recv.at[f, pl.ds(k * SLOTS, SLOTS)],
            row_ss.at[f, k], row_rs.at[f, k], ctx=to,
        )

    line = lax.broadcasted_iota(jnp.int32, (8, rows), 0)
    high = local // 16
    facts = jnp.where(line == 0, high, jnp.where(line == 1, local - high * 16, 1))
    facts = lax.dot_general(
        facts.astype(jnp.float32).astype(bf16), pick[...], (((1,), (1,)), ((), ())),
        preferred_element_type=jnp.float32,
    )
    goes_to = jnp.where(facts[2:3] > 0.5, facts[0:1] * 16.0 + facts[1:2], -1.0)
    goes_to = jnp.broadcast_to(goes_to, (8, peers * SLOTS))
    for i in range(peers // 2):
        tile = goes_to[:, i * 128 : (i + 1) * 128]
        meta_out[2 * i] = tile
        meta_out[2 * i + 1] = pltpu.roll(tile, SLOTS, 1)
    pl.semaphore_wait(barrier, peers - 1 + 3)
    for k in range(1, peers):
        meta_copy(k).start()
    meta_in[0] = meta_out[ctx]

    loads[0].wait()
    for load in loads[1:]:
        load.start()
    for f in range(IN_CHUNKS):
        send[f] = jnp.dot(
            pick[...], x_ref[:, f * chunk : (f + 1) * chunk], preferred_element_type=jnp.float32
        ).astype(bf16)
        for k in range(1, peers):
            row_copy(f, k).start()
        recv[f, 0:SLOTS, :] = send[f, pl.ds(pl.multiple_of(ctx * SLOTS, SLOTS), SLOTS), :]

    for i in range(rows // 128):
        here = slice(i * 128, (i + 1) * 128)
        angle = position_ref[:, here].astype(jnp.float32)
        angle = jnp.broadcast_to(angle, (128, 128)).T * turn_ref[0:1]
        cos_ref[here, :] = jnp.cos(angle)
        sin_ref[here, :] = jnp.sin(angle) * turn_ref[1:2]

    for k in range(1, peers):
        meta_copy(k).wait_recv()
    lane = lax.broadcasted_iota(jnp.int32, (8, 128), 1)
    for i in range(peers // 2):
        both = jnp.where(lane < SLOTS, meta_in[2 * i], pltpu.roll(meta_in[2 * i + 1], SLOTS, 1))
        both = both[0:1].astype(jnp.int32)
        at = lax.broadcasted_iota(jnp.int32, (rows, 128), 0)
        place[:, i * 128 : (i + 1) * 128] = jnp.where(at == both, 1.0, 0.0).astype(bf16)

    def piece(dy, other):
        return ((y + dy) % 4) * 2 + ((1 - zh) if other else zh)

    def spread(n, e):
        part, f = STEPS[n]
        size, half = PART_ROWS[part], PART_ROWS[part] // 2
        src, lo, size, to = (
            (piece(0, 0), 0, size, across),
            (piece(0, 0), 0, size, up),
            (piece(0, 0), 0, size, down),
            (piece(3, 0), 0, half, up),
            (piece(1, 0), half, half, down),
            (piece(0, 1), 0, size, up),
            (piece(0, 1), 0, size, down),
            (piece(2, 0), 0, size, across),
        )[e]
        ref = pieces[part].at[src, f, pl.ds(lo, size)]
        return remote(ref, ref, ag_ss.at[n, e], ag_rs.at[n, e], head=to)

    def product(part, index, columns):
        piece_rows = jnp.concatenate(
            [pieces[part][index, g] for g in range(PART_CHUNKS[part])], axis=1
        )
        deep = index * cols
        deep = pl.ds(deep if isinstance(deep, int) else pl.multiple_of(deep, cols), cols)
        return jnp.dot(piece_rows, w_ref[deep, columns], preferred_element_type=jnp.float32)

    def project(n, index, first=False):
        part, f = STEPS[n]
        if f < PART_CHUNKS[part] - 1:
            return
        term = product(part, index, slice(512, 768))
        acc[part][...] = term if first else acc[part][...] + term

    def begin(n):
        part, f = STEPS[n]
        if part == 0:
            for k in range(1, peers):
                row_copy(f, k).wait_recv()
        here = slice(starts[part], starts[part] + PART_ROWS[part])
        wide = IN_CHUNKS // PART_CHUNKS[part]
        for g in range(wide):
            pieces[part][piece(0, 0), f, :, g * chunk : (g + 1) * chunk] = jnp.dot(
                place[here, :], recv[f * wide + g], preferred_element_type=jnp.float32
            ).astype(bf16)
        for e in (1, 2, 0):
            spread(n, e).start()
        if n == IN_CHUNKS - 1:
            for load in loads[1:]:
                load.wait()
        project(n, piece(0, 0), first=True)

    def near(n):
        spread(n, 1).wait_recv()
        spread(n, 3).start()
        spread(n, 2).wait_recv()
        spread(n, 4).start()
        spread(n, 0).wait_recv()
        spread(n, 5).start()
        spread(n, 6).start()
        project(n, piece(3, 0))
        project(n, piece(1, 0))
        project(n, piece(0, 1))

    def far(n):
        spread(n, 3).wait_recv()
        spread(n, 4).wait_recv()
        spread(n, 7).start()
        project(n, piece(2, 0))

    def other(n):
        spread(n, 5).wait_recv()
        spread(n, 6).wait_recv()
        project(n, piece(3, 1))
        project(n, piece(1, 1))
        spread(n, 7).wait_recv()
        project(n, piece(2, 1))

    zl, x, core = ctx // 8, (ctx // 2) % 4, ctx % 2

    def block(dx, other_z, other_core=0):
        z = (1 - zl) if other_z else zl
        c = (1 - core) if other_core else core
        return z * 8 + ((x + dx) % 4) * 2 + c

    kv_pieces = ((0, 0), (0, 1), (3, 0), (1, 0), (2, 0), (3, 1), (1, 1), (2, 1))

    def share(part, e):
        right, left, over = block(1, 0), block(3, 0), block(0, 1)
        part_rows = PART_ROWS[part]
        if e >= 8:
            src, to = block(*kv_pieces[e - 8]), block(0, 0, 1)
        else:
            src, to = (
                (block(0, 0), over),
                (block(0, 0), right),
                (block(0, 0), left),
                (block(0, 0), block(2, 0)),
                (block(0, 1), right),
                (block(0, 1), left),
                (block(0, 1), block(2, 0)),
            )[e]
        ref = kv_ref.at[pl.ds(pl.multiple_of(src * rows + starts[part], 16), part_rows)]
        source = kv_own[part] if e in (0, 1, 2, 3, 8) else ref
        return remote(source, ref, kv_ss.at[part, e], kv_rs.at[part, e], ctx=to)

    def keep(part):
        at = pl.ds(pl.multiple_of(ctx * rows + starts[part], 16), PART_ROWS[part])
        return pltpu.make_async_copy(kv_own[part], kv_ref.at[at], kv_sem.at[part])

    def turn(tensor, here):
        return tensor * cos_ref[here, :] + pltpu.roll(tensor, HD // 2, 1) * sin_ref[here, :]

    def finish(part):
        here = slice(starts[part], starts[part] + PART_ROWS[part])
        kv_own[part][:, 0:HD] = turn(acc[part][:, 0:HD], here).astype(bf16)
        kv_own[part][:, HD : 2 * HD] = acc[part][:, HD : 2 * HD].astype(bf16)
        give(part, 0, zl == 0)
        give(part, 1, x < 3)
        give(part, 2, x == 0)
        give(part, 3, x < 2)
        share(part, 8).start()
        keep(part).start()

    def finish_queries(part):
        here = slice(starts[part], starts[part] + PART_ROWS[part])
        query = product(part, 0, slice(0, 512))
        for index in range(1, 8):
            query = query + product(part, index, slice(0, 512))
        for h in range(4):
            at = slice(h * HD, (h + 1) * HD)
            q_ref[here, at] = turn(query[:, at], here).astype(bf16)

    def give(part, e, when):
        @pl.when(when)
        def _():
            share(part, e).start()

    def share_near(part):
        @pl.when(zl == 1)
        def _():
            share(part, 0).wait_recv()
            for e in (4, 5, 6, 9):
                share(part, e).start()

    def pass_on(part, e, core_e, when):
        @pl.when(when)
        def _():
            share(part, e).wait_recv()
            share(part, core_e).start()

    def share_far(part):
        pass_on(part, 1, 10, x > 0)
        pass_on(part, 2, 11, x == 3)
        pass_on(part, 3, 12, x > 1)

    def share_other(part):
        @pl.when(zl == 1)
        def _():
            for e in (4, 5, 6):
                share(part, e).wait_recv()
                share(part, e + 9).start()

    count = len(STEPS)
    due = {}
    for part in range(PARTS):
        last = sum(PART_CHUNKS[: part + 1]) + 1
        for later, rank_in, act in (
            (0, 0, finish), (1, 1, share_near), (2, 1, share_far), (3, 1, share_other),
            (QUERIES_LATER, 2, finish_queries),
        ):
            due.setdefault(last + later, []).append((rank_in, part, act))
    begin(0)
    begin(1)
    begun = 2
    for n in range(max(due) + 1):
        if n < count:
            near(n)
        while begun < min(count, n + (3 if n + 3 <= IN_CHUNKS - 1 or n < 1 else AHEAD + 1)):
            begin(begun)
            begun += 1
        if 1 <= n <= count:
            far(n - 1)
        if 2 <= n <= count + 1:
            other(n - 2)
        for rank_in, part, act in sorted(due.get(n, []), key=lambda item: item[:2]):
            act(part)
    below = zl == 1
    sent = (
        (0, zl == 0), (1, x < 3), (2, x == 0), (3, x < 2), (4, below), (5, below), (6, below),
    )
    copied = (
        (8, None), (9, below), (10, x > 0), (11, x == 3), (12, x > 1), (13, below), (14, below),
        (15, below),
    )

    def drain(part, e, when, received):
        def wait():
            if received:
                share(part, e).wait_recv()
            else:
                share(part, e).wait_send()

        if when is None:
            wait()
        else:
            pl.when(when)(wait)

    for part in range(PARTS):
        for e, when in copied:
            drain(part, e, when, True)

    for k in range(1, peers):
        meta_copy(k).wait_send()
        for f in range(IN_CHUNKS):
            row_copy(f, k).wait_send()
    for n in range(count):
        for e in range(8):
            spread(n, e).wait_send()
    for part in range(PARTS):
        keep(part).wait()
        for e, when in sent + copied:
            drain(part, e, when, False)


def gather_and_project(node_rows, node_target, node_position, w_query, w_key, w_value):
    rows, cols = node_rows.shape
    peers = lax.axis_size("ctx")
    chunk = cols // IN_CHUNKS
    bf16 = jnp.bfloat16
    dma = pltpu.SemaphoreType.DMA
    vmem = pl.BlockSpec(memory_space=pltpu.VMEM)
    hbm = pl.BlockSpec(memory_space=pltpu.HBM)
    entry = np.arange(HD)
    inverse = ROPE_THETA ** ((entry % (HD // 2)) * (-2.0 / HD))
    turns = np.stack([inverse, np.where(entry < HD // 2, -1.0, 1.0)]).astype(np.float32)
    return pl.pallas_call(
        gather_kernel,
        out_shape=(
            pltpu.VMEM((rows, 512), bf16),
            jax.ShapeDtypeStruct((rows * peers, 256), bf16),
        ),
        in_specs=[vmem] * 3 + [hbm] * 4,
        out_specs=(vmem, hbm),
        scratch_shapes=[
            pltpu.VMEM((rows, cols), bf16),
            pltpu.VMEM((rows, HD), jnp.float32),
            pltpu.VMEM((rows, HD), jnp.float32),
            pltpu.VMEM((w_query.shape[0], 768), bf16),
            pltpu.VMEM((peers * SLOTS, rows), bf16),
            pltpu.VMEM((rows, peers * SLOTS), bf16),
            pltpu.VMEM((IN_CHUNKS, peers * SLOTS, chunk), bf16),
            pltpu.VMEM((IN_CHUNKS, peers * SLOTS, chunk), bf16),
            pltpu.VMEM((peers, 8, 128), jnp.float32),
            pltpu.VMEM((peers, 8, 128), jnp.float32),
            dma((4,)),
            dma((IN_CHUNKS, peers)),
            dma((IN_CHUNKS, peers)),
            dma((peers,)),
            dma((peers,)),
            dma((len(STEPS), 8)),
            dma((len(STEPS), 8)),
            dma((PARTS,)),
            dma((PARTS, 16)),
            dma((PARTS, 16)),
        ]
        + [pltpu.VMEM((8, n, r, cols // n), bf16) for r, n in zip(PART_ROWS, PART_CHUNKS)]
        + [pltpu.VMEM((r, 256), jnp.float32) for r in PART_ROWS]
        + [pltpu.VMEM((r, 256), bf16) for r in PART_ROWS],
        compiler_params=pltpu.CompilerParams(
            collective_id=2, has_side_effects=True, vmem_limit_bytes=60 * MIB
        ),
        name="gather_and_project",
    )(
        node_target.reshape(1, rows), node_position.reshape(1, rows), jnp.asarray(turns), node_rows,
        w_query, w_key, w_value,
    )


def on_device(node_rows, node_target, node_position, block_mask, w_query, w_key, w_value, w_out):
    queries, kv = gather_and_project(
        node_rows, node_target, node_position, w_query, w_key, w_value
    )
    queries = pltpu.with_memory_space_constraint(queries, pltpu.VMEM)
    attended = attend(block_mask, queries, kv)
    attended = pltpu.with_memory_space_constraint(attended, pltpu.VMEM)
    return project_out(attended, w_out)


def solution(mesh):
    placed = (
        P("ctx", "head"),
        P("ctx"),
        P("ctx"),
        P("ctx", None),
        P(None, "head"),
        P(None, "head"),
        P(None, "head"),
        P("head", None),
    )
    return jax.shard_map(
        on_device, mesh=mesh, in_specs=placed, out_specs=P(("ctx", "head"), None), check_vma=False
    )
```

```python
import math

import jax
import jax.numpy as jnp
import numpy as np
from jax import lax
from jax.experimental import pallas as pl
from jax.experimental.pallas import tpu as pltpu
from jax.sharding import PartitionSpec as P

HD = 128
BLOCK = 128
ROPE_THETA = 500000.0
NEG_LARGE = -1e30
MIB = 1024 * 1024


def attend_kernel(mask_ref, q_ref, kv_hbm, out_ref, list_ref, kv_ref, own_ref, acc_ref, stat_ref, sem):
    ctx = lax.axis_index("ctx")
    rows = q_ref.shape[0]
    local_blocks = rows // BLOCK
    heads = q_ref.shape[1] // HD
    block_count = mask_ref.shape[1]
    width = heads * BLOCK
    scale = math.log2(math.e) / math.sqrt(HD)
    own = pl.ds(pl.multiple_of(ctx * rows, BLOCK), rows)
    own_load = pltpu.make_async_copy(kv_hbm.at[own], own_ref, sem.at[0])
    load = pltpu.make_async_copy(kv_hbm, kv_ref, sem.at[1])
    own_load.start()
    load.start()

    def build(kb, counts):
        for b in range(local_blocks):
            list_ref[b, counts[b]] = kb
        return tuple(n + mask_ref[b, kb] for b, n in enumerate(counts))

    counts = lax.fori_loop(
        0, block_count, build, (jnp.int32(0),) * local_blocks, unroll=8
    )

    def queries_of(b):
        at = slice(b * BLOCK, (b + 1) * BLOCK)
        return jnp.concatenate([q_ref[at, h * HD : (h + 1) * HD] for h in range(heads)], axis=0)

    def score(keys, b):
        return scale * lax.dot_general(
            keys, queries_of(b), (((1,), (1,)), ((), ())), preferred_element_type=jnp.float32
        )

    def mix(values, weights):
        return lax.dot_general(
            values, weights.astype(jnp.bfloat16), (((0,), (0,)), ((), ())),
            preferred_element_type=jnp.float32,
        )

    own_load.wait()
    key_at = lax.broadcasted_iota(jnp.int32, (BLOCK, width), 0)
    query_at = lax.broadcasted_iota(jnp.int32, (BLOCK, width), 1) % BLOCK
    for b in range(local_blocks):
        at = slice(b * BLOCK, (b + 1) * BLOCK)
        scores = jnp.where(key_at <= query_at, score(own_ref[at, 0:HD], b), NEG_LARGE)
        highest = jnp.max(scores, axis=0, keepdims=True)
        weights = jnp.exp2(scores - highest)
        stat_ref[b, 0:1] = highest
        stat_ref[b, 1:2] = jnp.sum(weights, axis=0, keepdims=True)
        acc_ref[b] = mix(own_ref[at, HD : 2 * HD], weights)
    load.wait()

    def add_two(b, i):
        places, drops = [], []
        for at in (2 * i, 2 * i + 1):
            real = at < counts[b]
            kb = jnp.where(real, list_ref[b, jnp.where(real, at, 0)], 0)
            places.append(pl.ds(pl.multiple_of(kb * BLOCK, BLOCK), BLOCK))
            drops.append(jnp.where(real, 0.0, NEG_LARGE).astype(jnp.float32))
        keys = jnp.concatenate([kv_ref[at, 0:HD] for at in places], axis=0)
        values = jnp.concatenate([kv_ref[at, HD : 2 * HD] for at in places], axis=0)
        scores = score(keys, b)
        scores = jnp.concatenate(
            [scores[:BLOCK] + drops[0], scores[BLOCK:] + drops[1]], axis=0
        )
        old = stat_ref[b, 0:1]
        highest = jnp.maximum(old, jnp.max(scores, axis=0, keepdims=True))
        factor = jnp.exp2(old - highest)
        weights = jnp.exp2(scores - highest)
        stat_ref[b, 0:1] = highest
        stat_ref[b, 1:2] = stat_ref[b, 1:2] * factor + jnp.sum(weights, axis=0, keepdims=True)
        acc_ref[b] = acc_ref[b] * factor + mix(values, weights)

    for b in range(0, local_blocks, 2):

        def step(i, carry, b=b):
            add_two(b, i)
            add_two(b + 1, i)
            return carry

        lax.fori_loop(0, (jnp.maximum(counts[b], counts[b + 1]) + 1) // 2, step, 0)
    for b in range(local_blocks):
        attended = (acc_ref[b] * (1.0 / stat_ref[b, 1:2])).astype(jnp.bfloat16)
        for h in range(heads):
            out_ref[b * BLOCK : (b + 1) * BLOCK, h * HD : (h + 1) * HD] = attended[
                :, h * BLOCK : (h + 1) * BLOCK
            ].T


def attend(block_mask, queries, kv):
    rows, width = queries.shape
    blocks = rows // BLOCK
    return pl.pallas_call(
        attend_kernel,
        out_shape=pltpu.VMEM(queries.shape, jnp.bfloat16),
        in_specs=[
            pl.BlockSpec(memory_space=pltpu.SMEM),
            pl.BlockSpec(memory_space=pltpu.VMEM),
            pl.BlockSpec(memory_space=pltpu.HBM),
        ],
        out_specs=pl.BlockSpec(memory_space=pltpu.VMEM),
        scratch_shapes=[
            pltpu.SMEM((blocks, 128), jnp.int32),
            pltpu.VMEM(kv.shape, jnp.bfloat16),
            pltpu.VMEM((rows, kv.shape[1]), jnp.bfloat16),
            pltpu.VMEM((blocks, HD, width), jnp.float32),
            pltpu.VMEM((blocks, 8, width), jnp.float32),
            pltpu.SemaphoreType.DMA((2,)),
        ],
        compiler_params=pltpu.CompilerParams(vmem_limit_bytes=60 * MIB),
        name="attend",
    )(block_mask, queries, kv)


def ring_places():
    head = lax.axis_index("head")
    y, zh = head // 2, head % 2
    up = ((y + 1) % 4) * 2 + zh
    down = ((y + 3) % 4) * 2 + zh
    across = y * 2 + (1 - zh)
    return y, zh, up, down, across


def remote(src, dst, send_sem, recv_sem, **place):
    return pltpu.make_async_remote_copy(
        src_ref=src,
        dst_ref=dst,
        send_sem=send_sem,
        recv_sem=recv_sem,
        device_id=place,
        device_id_type=pl.DeviceIdType.MESH,
    )


OUT_CHUNKS = 4


def project_out_kernel(
    att_ref, w_hbm, out_ref, w_ref, part, far_out, far_in, near_out, near_in, other_out, other_in,
    z_out, z_in, w_sem, far_ss, far_rs, near_ss, near_rs, other_ss, other_rs, z_ss, z_rs,
):
    y, zh, up, down, across = ring_places()
    cw = part.shape[2]
    half = cw // 2
    seat = part.shape[1] // 8
    loads = [
        pltpu.make_async_copy(w_hbm.at[:, pl.ds(c * cw, cw)], w_ref.at[c], w_sem.at[c])
        for c in range(OUT_CHUNKS)
    ]
    loads[0].start()
    barrier = pltpu.get_barrier_semaphore()
    for peer in (up, down, across):
        pl.semaphore_signal(
            barrier, inc=1, device_id={"head": peer}, device_id_type=pl.DeviceIdType.MESH
        )

    def rows_of(c, dy, other, lo=0, size=None):
        index = ((y + dy) % 4) * 2 + ((1 - zh) if other else zh)
        return part[
            c, pl.ds(pl.multiple_of(index * seat, seat), seat), lo : lo + (size or cw)
        ]

    def far(c, side):
        return remote(
            far_out.at[c, side], far_in.at[c, side], far_ss.at[c, side], far_rs.at[c, side],
            head=(up, down)[side],
        )

    def near(c, side, at):
        return remote(
            near_out.at[c, side, at], near_in.at[c, side, at],
            near_ss.at[c, side, at], near_rs.at[c, side, at],
            head=(up, down)[side],
        )

    def other(c, side):
        return remote(
            other_out.at[c, side], other_in.at[c, side], other_ss.at[c, side],
            other_rs.at[c, side], head=(up, down)[side],
        )

    def cross(c, which):
        return remote(
            z_out.at[c, which], z_in.at[c, which], z_ss.at[c, which], z_rs.at[c, which],
            head=across,
        )

    f32, bf16 = jnp.float32, jnp.bfloat16

    def first(c):
        loads[c].wait()
        if c == 0:
            for load in loads[1:]:
                load.start()
        part[c] = jnp.dot(att_ref[...], w_ref[c], preferred_element_type=f32)
        if c == 0:
            pl.semaphore_wait(barrier, 3)
        z_out[c, 0] = rows_of(c, 2, True).astype(bf16)
        cross(c, 0).start()
        for side, dy in ((0, 1), (1, 3)):
            other_out[c, side] = rows_of(c, dy, True).astype(bf16)
            other(c, side).start()
        near_out[c, 0, 1] = rows_of(c, 1, False, half, half).astype(bf16)
        near(c, 0, 1).start()
        near_out[c, 1, 0] = rows_of(c, 3, False, 0, half).astype(bf16)
        near(c, 1, 0).start()

    def second(c):
        cross(c, 0).wait_recv()
        for side in range(2):
            far_out[c, side] = (
                rows_of(c, 2, False, side * half, half)
                + z_in[c, 0, :, side * half : (side + 1) * half].astype(f32)
            ).astype(bf16)
            far(c, side).start()

    def third(c):
        for side, dy in ((0, 1), (1, 3)):
            far(c, side).wait_recv()
            near_out[c, side, side] = (
                rows_of(c, dy, False, side * half, half) + far_in[c, side].astype(f32)
            ).astype(bf16)
            near(c, side, side).start()

    def fourth(c):
        other(c, 0).wait_recv()
        other(c, 1).wait_recv()
        z_out[c, 1] = (
            rows_of(c, 0, True) + other_in[c, 0].astype(f32) + other_in[c, 1].astype(f32)
        ).astype(bf16)
        cross(c, 1).start()

    def fifth(c):
        for side in range(2):
            for at in range(2):
                near(c, side, at).wait_recv()
        cross(c, 1).wait_recv()
        for at in range(2):
            here = slice(at * half, (at + 1) * half)
            out_ref[:, c * cw + at * half : c * cw + (at + 1) * half] = (
                rows_of(c, 0, False, at * half, half)
                + near_in[c, 0, at].astype(f32)
                + near_in[c, 1, at].astype(f32)
                + z_in[c, 1, :, here].astype(f32)
            ).astype(bf16)

    first(0)
    first(1)
    for n in range(OUT_CHUNKS + 3):
        if n < OUT_CHUNKS:
            second(n)
        if n + 2 < OUT_CHUNKS:
            first(n + 2)
        if 1 <= n <= OUT_CHUNKS:
            third(n - 1)
            fourth(n - 1)
        if n >= 3:
            fifth(n - 3)
    for c in range(OUT_CHUNKS):
        for side in range(2):
            far(c, side).wait_send()
            other(c, side).wait_send()
            cross(c, side).wait_send()
            for at in range(2):
                near(c, side, at).wait_send()


def project_out(attended, w_out):
    rows, depth = attended.shape
    width = w_out.shape[1]
    n, cw = OUT_CHUNKS, width // OUT_CHUNKS
    half = cw // 2
    seat = rows // 8
    bf16 = jnp.bfloat16
    dma = pltpu.SemaphoreType.DMA
    return pl.pallas_call(
        project_out_kernel,
        out_shape=pltpu.VMEM((seat, width), bf16),
        in_specs=[
            pl.BlockSpec(memory_space=pltpu.VMEM),
            pl.BlockSpec(memory_space=pltpu.HBM),
        ],
        out_specs=pl.BlockSpec(memory_space=pltpu.VMEM),
        scratch_shapes=[
            pltpu.VMEM((n, depth, cw), bf16),
            pltpu.VMEM((n, rows, cw), jnp.float32),
            pltpu.VMEM((n, 2, seat, half), bf16),
            pltpu.VMEM((n, 2, seat, half), bf16),
            pltpu.VMEM((n, 2, 2, seat, half), bf16),
            pltpu.VMEM((n, 2, 2, seat, half), bf16),
            pltpu.VMEM((n, 2, seat, cw), bf16),
            pltpu.VMEM((n, 2, seat, cw), bf16),
            pltpu.VMEM((n, 2, seat, cw), bf16),
            pltpu.VMEM((n, 2, seat, cw), bf16),
            dma((n,)),
            dma((n, 2)),
            dma((n, 2)),
            dma((n, 2, 2)),
            dma((n, 2, 2)),
            dma((n, 2)),
            dma((n, 2)),
            dma((n, 2)),
            dma((n, 2)),
        ],
        compiler_params=pltpu.CompilerParams(
            collective_id=1, has_side_effects=True, vmem_limit_bytes=60 * MIB
        ),
        name="project_out",
    )(attended, w_out)


IN_CHUNKS = 2
PART_ROWS = (256, 128, 128)
PART_CHUNKS = (2, 1, 1)
SLOTS = 64
AHEAD = 3
QUERIES_LATER = 0
STEPS = [(p, f) for p, n in enumerate(PART_CHUNKS) for f in range(n)]
PARTS = len(PART_ROWS)


def gather_kernel(
    target_ref, position_ref, turn_ref, x_hbm, wq_hbm, wk_hbm, wv_hbm, q_ref, kv_ref,
    x_ref, cos_ref, sin_ref, w_ref, pick, place, send, recv, meta_out, meta_in, in_sem, row_ss,
    row_rs, meta_ss, meta_rs, ag_ss, ag_rs, kv_sem, kv_ss, kv_rs, *per_part,
):
    ctx = lax.axis_index("ctx")
    peers = lax.axis_size("ctx")
    rows, cols = x_ref.shape
    chunk = cols // IN_CHUNKS
    pieces, acc, kv_own = (per_part[i * PARTS : (i + 1) * PARTS] for i in range(3))
    starts = [sum(PART_ROWS[:p]) for p in range(PARTS)]
    y, zh, up, down, across = ring_places()
    bf16 = jnp.bfloat16
    loads = [
        pltpu.make_async_copy(src, dst, in_sem.at[i])
        for i, (src, dst) in enumerate(
            (
                (x_hbm, x_ref),
                (wq_hbm, w_ref.at[:, 0:512]),
                (wk_hbm, w_ref.at[:, 512:640]),
                (wv_hbm, w_ref.at[:, 640:768]),
            )
        )
    ]
    loads[0].start()
    barrier = pltpu.get_barrier_semaphore()
    for k in range(1, peers):
        pl.semaphore_signal(
            barrier, inc=1, device_id={"ctx": (ctx + k) % peers},
            device_id_type=pl.DeviceIdType.MESH,
        )
    for peer in (up, down, across):
        pl.semaphore_signal(
            barrier, inc=1, device_id={"head": peer}, device_id_type=pl.DeviceIdType.MESH
        )

    target = target_ref[...]
    owner = target // rows
    local = target - owner * rows
    owned = lax.broadcasted_iota(jnp.int32, (peers, rows), 0) == owner
    owned_f = jnp.where(owned, 1.0, 0.0).astype(jnp.float32)
    earlier = (
        lax.broadcasted_iota(jnp.int32, (rows, rows), 0)
        < lax.broadcasted_iota(jnp.int32, (rows, rows), 1)
    )
    before = jnp.dot(
        owned_f.astype(bf16),
        jnp.where(earlier, 1.0, 0.0).astype(bf16),
        preferred_element_type=jnp.float32,
    )
    rank = jnp.sum(owned_f * before, axis=0, keepdims=True)
    slot = owner * SLOTS + rank.astype(jnp.int32)
    for i in range(peers):
        at = lax.broadcasted_iota(jnp.int32, (SLOTS, rows), 0) + i * SLOTS
        pick[i * SLOTS : (i + 1) * SLOTS, :] = jnp.where(at == slot, 1.0, 0.0).astype(bf16)

    def meta_copy(k):
        to = (ctx + k) % peers
        return remote(meta_out.at[to], meta_in.at[k], meta_ss.at[k], meta_rs.at[k], ctx=to)

    def row_copy(f, k):
        to = (ctx + k) % peers
        return remote(
            send.at[f, pl.ds(pl.multiple_of(to * SLOTS, SLOTS), SLOTS)],
            recv.at[f, pl.ds(k * SLOTS, SLOTS)],
            row_ss.at[f, k], row_rs.at[f, k], ctx=to,
        )

    line = lax.broadcasted_iota(jnp.int32, (8, rows), 0)
    high = local // 16
    facts = jnp.where(line == 0, high, jnp.where(line == 1, local - high * 16, 1))
    facts = lax.dot_general(
        facts.astype(jnp.float32).astype(bf16), pick[...], (((1,), (1,)), ((), ())),
        preferred_element_type=jnp.float32,
    )
    goes_to = jnp.where(facts[2:3] > 0.5, facts[0:1] * 16.0 + facts[1:2], -1.0)
    goes_to = jnp.broadcast_to(goes_to, (8, peers * SLOTS))
    for i in range(peers // 2):
        tile = goes_to[:, i * 128 : (i + 1) * 128]
        meta_out[2 * i] = tile
        meta_out[2 * i + 1] = pltpu.roll(tile, SLOTS, 1)
    pl.semaphore_wait(barrier, peers - 1 + 3)
    for k in range(1, peers):
        meta_copy(k).start()
    meta_in[0] = meta_out[ctx]

    loads[0].wait()
    for load in loads[1:]:
        load.start()
    for f in range(IN_CHUNKS):
        send[f] = jnp.dot(
            pick[...], x_ref[:, f * chunk : (f + 1) * chunk], preferred_element_type=jnp.float32
        ).astype(bf16)
        for k in range(1, peers):
            row_copy(f, k).start()
        recv[f, 0:SLOTS, :] = send[f, pl.ds(pl.multiple_of(ctx * SLOTS, SLOTS), SLOTS), :]

    for i in range(rows // 128):
        here = slice(i * 128, (i + 1) * 128)
        angle = position_ref[:, here].astype(jnp.float32)
        angle = jnp.broadcast_to(angle, (128, 128)).T * turn_ref[0:1]
        cos_ref[here, :] = jnp.cos(angle)
        sin_ref[here, :] = jnp.sin(angle) * turn_ref[1:2]

    for k in range(1, peers):
        meta_copy(k).wait_recv()
    lane = lax.broadcasted_iota(jnp.int32, (8, 128), 1)
    for i in range(peers // 2):
        both = jnp.where(lane < SLOTS, meta_in[2 * i], pltpu.roll(meta_in[2 * i + 1], SLOTS, 1))
        both = both[0:1].astype(jnp.int32)
        at = lax.broadcasted_iota(jnp.int32, (rows, 128), 0)
        place[:, i * 128 : (i + 1) * 128] = jnp.where(at == both, 1.0, 0.0).astype(bf16)

    def piece(dy, other):
        return ((y + dy) % 4) * 2 + ((1 - zh) if other else zh)

    def spread(n, e):
        part, f = STEPS[n]
        size, half = PART_ROWS[part], PART_ROWS[part] // 2
        src, lo, size, to = (
            (piece(0, 0), 0, size, across),
            (piece(0, 0), 0, size, up),
            (piece(0, 0), 0, size, down),
            (piece(3, 0), 0, half, up),
            (piece(1, 0), half, half, down),
            (piece(0, 1), 0, size, up),
            (piece(0, 1), 0, size, down),
            (piece(2, 0), 0, size, across),
        )[e]
        ref = pieces[part].at[src, f, pl.ds(lo, size)]
        return remote(ref, ref, ag_ss.at[n, e], ag_rs.at[n, e], head=to)

    def product(part, index, columns):
        piece_rows = jnp.concatenate(
            [pieces[part][index, g] for g in range(PART_CHUNKS[part])], axis=1
        )
        deep = index * cols
        deep = pl.ds(deep if isinstance(deep, int) else pl.multiple_of(deep, cols), cols)
        return jnp.dot(piece_rows, w_ref[deep, columns], preferred_element_type=jnp.float32)

    def project(n, index, first=False):
        part, f = STEPS[n]
        if f < PART_CHUNKS[part] - 1:
            return
        term = product(part, index, slice(512, 768))
        acc[part][...] = term if first else acc[part][...] + term

    def begin(n):
        part, f = STEPS[n]
        if part == 0:
            for k in range(1, peers):
                row_copy(f, k).wait_recv()
        here = slice(starts[part], starts[part] + PART_ROWS[part])
        wide = IN_CHUNKS // PART_CHUNKS[part]
        for g in range(wide):
            pieces[part][piece(0, 0), f, :, g * chunk : (g + 1) * chunk] = jnp.dot(
                place[here, :], recv[f * wide + g], preferred_element_type=jnp.float32
            ).astype(bf16)
        for e in (1, 2, 0):
            spread(n, e).start()
        if n == IN_CHUNKS - 1:
            for load in loads[1:]:
                load.wait()
        project(n, piece(0, 0), first=True)

    def near(n):
        spread(n, 1).wait_recv()
        spread(n, 3).start()
        spread(n, 2).wait_recv()
        spread(n, 4).start()
        spread(n, 0).wait_recv()
        spread(n, 5).start()
        spread(n, 6).start()
        project(n, piece(3, 0))
        project(n, piece(1, 0))
        project(n, piece(0, 1))

    def far(n):
        spread(n, 3).wait_recv()
        spread(n, 4).wait_recv()
        spread(n, 7).start()
        project(n, piece(2, 0))

    def other(n):
        spread(n, 5).wait_recv()
        spread(n, 6).wait_recv()
        project(n, piece(3, 1))
        project(n, piece(1, 1))
        spread(n, 7).wait_recv()
        project(n, piece(2, 1))

    zl, x, core = ctx // 8, (ctx // 2) % 4, ctx % 2

    def block(dx, other_z, other_core=0):
        z = (1 - zl) if other_z else zl
        c = (1 - core) if other_core else core
        return z * 8 + ((x + dx) % 4) * 2 + c

    kv_pieces = ((0, 0), (0, 1), (3, 0), (1, 0), (2, 0), (3, 1), (1, 1), (2, 1))

    def share(part, e):
        right, left, over = block(1, 0), block(3, 0), block(0, 1)
        part_rows = PART_ROWS[part]
        if e >= 8:
            src, to = block(*kv_pieces[e - 8]), block(0, 0, 1)
        else:
            src, to = (
                (block(0, 0), over),
                (block(0, 0), right),
                (block(0, 0), left),
                (block(0, 0), block(2, 0)),
                (block(0, 1), right),
                (block(0, 1), left),
                (block(0, 1), block(2, 0)),
            )[e]
        ref = kv_ref.at[pl.ds(pl.multiple_of(src * rows + starts[part], 16), part_rows)]
        source = kv_own[part] if e in (0, 1, 2, 3, 8) else ref
        return remote(source, ref, kv_ss.at[part, e], kv_rs.at[part, e], ctx=to)

    def keep(part):
        at = pl.ds(pl.multiple_of(ctx * rows + starts[part], 16), PART_ROWS[part])
        return pltpu.make_async_copy(kv_own[part], kv_ref.at[at], kv_sem.at[part])

    def turn(tensor, here):
        return tensor * cos_ref[here, :] + pltpu.roll(tensor, HD // 2, 1) * sin_ref[here, :]

    def finish(part):
        here = slice(starts[part], starts[part] + PART_ROWS[part])
        kv_own[part][:, 0:HD] = turn(acc[part][:, 0:HD], here).astype(bf16)
        kv_own[part][:, HD : 2 * HD] = acc[part][:, HD : 2 * HD].astype(bf16)
        give(part, 0, zl == 0)
        give(part, 1, x < 3)
        give(part, 2, x == 0)
        give(part, 3, x < 2)
        share(part, 8).start()
        keep(part).start()

    def finish_queries(part):
        here = slice(starts[part], starts[part] + PART_ROWS[part])
        query = product(part, 0, slice(0, 512))
        for index in range(1, 8):
            query = query + product(part, index, slice(0, 512))
        for h in range(4):
            at = slice(h * HD, (h + 1) * HD)
            q_ref[here, at] = turn(query[:, at], here).astype(bf16)

    def give(part, e, when):
        @pl.when(when)
        def _():
            share(part, e).start()

    def share_near(part):
        @pl.when(zl == 1)
        def _():
            share(part, 0).wait_recv()
            for e in (4, 5, 6, 9):
                share(part, e).start()

    def pass_on(part, e, core_e, when):
        @pl.when(when)
        def _():
            share(part, e).wait_recv()
            share(part, core_e).start()

    def share_far(part):
        pass_on(part, 1, 10, x > 0)
        pass_on(part, 2, 11, x == 3)
        pass_on(part, 3, 12, x > 1)

    def share_other(part):
        @pl.when(zl == 1)
        def _():
            for e in (4, 5, 6):
                share(part, e).wait_recv()
                share(part, e + 9).start()

    count = len(STEPS)
    due = {}
    for part in range(PARTS):
        last = sum(PART_CHUNKS[: part + 1]) + 1
        for later, rank_in, act in (
            (0, 0, finish), (1, 1, share_near), (2, 1, share_far), (3, 1, share_other),
            (QUERIES_LATER, 2, finish_queries),
        ):
            due.setdefault(last + later, []).append((rank_in, part, act))
    begin(0)
    begin(1)
    begun = 2
    for n in range(max(due) + 1):
        if n < count:
            near(n)
        while begun < min(count, n + (3 if n + 3 <= IN_CHUNKS - 1 or n < 1 else AHEAD + 1)):
            begin(begun)
            begun += 1
        if 1 <= n <= count:
            far(n - 1)
        if 2 <= n <= count + 1:
            other(n - 2)
        for rank_in, part, act in sorted(due.get(n, []), key=lambda item: item[:2]):
            act(part)
    below = zl == 1
    sent = (
        (0, zl == 0), (1, x < 3), (2, x == 0), (3, x < 2), (4, below), (5, below), (6, below),
    )
    copied = (
        (8, None), (9, below), (10, x > 0), (11, x == 3), (12, x > 1), (13, below), (14, below),
        (15, below),
    )

    def drain(part, e, when, received):
        def wait():
            if received:
                share(part, e).wait_recv()
            else:
                share(part, e).wait_send()

        if when is None:
            wait()
        else:
            pl.when(when)(wait)

    for part in range(PARTS):
        for e, when in copied:
            drain(part, e, when, True)

    for k in range(1, peers):
        meta_copy(k).wait_send()
        for f in range(IN_CHUNKS):
            row_copy(f, k).wait_send()
    for n in range(count):
        for e in range(8):
            spread(n, e).wait_send()
    for part in range(PARTS):
        keep(part).wait()
        for e, when in sent + copied:
            drain(part, e, when, False)


def gather_and_project(node_rows, node_target, node_position, w_query, w_key, w_value):
    rows, cols = node_rows.shape
    peers = lax.axis_size("ctx")
    chunk = cols // IN_CHUNKS
    bf16 = jnp.bfloat16
    dma = pltpu.SemaphoreType.DMA
    vmem = pl.BlockSpec(memory_space=pltpu.VMEM)
    hbm = pl.BlockSpec(memory_space=pltpu.HBM)
    entry = np.arange(HD)
    inverse = ROPE_THETA ** ((entry % (HD // 2)) * (-2.0 / HD))
    turns = np.stack([inverse, np.where(entry < HD // 2, -1.0, 1.0)]).astype(np.float32)
    return pl.pallas_call(
        gather_kernel,
        out_shape=(
            pltpu.VMEM((rows, 512), bf16),
            jax.ShapeDtypeStruct((rows * peers, 256), bf16),
        ),
        in_specs=[vmem] * 3 + [hbm] * 4,
        out_specs=(vmem, hbm),
        scratch_shapes=[
            pltpu.VMEM((rows, cols), bf16),
            pltpu.VMEM((rows, HD), jnp.float32),
            pltpu.VMEM((rows, HD), jnp.float32),
            pltpu.VMEM((w_query.shape[0], 768), bf16),
            pltpu.VMEM((peers * SLOTS, rows), bf16),
            pltpu.VMEM((rows, peers * SLOTS), bf16),
            pltpu.VMEM((IN_CHUNKS, peers * SLOTS, chunk), bf16),
            pltpu.VMEM((IN_CHUNKS, peers * SLOTS, chunk), bf16),
            pltpu.VMEM((peers, 8, 128), jnp.float32),
            pltpu.VMEM((peers, 8, 128), jnp.float32),
            dma((4,)),
            dma((IN_CHUNKS, peers)),
            dma((IN_CHUNKS, peers)),
            dma((peers,)),
            dma((peers,)),
            dma((len(STEPS), 8)),
            dma((len(STEPS), 8)),
            dma((PARTS,)),
            dma((PARTS, 16)),
            dma((PARTS, 16)),
        ]
        + [pltpu.VMEM((8, n, r, cols // n), bf16) for r, n in zip(PART_ROWS, PART_CHUNKS)]
        + [pltpu.VMEM((r, 256), jnp.float32) for r in PART_ROWS]
        + [pltpu.VMEM((r, 256), bf16) for r in PART_ROWS],
        compiler_params=pltpu.CompilerParams(
            collective_id=2, has_side_effects=True, vmem_limit_bytes=60 * MIB
        ),
        name="gather_and_project",
    )(
        node_target.reshape(1, rows), node_position.reshape(1, rows), jnp.asarray(turns), node_rows,
        w_query, w_key, w_value,
    )


def on_device(node_rows, node_target, node_position, block_mask, w_query, w_key, w_value, w_out):
    queries, kv = gather_and_project(
        node_rows, node_target, node_position, w_query, w_key, w_value
    )
    queries = pltpu.with_memory_space_constraint(queries, pltpu.VMEM)
    attended = attend(block_mask, queries, kv)
    attended = pltpu.with_memory_space_constraint(attended, pltpu.VMEM)
    return project_out(attended, w_out)


def solution(mesh):
    placed = (
        P("ctx", "head"),
        P("ctx"),
        P("ctx"),
        P("ctx", None),
        P(None, "head"),
        P(None, "head"),
        P(None, "head"),
        P("head", None),
    )
    return jax.shard_map(
        on_device, mesh=mesh, in_specs=placed, out_specs=P(("ctx", "head"), None), check_vma=False
    )
```
